32 devices in a mesh: rows: 16 (over z, y, x), task: 2 (over core).
Axes of the slice: x: 2, y: 2, z: 4, core: 2. Of those that a mesh axis runs over, the one named last changes fastest.
Arguments:
- emb: bfloat16 [98304, 416], P('rows'), may hold values from -6 to 6
- dense: bfloat16 [98304, 13], P('rows'), may hold values from -6 to 6
- group_sizes: int32 [48, 512], P('rows'), may hold values from 1 to 16, 2048 in all within a row
- labels: int32 [2, 98304], P('task', 'rows'), may hold values 0 or 1
- w_emb: bfloat16 [416, 512], P(None, 'rows'), may hold values from -0.3125 to 0.3125
- w_dense: bfloat16 [13, 512], P(None, 'rows'), may hold values from -0.3125 to 0.3125
- b_in: bfloat16 [512], P('rows'), may hold values from -4 to 4
- expert_w1: bfloat16 [8, 512, 256], P('task', 'rows'), may hold values from -0.25 to 0.25
- expert_b1: bfloat16 [8, 256], P('task', 'rows'), may hold values from -4 to 4
- expert_w2: bfloat16 [8, 256, 128], P('task', 'rows'), may hold values from -0.375 to 0.375
- expert_b2: bfloat16 [8, 128], P('task', 'rows'), may hold values from -4 to 4
- gate_w: bfloat16 [2, 512, 8], P('task', 'rows'), may hold values from -0.125 to 0.125
- gate_b: bfloat16 [2, 8], P('task'), may hold values from -4 to 4
- tower_w1: bfloat16 [2, 128, 64], P('task', 'rows'), may hold values from -1 to 1
- tower_b1: bfloat16 [2, 64], P('task'), may hold values from -4 to 4
- tower_w2: bfloat16 [2, 64], P('task'), may hold values from -1.5 to 1.5
- tower_b2: bfloat16 [2], P('task'), may hold values from -6 to 6
Outputs:
- emb_grad: float32 [98304, 416], P('rows')
- dense_grad: float32 [98304, 13], P('rows')
- w_emb_grad: float32 [416, 512], P(None, 'rows')
- w_dense_grad: float32 [13, 512], P(None, 'rows')
- b_in_grad: float32 [512], P('rows')
- expert_w1_grad: float32 [8, 512, 256], P('task', 'rows')
- expert_b1_grad: float32 [8, 256], P('task', 'rows')
- expert_w2_grad: float32 [8, 256, 128], P('task', 'rows')
- expert_b2_grad: float32 [8, 128], P('task', 'rows')
- gate_w_grad: float32 [2, 512, 8], P('task', 'rows')
- gate_b_grad: float32 [2, 8], P('task')
- tower_w1_grad: float32 [2, 128, 64], P('task', 'rows')
- tower_b1_grad: float32 [2, 64], P('task')
- tower_w2_grad: float32 [2, 64], P('task')
- tower_b2_grad: float32 [2], P('task')
The draws below stay inside these ranges and needn't reach their ends.
Inputs may be any that keep to these rules, and one draw needn't show every extreme that they name: Each row of group_sizes sums to 2048; its largest entry is exactly 16.
All inputs are finite; a program needn't handle non-finite values. No bound on the sum of `labels` on one device may be relied on, other than what follows from the above.
Results may differ from the reference program's by a relative error of at most 0.02.
Values may be sent and summed in bfloat16 or wider, within the bound.
No kernel may reach another device: no remote copies, remote signals or barrier semaphores. Data moves between devices by JAX's collectives and lax.ppermute only.
A program may use at most 192 MiB of HBM per device.

```python
import math
import jax
import jax.numpy as jnp
import numpy as np
from jax import lax

EMB = 416
DENSE = 13
D_MODEL = 512
EXPERTS = 8
EXP_HID = 256
EXP_OUT = 128
TOWER = 64
TASKS = 2
MB = 3
MB_ROWS = 2048
MOST = 16
GROUPS = 512
ROWS = 98304
USERS = 24576
N_ROWS = 16


def touch_ends(drawn, key, smallest, top_value):
    shape = drawn.shape
    index_at = [jax.random.randint(jax.random.fold_in(key, axis), (), 0, shape[axis]) for axis in range(len(shape))]
    drawn = drawn.at[tuple(index_at)].set(smallest)
    longest = shape.index(max(shape))
    index_at[longest] = (index_at[longest] + 1) % shape[longest]
    return drawn.at[tuple(index_at)].set(top_value)


def levels(own_key, dims, cuts, smallest, top_value):
    loudness = 1.0
    for axis_at, shards_of in cuts:
        steps = jax.random.uniform(jax.random.fold_in(jax.random.fold_in(own_key, 6), axis_at), (shards_of,), jnp.float32, smallest / len(cuts), top_value / len(cuts))
        loudness = loudness * jnp.repeat(jnp.exp(steps), dims[axis_at] // shards_of).reshape((-1,) + (1,) * (len(dims) - 1 - axis_at))
    return loudness


def length_profile(amount, total, bound, lean):
    weights = [(1 << 20) // math.isqrt(grade ** lean) + 1 for grade in range(2, amount + 1)]
    rest, holding = total - bound - (amount - 1), [1] * (amount - 1)
    while rest > 0:
        movable = [i for i in range(amount - 1) if holding[i] < bound]
        pool, left = sum([weights[i] for i in movable]), rest
        for i in movable:
            more = min(bound - holding[i], max(1, left * weights[i] // pool), rest)
            holding[i] = holding[i] + more
            rest = rest - more
    return np.array([bound] + holding)


def ragged(own_key, number_of, total, reach, slope):
    if number_of == 2:
        one = jax.random.randint(own_key, (), max(1, total - reach), min(reach, total - 1) + 1)
        return jnp.stack([one, total - one])
    lengths = jnp.asarray(length_profile(number_of, total, reach, slope), jnp.int32)
    twos = (number_of - 1) // 2
    source_of, sink = lengths[1:1 + 2 * twos:2], lengths[2:2 + 2 * twos:2]
    margin = jnp.minimum(source_of - 1, reach - sink)
    shifted = jax.random.randint(jax.random.fold_in(own_key, 1), (twos,), 0, 1 << 20) % (margin + 1)
    lengths = lengths.at[1:1 + 2 * twos:2].set(source_of - shifted).at[2:2 + 2 * twos:2].set(sink + shifted)
    return lengths[jax.random.permutation(jax.random.fold_in(own_key, 2), number_of)]


def normal_values(key, extent, scale, bound, cuts=(), held_as=jnp.bfloat16):
    gain = levels(key, extent, cuts, -0.22, 0.18) if cuts else 1.0
    drawn = jax.random.normal(key, extent, jnp.float32) * scale * gain
    return jnp.minimum(jnp.maximum(drawn, -bound), bound).astype(held_as)


def setup_inputs(seed: int = 0) -> dict:
    key_of = jax.random.split(jax.random.key(seed), 18)
    emb = normal_values(key_of[0], (ROWS, EMB), 1.0, 6.0, ((0, 16),))
    dense = normal_values(key_of[1], (ROWS, DENSE), 1.0, 6.0, ((0, 16),))
    group_sizes = jax.vmap(lambda own: ragged(own, GROUPS, MB_ROWS, MOST, 2))(jax.random.split(key_of[2], (N_ROWS * MB))).reshape((N_ROWS * MB, GROUPS)).astype(jnp.int32)
    labels = touch_ends((jax.random.randint(key_of[3], (TASKS, ROWS), 0, 2) < 1).astype(jnp.int32), jax.random.fold_in(key_of[3], 1), 0, 1)
    w_emb = normal_values(key_of[4], (EMB, D_MODEL), (EMB + DENSE) ** -0.5, 0.3125, ((1, 16),))
    w_dense = normal_values(key_of[5], (DENSE, D_MODEL), (EMB + DENSE) ** -0.5, 0.3125, ((1, 16),))
    b_in = normal_values(key_of[6], (D_MODEL,), 0.3, 4.0, ((0, 16),))
    expert_w1 = normal_values(key_of[7], (EXPERTS, D_MODEL, EXP_HID), D_MODEL ** -0.5, 0.25, ((0, 2), (1, 16)))
    expert_b1 = normal_values(key_of[8], (EXPERTS, EXP_HID), 0.3, 4.0, ((0, 2), (1, 16)))
    expert_w2 = normal_values(key_of[9], (EXPERTS, EXP_HID, EXP_OUT), EXP_HID ** -0.5, 0.375, ((0, 2), (1, 16)))
    expert_b2 = normal_values(key_of[10], (EXPERTS, EXP_OUT), 0.3, 4.0, ((0, 2), (1, 16)))
    gate_w = normal_values(key_of[11], (TASKS, D_MODEL, EXPERTS), (4 * D_MODEL) ** -0.5, 0.125, ((0, 2), (1, 16)))
    gate_b = normal_values(key_of[12], (TASKS, EXPERTS), 0.3, 4.0, ((0, 2),))
    tower_w1 = normal_values(key_of[13], (TASKS, EXP_OUT, TOWER), (EXP_OUT // 4) ** -0.5, 1.0, ((0, 2), (1, 16)))
    tower_b1 = normal_values(key_of[14], (TASKS, TOWER), 0.3, 4.0, ((0, 2),))
    tower_w2 = normal_values(key_of[15], (TASKS, TOWER), (TOWER // 4) ** -0.5, 1.5, ((0, 2),))
    tower_b2 = normal_values(key_of[16], (TASKS,), 0.5, 6.0, ((0, 2),))
    return {"emb": emb, "dense": dense, "group_sizes": group_sizes, "labels": labels, "w_emb": w_emb, "w_dense": w_dense, "b_in": b_in, "expert_w1": expert_w1, "expert_b1": expert_b1, "expert_w2": expert_w2, "expert_b2": expert_b2, "gate_w": gate_w, "gate_b": gate_b, "tower_w1": tower_w1, "tower_b1": tower_b1, "tower_w2": tower_w2, "tower_b2": tower_b2}


@jax.custom_vjp
def low(v):
    return lax.optimization_barrier(v.astype(jnp.bfloat16)).astype(jnp.float32)

@jax.custom_vjp
def low_back(v):
    return v

def low_keep(v):
    return (low(v), None)

def low_pass(kept, grad):
    return (grad,)

def back_keep(v):
    return (v, None)

def back_low(kept, grad):
    return (low(grad),)
low.defvjp(low_keep, low_pass)
low_back.defvjp(back_keep, back_low)
HIGHEST = lax.Precision.HIGHEST

def matmul(left, right):
    return jnp.dot(left, right, precision=HIGHEST, preferred_element_type=jnp.float32)

def row_weights(group_rows):
    group_ends = jnp.cumsum(group_rows).astype(jnp.int32)
    group_starts = group_ends - group_rows
    places = jnp.arange(MB_ROWS, dtype=jnp.int32)[:, None]
    inside = (places >= group_starts[None, :]) & (places < group_ends[None, :])
    inverse = 1.0 / group_rows.astype(jnp.float32)
    return lax.optimization_barrier(jnp.sum(jnp.where(inside, inverse[None, :], jnp.zeros_like(inverse)[None, :]), axis=1))

def layer_sum(params, features, dense_in, weights_row, labels_block):
    w_emb, w_dense, b_in, expert_w1, expert_b1, expert_w2, expert_b2, gate_w, gate_b, tower_w1, tower_b1, tower_w2, tower_b2 = params
    hidden = low_back(matmul(features, w_emb) + matmul(dense_in, w_dense) + b_in[None, :])
    shared = low(hidden)
    half_count = EXPERTS // 2
    task_views = []
    outputs = []
    for task_id in range(TASKS):
        view = low_back(shared)
        offset = task_id * half_count
        first_pre = low_back(jnp.einsum('rd,kdf->rkf', view, expert_w1[offset:offset + half_count], precision=HIGHEST) + expert_b1[None, offset:offset + half_count])
        middle = low(jax.nn.silu(first_pre))
        second_pre = low_back(jnp.einsum('rkf,kfo->rko', middle, expert_w2[offset:offset + half_count], precision=HIGHEST) + expert_b2[None, offset:offset + half_count])
        outputs.append(low(jax.nn.silu(second_pre)))
        task_views.append(view)
    experts_all = jnp.concatenate(outputs, axis=1)
    summed = jnp.zeros((), jnp.float32)
    for task_id in range(TASKS):
        logits = matmul(task_views[task_id], gate_w[task_id]) + gate_b[task_id][None, :]
        gate_probs = jax.nn.softmax(logits, axis=-1)
        mixture = jnp.einsum('rk,rko->ro', gate_probs, low_back(experts_all), precision=HIGHEST)
        tower_in = low(low_back(mixture))
        tower_pre = low_back(matmul(tower_in, tower_w1[task_id]) + tower_b1[task_id][None, :])
        tower_act = jax.nn.silu(tower_pre)
        task_logit = lax.optimization_barrier(jnp.sum(tower_act * tower_w2[task_id][None, :], axis=1)) + tower_b2[task_id]
        target = labels_block[task_id]
        summed = summed + jnp.sum(weights_row * (jax.nn.softplus(task_logit) - target * task_logit))
    return summed

def reference(emb, dense, group_sizes, labels, w_emb, w_dense, b_in, expert_w1, expert_b1, expert_w2, expert_b2, gate_w, gate_b, tower_w1, tower_b1, tower_w2, tower_b2):
    params = tuple((weight.astype(jnp.float32) for weight in (w_emb, w_dense, b_in, expert_w1, expert_b1, expert_w2, expert_b2, gate_w, gate_b, tower_w1, tower_b1, tower_w2, tower_b2)))
    blocks = N_ROWS * MB
    emb_blocks = emb.astype(jnp.float32).reshape(blocks, MB_ROWS, EMB)
    dense_blocks = dense.astype(jnp.float32).reshape(blocks, MB_ROWS, DENSE)
    label_blocks = jnp.transpose(labels.astype(jnp.float32).reshape(TASKS, blocks, MB_ROWS), (1, 0, 2))

    def one_block(running, block_item):
        features, dense_in, group_rows, labels_block = block_item
        weights_row = row_weights(group_rows)

        def inner(weights_in, feat_in, dense_part):
            return layer_sum(weights_in, feat_in, dense_part, weights_row, labels_block)
        block_sum, pullback = jax.vjp(inner, params, features, dense_in)
        block_grads = pullback(jnp.ones_like(block_sum))
        running = jax.tree.map(jnp.add, running, block_grads[0])
        return (running, (block_grads[1], block_grads[2]))
    zero_grads = jax.tree.map(jnp.zeros_like, params)
    totals, (emb_grad, dense_grad) = lax.scan(one_block, zero_grads, (emb_blocks, dense_blocks, group_sizes, label_blocks))
    scaled = [part / USERS for part in totals]
    return (emb_grad.reshape(ROWS, EMB), dense_grad.reshape(ROWS, DENSE), scaled[0], scaled[1], scaled[2], scaled[3], scaled[4], scaled[5], scaled[6], scaled[7], scaled[8], scaled[9], scaled[10], scaled[11], scaled[12])
```

```python
import functools

import jax
import jax.numpy as jnp
from jax import lax
from jax.experimental import pallas as pl
from jax.experimental.pallas import tpu as pltpu
from jax.sharding import PartitionSpec as P

F32 = jnp.float32
BF = jnp.bfloat16
NT = (((1,), (1,)), ((), ()))
D, FH, EO, TW, NE = 512, 256, 128, 64, 8
HALF = NE // 2
EMB, DENSE = 416, 13
XR = 448
PC = 512 + HALF * FH
QC = HALF * EO + 256
FG = NE * FH + 128
TILE = 512
BOTH = (((0, 1), (1, 0)))


def mm(a, b):
    return jnp.dot(a, b, preferred_element_type=F32)


def mm_nt(a, b):
    return lax.dot_general(a, b, NT, preferred_element_type=F32)


def act_pair(half):
    t = jnp.tanh(half)
    q = 1.0 + t
    m = half * q
    return m, q + m * (1.0 - t)


def swap_halves(a, flag):
    return jnp.where(flag, jnp.concatenate([a[HALF:NE], a[0:HALF]], axis=0), a)


def lane_fold(a):
    total = a[:, 0:128]
    for c in range(1, a.shape[1] // 128):
        total = total + a[:, 128 * c : 128 * c + 128]
    return total


def main_kernel(pieces, chunks, tab_ref, *refs):
    emb_ref, dense_ref, row_ref, vec_ref = refs[:4]
    p_refs = (refs[4 : 4 + pieces], refs[4 + pieces : 4 + 2 * pieces])
    q_refs = (refs[4 + 2 * pieces : 4 + 3 * pieces], refs[4 + 3 * pieces : 4 + 4 * pieces])
    refs = refs[4 + 4 * pieces :]
    eg_ref, dg_ref, hg_ref, wa_ref, dpo_ref, dpx_ref, dqo_ref, dqx_ref = refs[:8]
    (
        x_s, hid_s, mid_s, sl1_s, out_s, sl2_s, sg_s, fg_s, mix_s,
        wat_s, wa_s, w1t_s, gt_s, w1_s, w2t_s, w2_s, b1_s, b2_s, gb_s, tt_s, tw_s, tcol_s, q_s,
        dwa_s, dw1_s, dw2_s, dtw_s, dcol_s, dlog_s, db1_s, ob_s,
    ) = refs[8:]
    n = emb_ref.shape[1]
    fs, osz = FH // chunks, EO // chunks
    step = pl.program_id(0)
    second_core = tab_ref[0] == 1

    @pl.when(step == 0)
    def _():
        rows = lax.broadcasted_iota(jnp.int32, (32, n), 0)
        x_s[EMB:XR, :] = jnp.where(rows == DENSE, 1.0, 0.0).astype(BF)
        ones = jnp.where(lax.broadcasted_iota(jnp.int32, (16, n), 0) == 0, 1.0, 0.0).astype(BF)
        hid_s[D : D + 16, :] = ones
        for k in range(NE):
            mid_s[k, FH : FH + 16, :] = ones
        mix_s[2 * EO : 2 * EO + 16, :] = ones
        fg_s[NE * FH + 16 : FG, :] = jnp.zeros((FG - NE * FH - 16, n), BF)
        for ref in (dwa_s, dw1_s, dw2_s, dtw_s, dcol_s, dlog_s):
            ref[...] = jnp.zeros_like(ref)
        gates = []
        for side in range(2):
            base = HALF * FH * side
            start = 0
            for ref in p_refs[side]:
                size = ref.shape[0] * ref.shape[1]
                flat = ref[...].reshape(size, PC)
                if side == 0:
                    wat_s[start : start + size, :] = flat[:, 0:XR]
                w1_s[start : start + size, base : base + HALF * FH] = flat[:, 512:PC]
                gt_s[start : start + size, :] = flat[:, 384:512].astype(F32)
                start += size
            gates.append(swap_halves(gt_s[...].T[48 : 48 + NE], second_core))
            for k in range(HALF):
                block = w1_s[:, base + FH * k : base + FH * k + FH]
                w1t_s[base + FH * k : base + FH * k + FH, :] = (block.astype(F32).T * 0.5).astype(BF)
            at = 0
            for ref in q_refs[side]:
                for c in range(ref.shape[0]):
                    q_s[tab_ref[1 + at]] = ref[c].astype(F32)
                    at += 1
            cols = HALF * EO
            w2 = q_s[:, :, 0:cols].reshape(FH, cols) * 0.5
            w2_s[:, cols * side : cols * side + cols] = w2.astype(BF)
            w2t_s[cols * side : cols * side + cols, :] = w2.T.astype(BF)
            b1_s[side] = q_s[:, :, cols : cols + 128].reshape(FH, 128) * 0.5
            last = q_s[:, 0:osz, cols + 128 : QC].reshape(EO, 128)
            b2_s[side] = last * 0.5
            tower = last[:, 0:TW]
            rest = jnp.zeros_like(tower)
            both = jnp.concatenate([tower, rest] if side == 0 else [rest, tower], axis=1)
            tw_s[EO * side : EO * side + EO, :] = both.astype(BF)
            tt_s[:, EO * side : EO * side + EO] = (both.T * 0.5).astype(BF)
        wa_s[...] = wat_s[...].astype(F32).T.astype(BF)
        wa_ref[...] = wa_s[...]
        gates = jnp.concatenate(gates, axis=0)
        gt_s[0:16, 0:128] = gates[:, 0:128]
        w1t_s[NE * FH : NE * FH + 16, :] = gates.astype(BF)
        pad = jnp.concatenate([gates, jnp.zeros((112, D), F32)], axis=0)
        w1_s[:, NE * FH : FG] = pad.T.astype(BF)
        vec = vec_ref[...].T
        gb_s[...] = jnp.concatenate([swap_halves(vec[0:NE, 1 + s : 2 + s], second_core) for s in range(2)], axis=0)
        b1 = jnp.concatenate([vec[NE : NE + TW, 1 + s : 2 + s] for s in range(2)], axis=0)
        head = jnp.concatenate([vec[NE + TW : NE + 2 * TW, 1 + s : 2 + s] for s in range(2)], axis=0)
        last = jnp.concatenate([vec[NE + 2 * TW : NE + 2 * TW + 1, 1 + s : 2 + s] for s in range(2)] * 64, axis=0)
        tcol_s[...] = jnp.concatenate([b1 * 0.5, head, head * 0.5, last], axis=1)

    x_s[0:EMB, :] = emb_ref[...]
    x_s[EMB : EMB + DENSE, :] = dense_ref[...]
    x = x_s[...]
    hid = mm(wat_s[...], x).astype(BF)
    hid_s[0:D, :] = hid
    logits = mm(w1t_s[NE * FH : NE * FH + 16, :], hid) + gb_s[...]
    probs = []
    for t in range(2):
        lt = logits[NE * t : NE * t + NE]
        e = jnp.exp(lt - jnp.max(lt, axis=0, keepdims=True))
        probs.append(e / jnp.sum(e, axis=0, keepdims=True))
    mix = [None, None]
    pend = None
    nxt = mm(w1t_s[0:FH, :], hid)
    for k in range(NE + 1):
        h = nxt
        if k < NE - 1:
            nxt = mm(w1t_s[FH * (k + 1) : FH * (k + 2), :], hid)
        if k < NE:
            m, s = act_pair(h + b1_s[k // HALF, :, k % HALF : k % HALF + 1])
            mb = m.astype(BF)
            mid_s[k, 0:FH, :] = mb
            sl1_s[FH * k : FH * k + FH, :] = s.astype(BF)
            h2 = mm(w2t_s[EO * k : EO * k + EO, :], mb)
        if pend is not None:
            j = k - 1
            o, s = act_pair(pend + b2_s[j // HALF, :, TW + j % HALF : TW + j % HALF + 1])
            out_s[EO * j : EO * j + EO, :] = o.astype(out_s.dtype)
            sl2_s[EO * j : EO * j + EO, :] = s.astype(sl2_s.dtype)
            for t in range(2):
                term = probs[t][j : j + 1, :] * o
                mix[t] = term if j == 0 else mix[t] + term
        pend = h2
    mix_s[0:EO, :] = mix[0].astype(BF)
    mix_s[EO : 2 * EO, :] = mix[1].astype(BF)
    act, slope = act_pair(mm(tt_s[...], mix_s[0 : 2 * EO, :]) + tcol_s[:, 0:1])
    weighted = act * tcol_s[:, 1:2]
    lgos = []
    for t in range(2):
        logit = jnp.sum(weighted[TW * t : TW * t + TW], axis=0, keepdims=True) + tcol_s[t : t + 1, 3:4]
        lgos.append(row_ref[0:1, :] * (0.5 * jnp.tanh(0.5 * logit) + 0.5 - row_ref[1 + t : 2 + t, :]))
    lgo = jnp.concatenate([jnp.broadcast_to(lgos[t], (TW, n)) for t in range(2)], axis=0)
    dcol_s[...] += lane_fold(lgo * act)
    dlog_s[...] += lane_fold(jnp.concatenate([jnp.broadcast_to(lgos[t], (8, n)) for t in range(2)], axis=0))
    tg = (lgo * (tcol_s[:, 2:3] * slope)).astype(BF)
    dtw_s[...] += mm_nt(mix_s[...], tg)
    mgh = mm(tw_s[...], tg) * 0.5
    pgs = [[], []]
    mgs = [None] * NE
    for k in range(NE + 2):
        if k < NE:
            o = out_s[EO * k : EO * k + EO, :].astype(F32)
            og = None
            for t in range(2):
                mg = mgh[EO * t : EO * t + EO]
                pgs[t].append(jnp.sum(o * mg, axis=0, keepdims=True))
                term = probs[t][k : k + 1, :] * mg
                og = term if og is None else og + term
            sg = (og * sl2_s[EO * k : EO * k + EO, :].astype(F32)).astype(BF)
            sg_s[EO * k : EO * k + EO, :] = sg
            mgs[k] = mm(w2_s[:, EO * k : EO * k + EO], sg)
        if 1 <= k < NE + 1:
            j = k - 1
            dw2_s[:, EO * j : EO * j + EO] += mm_nt(mid_s[j], sg_s[EO * j : EO * j + EO, :])
            fg = (mgs[j] * sl1_s[FH * j : FH * j + FH, :].astype(F32)).astype(BF)
            fg_s[FH * j : FH * j + FH, :] = fg
        if k >= 2:
            j = k - 2
            dw1_s[:, FH * j : FH * j + FH] += mm_nt(hid_s[...], fg_s[FH * j : FH * j + FH, :])
    lgs = []
    for t in range(2):
        pg = jnp.concatenate(pgs[t], axis=0)
        lgs.append(2.0 * probs[t] * (pg - jnp.sum(probs[t] * pg, axis=0, keepdims=True)))
    fg_s[NE * FH : NE * FH + 16, :] = jnp.concatenate(lgs, axis=0).astype(BF)
    dw1_s[:, NE * FH : FG] += mm_nt(hid_s[...], fg_s[NE * FH : FG, :])
    hg = mm(w1_s[...], fg_s[...]).astype(BF)
    hg_ref[...] = hg
    dwa_s[...] += mm_nt(hg, x)
    eg = mm(wa_s[...], hg)
    eg_ref[...] = eg[0:EMB]
    dg_ref[...] = eg[EMB : EMB + DENSE]

    @pl.when(step == pl.num_programs(0) - 1)
    def _():
        gate = dw1_s[0 : D + 16, NE * FH : FG].T
        dlog = jnp.sum(dlog_s[...], axis=1, keepdims=True)
        dcol = jnp.sum(dcol_s[...].T, axis=0, keepdims=True)
        for side, (dp_ref, dq_ref) in enumerate(((dpo_ref, dqo_ref), (dpx_ref, dqx_ref))):
            own_gate = swap_halves(gate[NE * side : NE * side + NE], second_core)
            col = jnp.concatenate([own_gate[:, 0:D], jnp.zeros((120, D), F32)], axis=0).T
            dp_ref[:, 0:384] = dwa_s[:, 0:384].astype(BF)
            dp_ref[:, 384:512] = jnp.concatenate([dwa_s[:, 384:432], col[:, 0:80]], axis=1).astype(BF)
            dp_ref[:, 512:PC] = dw1_s[0:D, HALF * FH * side : HALF * FH * side + HALF * FH].astype(BF)
            b1 = [dw1_s[D : D + 1, FH * k : FH * k + FH] for k in range(HALF * side, HALF * side + HALF)]
            db1_s[...] = jnp.concatenate(b1 + [jnp.zeros((124, FH), F32)], axis=0).T
            b2 = [dw2_s[FH : FH + 1, EO * k : EO * k + EO] for k in range(HALF * side, HALF * side + HALF)]
            b2 = jnp.concatenate(b2 + [jnp.zeros((60, EO), F32)], axis=0).T
            tower = dtw_s[EO * side : EO * side + EO, TW * side : TW * side + TW]
            ob_s[...] = jnp.concatenate([tower, b2], axis=1)
            lanes = slice(TW * side, TW * side + TW)
            line = jnp.concatenate([dtw_s[2 * EO : 2 * EO + 1, lanes], dcol[:, lanes]], axis=1)
            gate_b = jnp.sum(jnp.where(lax.broadcasted_iota(jnp.int32, (NE, D + 16), 1) == D, own_gate, 0.0), axis=1, keepdims=True)
            small = jnp.concatenate([gate_b, dlog[8 * side : 8 * side + 8]], axis=0)
            small = jnp.concatenate([jnp.broadcast_to(small, (16, 128)), jnp.zeros((112, 128), F32)], axis=0).T[0:1]
            tail = jnp.concatenate([line, small, jnp.zeros((fs - osz - 2, 128), F32)], axis=0)
            for c in range(chunks):
                at = tab_ref[1 + c]
                body_rows = dw2_s[pl.ds(pl.multiple_of(at * fs, fs), fs), HALF * EO * side : HALF * EO * side + HALF * EO]
                dq_ref[fs * c : fs * c + fs, 0 : HALF * EO] = body_rows.astype(BF)
                dq_ref[fs * c : fs * c + fs, HALF * EO : HALF * EO + 128] = db1_s[pl.ds(pl.multiple_of(at * fs, fs), fs), :].astype(BF)
                o_rows = ob_s[pl.ds(pl.multiple_of(at * osz, osz), osz), :]
                dq_ref[fs * c : fs * c + fs, HALF * EO + 128 : QC] = jnp.concatenate([o_rows, tail], axis=0).astype(BF)


def main_call(table, embt, denset, rowdata, p_own, p_other, q_own, q_other):
    rows = embt.shape[1]
    half = rows // 2
    steps = half // TILE
    pieces = len(p_own)
    chunks = sum(a.shape[0] for a in q_own)

    def own(i, c):
        return (0, c[0] * steps + i)

    def const2(i, c):
        return (0, 0)

    def const3(i, c):
        return (0, 0, 0)

    weights = [*p_own, *p_other, *q_own, *q_other]
    vec_at = rows // 256
    spec = pltpu.PrefetchScalarGridSpec(
        num_scalar_prefetch=1,
        grid=(steps,),
        in_specs=[
            pl.BlockSpec((EMB, TILE), own),
            pl.BlockSpec((DENSE, TILE), own),
            pl.BlockSpec((8, TILE), own),
            pl.BlockSpec((8, 256), lambda i, c: (0, vec_at), pipeline_mode=pl.Buffered(1)),
        ]
        + [pl.BlockSpec(a.shape, const3, pipeline_mode=pl.Buffered(1)) for a in weights],
        out_specs=[
            pl.BlockSpec((EMB, TILE), own),
            pl.BlockSpec((DENSE, TILE), own),
            pl.BlockSpec((D, TILE), lambda i, c: (0, i)),
            pl.BlockSpec((XR, D), const2),
            pl.BlockSpec((D, PC), const2),
            pl.BlockSpec((D, PC), const2),
            pl.BlockSpec((FH, QC), const2),
            pl.BlockSpec((FH, QC), const2),
        ],
        scratch_shapes=[
            pltpu.VMEM((XR, TILE), BF),
            pltpu.VMEM((D + 16, TILE), BF),
            pltpu.VMEM((NE, FH + 16, TILE), BF),
            pltpu.VMEM((NE * FH, TILE), BF),
            pltpu.VMEM((NE * EO, TILE), F32),
            pltpu.VMEM((NE * EO, TILE), F32),
            pltpu.VMEM((NE * EO, TILE), BF),
            pltpu.VMEM((FG, TILE), BF),
            pltpu.VMEM((2 * EO + 16, TILE), BF),
            pltpu.VMEM((D, XR), BF),
            pltpu.VMEM((XR, D), BF),
            pltpu.VMEM((NE * FH + 16, D), BF),
            pltpu.VMEM((D, 128), F32),
            pltpu.VMEM((D, FG), BF),
            pltpu.VMEM((NE * EO, FH), BF),
            pltpu.VMEM((FH, NE * EO), BF),
            pltpu.VMEM((2, FH, 128), F32),
            pltpu.VMEM((2, EO, 128), F32),
            pltpu.VMEM((16, 1), F32),
            pltpu.VMEM((2 * TW, 2 * EO), BF),
            pltpu.VMEM((2 * EO, 2 * TW), BF),
            pltpu.VMEM((2 * TW, 4), F32),
            pltpu.VMEM((chunks, FH // chunks, QC), F32),
            pltpu.VMEM((D, XR), F32),
            pltpu.VMEM((D + 16, FG), F32),
            pltpu.VMEM((FH + 16, NE * EO), F32),
            pltpu.VMEM((2 * EO + 16, 2 * TW), F32),
            pltpu.VMEM((2 * TW, 128), F32),
            pltpu.VMEM((16, 128), F32),
            pltpu.VMEM((FH, 128), F32),
            pltpu.VMEM((EO, 128), F32),
        ],
    )
    return pl.pallas_call(
        functools.partial(main_kernel, pieces, chunks),
        grid_spec=spec,
        out_shape=[
            jax.ShapeDtypeStruct((EMB, rows), F32),
            jax.ShapeDtypeStruct((DENSE, rows), F32),
            jax.ShapeDtypeStruct((D, half), BF),
            jax.ShapeDtypeStruct((XR, D), BF),
            jax.ShapeDtypeStruct((D, PC), BF),
            jax.ShapeDtypeStruct((D, PC), BF),
            jax.ShapeDtypeStruct((FH, QC), BF),
            jax.ShapeDtypeStruct((FH, QC), BF),
        ],
        compiler_params=pltpu.CompilerParams(vmem_limit_bytes=60 * 1024 * 1024),
        cost_estimate=pl.CostEstimate(flops=30_000_000_000, bytes_accessed=24_000_000, transcendentals=0),
    )(table, embt, denset, rowdata, rowdata, *weights)


def other_kernel(tab_ref, hg_ref, wa_ref, eg_in, dg_in, eg_ref, dg_ref):
    eg = mm(wa_ref[...], hg_ref[...])
    eg_ref[...] = eg[0:EMB]
    dg_ref[...] = eg[EMB : EMB + DENSE]


def other_call(table, hg, wa, eg, dg):
    steps = hg.shape[1] // TILE

    def far(i, c):
        return (0, (1 - c[0]) * steps + i)

    spec = pltpu.PrefetchScalarGridSpec(
        num_scalar_prefetch=1,
        grid=(steps,),
        in_specs=[
            pl.BlockSpec((D, TILE), lambda i, c: (0, i)),
            pl.BlockSpec((XR, D), lambda i, c: (0, 0)),
            pl.BlockSpec(memory_space=pl.ANY),
            pl.BlockSpec(memory_space=pl.ANY),
        ],
        out_specs=[pl.BlockSpec((EMB, TILE), far), pl.BlockSpec((DENSE, TILE), far)],
    )
    return pl.pallas_call(
        other_kernel,
        grid_spec=spec,
        out_shape=[jax.ShapeDtypeStruct(eg.shape, F32), jax.ShapeDtypeStruct(dg.shape, F32)],
        input_output_aliases={3: 0, 4: 1},
        compiler_params=pltpu.CompilerParams(vmem_limit_bytes=32 * 1024 * 1024),
        cost_estimate=pl.CostEstimate(flops=1_500_000_000, bytes_accessed=9_000_000, transcendentals=0),
    )(table, hg, wa, eg, dg)


def hop(a, mask, size):
    return lax.ppermute(a, "rows", [(i, i ^ mask) for i in range(size)])


def partner(a):
    return lax.ppermute(a, "task", [(0, 1), (1, 0)])


def pad_to(a, rows, cols):
    return jnp.pad(a, ((0, rows - a.shape[0]), (0, cols - a.shape[1])))


def body(
    emb, dense, group_sizes, labels, w_emb, w_dense, b_in, expert_w1, expert_b1, expert_w2, expert_b2,
    gate_w, gate_b, tower_w1, tower_b1, tower_w2, tower_b2,
):
    size = lax.axis_size("rows")
    core = lax.axis_index("task")
    place = lax.axis_index("rows")
    batches = group_sizes.shape[0]
    batch_rows = emb.shape[0] // batches
    user_count = group_sizes.shape[1] * batches * size
    ds, fs, osz = D // size, FH // size, EO // size
    fast = size == 16

    first = jnp.concatenate([w_emb.T, w_dense.T, b_in[:, None], jnp.zeros((ds, 2), BF), gate_w[0], jnp.zeros((ds, 72), BF)], axis=1)
    p_shard = jnp.concatenate([first, jnp.transpose(expert_w1, (1, 0, 2)).reshape(ds, HALF * FH)], axis=1)
    q_shard = jnp.concatenate([jnp.transpose(expert_w2, (1, 0, 2)).reshape(fs, HALF * EO), pad_to(expert_b1.T, fs, 128)], axis=1)
    o_shard = pad_to(jnp.concatenate([tower_w1[0], expert_b2.T], axis=1), osz, 128)
    vec = jnp.concatenate([gate_b, tower_b1, tower_w2, tower_b2[:, None], jnp.zeros((1, 119), BF)], axis=1)
    line = jnp.concatenate([labels.astype(BF), vec], axis=1)
    far_line = partner(line)

    ends = jnp.cumsum(group_sizes, axis=1)
    starts = ends - group_sizes
    places = jnp.arange(batch_rows, dtype=jnp.int32)[None, :, None]
    inside = (places >= starts[:, None, :]) & (places < ends[:, None, :])
    inverse = 1.0 / group_sizes.astype(F32)
    weights_row = jnp.sum(jnp.where(inside, inverse[:, None, :], 0.0), axis=2).reshape(1, -1)
    weights_row = jnp.pad(weights_row, ((0, 0), (0, 256)))
    rowdata = jnp.concatenate([weights_row, line.astype(F32), far_line.astype(F32), jnp.zeros((5, line.shape[1]), F32)], axis=0)

    if fast:
        q_shard = jnp.concatenate([q_shard, pad_to(o_shard, fs, 128)], axis=1)
        zp = jnp.stack([p_shard] + [hop(p_shard, 4 * a, size) for a in range(1, 4)])
        zq = jnp.stack([q_shard] + [hop(q_shard, b, size) for b in range(1, 4)])
        p_own = [zp] + [hop(zp, b, size) for b in range(1, 4)]
        q_own = [zq] + [hop(zq, 4 * a, size) for a in range(1, 4)]
        order = place ^ jnp.arange(16, dtype=jnp.int32)
    else:
        q_all = lax.all_gather(q_shard, "rows", axis=0, tiled=True)
        o_all = lax.all_gather(o_shard, "rows", axis=0, tiled=True)
        p_own = [lax.all_gather(p_shard, "rows", axis=0, tiled=True)[None]]
        q_own = [jnp.concatenate([q_all, pad_to(o_all, FH, 128)], axis=1)[None]]
        order = jnp.zeros((1,), jnp.int32)
    p_other = [partner(a) for a in p_own]
    q_other = [partner(a) for a in q_own]
    table = jnp.concatenate([core[None].astype(jnp.int32), order])

    eg, dg, hg, wa, dp_own, dp_other, dq_own, dq_other = main_call(
        table, emb.T, dense.T, rowdata, p_own, p_other, q_own, q_other
    )
    dp = (dp_own.astype(F32) + partner(dp_other).astype(F32)).astype(BF)
    dq = (dq_own.astype(F32) + partner(dq_other).astype(F32)).astype(BF)
    far_hg = partner(hg)
    eg, dg = other_call(table, far_hg, wa, eg, dg)

    if fast:
        dp = dp.reshape(4, 4, ds, PC)
        dq = dq.reshape(4, 4, fs, QC)
        sp = dp[0].astype(F32) + sum(hop(dp[b], b, size).astype(F32) for b in range(1, 4))
        sq = dq[0].astype(F32) + sum(hop(dq[a], 4 * a, size).astype(F32) for a in range(1, 4))
        sp, sq = sp.astype(BF), sq.astype(BF)
        tp = sp[0].astype(F32) + sum(hop(sp[a], 4 * a, size).astype(F32) for a in range(1, 4))
        tq = sq[0].astype(F32) + sum(hop(sq[b], b, size).astype(F32) for b in range(1, 4))
        to = tq[0:osz, QC - 128 : QC]
        ts = tq[osz : osz + 2, QC - 128 : QC]
    else:
        tp = lax.psum_scatter(dp.astype(F32), "rows", scatter_dimension=0, tiled=True)
        tq = lax.psum_scatter(dq[:, 0 : QC - 128].astype(F32), "rows", scatter_dimension=0, tiled=True)
        to = lax.psum_scatter(dq[0:EO, QC - 128 : QC].astype(F32), "rows", scatter_dimension=0, tiled=True)
        ts = lax.psum(dq[EO : EO + 2, QC - 128 : QC].astype(F32), "rows")
    scale = 1.0 / user_count
    tp, tq, to, ts = tp * scale, tq * scale, to * scale, ts * scale
    return (
        eg.T,
        dg.T,
        tp[:, 0:EMB].T,
        tp[:, EMB : EMB + DENSE].T,
        tp[:, EMB + DENSE],
        jnp.transpose(tp[:, 512:PC].reshape(ds, HALF, FH), (1, 0, 2)),
        tq[:, HALF * EO : HALF * EO + HALF].T,
        jnp.transpose(tq[:, 0 : HALF * EO].reshape(fs, HALF, EO), (1, 0, 2)),
        to[:, TW : TW + HALF].T,
        tp[:, 432:440][None],
        ts[1:2, 0:NE],
        to[:, 0:TW][None],
        ts[0:1, 0:TW],
        ts[0:1, TW : 2 * TW],
        ts[1, NE : NE + 1],
    )


def solution(mesh):
    in_specs = (
        P("rows", None),
        P("rows", None),
        P("rows", None),
        P("task", "rows"),
        P(None, "rows"),
        P(None, "rows"),
        P("rows"),
        P("task", "rows", None),
        P("task", "rows"),
        P("task", "rows", None),
        P("task", "rows"),
        P("task", "rows", None),
        P("task", None),
        P("task", "rows", None),
        P("task", None),
        P("task", None),
        P("task"),
    )
    out_specs = (
        P("rows", None),
        P("rows", None),
        P(None, "rows"),
        P(None, "rows"),
        P("rows"),
        P("task", "rows", None),
        P("task", "rows"),
        P("task", "rows", None),
        P("task", "rows"),
        P("task", "rows", None),
        P("task", None),
        P("task", "rows", None),
        P("task", None),
        P("task", None),
        P("task"),
    )
    return jax.shard_map(body, mesh=mesh, in_specs=in_specs, out_specs=out_specs, check_vma=False)
```

```python
import functools

import jax
import jax.numpy as jnp
from jax import lax
from jax.experimental import pallas as pl
from jax.experimental.pallas import tpu as pltpu
from jax.sharding import PartitionSpec as P

F32 = jnp.float32
BF = jnp.bfloat16
NT = (((1,), (1,)), ((), ()))
D, FH, EO, TW, NE = 512, 256, 128, 64, 8
HALF = NE // 2
EMB, DENSE = 416, 13
XR = 448
QA = HALF * EO
QD = QA + 128
QC = QD + 512
B1, GA = 72, 80
FG = NE * FH + 128
TILE = 512


def mm(a, b):
    return jnp.dot(a, b, preferred_element_type=F32)


def mm_nt(a, b):
    return lax.dot_general(a, b, NT, preferred_element_type=F32)


def act_pair(half):
    t = jnp.tanh(half)
    q = 1.0 + t
    m = half * q
    return m, q + m * (1.0 - t)


def swap_halves(a, flag):
    return jnp.where(flag, jnp.concatenate([a[HALF:NE], a[0:HALF]], axis=0), a)


def lane_fold(a):
    total = a[:, 0:128]
    for c in range(1, a.shape[1] // 128):
        total = total + a[:, 128 * c : 128 * c + 128]
    return total


def p_order(at, chunks):
    return at if chunks == 1 else at % 4 * 4 + at // 4


def main_kernel(pieces, chunks, batch_rows, tab_ref, *refs):
    emb_ref, dense_ref, lab_ref, far_lab_ref, sizes_ref, vec_ref, far_vec_ref = refs[:7]
    p_refs = (refs[7 : 7 + pieces], refs[7 + pieces : 7 + 2 * pieces])
    q_refs = (refs[7 + 2 * pieces : 7 + 3 * pieces], refs[7 + 3 * pieces : 7 + 4 * pieces])
    refs = refs[7 + 4 * pieces :]
    hg_ref, wat_s = refs[:2]
    dp_refs, dq_refs = refs[2:4], refs[4:6]
    (
        x_s, hid_s, mid_s, sl1_s, out_s, sl2_s, sg_s, fg_s, mix_s,
        w1_s, w1t_s, ga_s, w2t_s, w2_s, b1_s, b2_s, gb_s, tt_s, tw_s, tcol_s, q_s, start_s, end_s, inv_s,
        dwa_s, dw1_s, dw2_s, dtw_s, dcol_s, dlog_s, dsm_s,
    ) = refs[6:]
    n = emb_ref.shape[1]
    fs, osz, ds = FH // chunks, EO // chunks, D // chunks
    step = pl.program_id(0)
    core = tab_ref[0]
    second_core = core == 1

    @pl.when(step == 0)
    def _():
        rows = lax.broadcasted_iota(jnp.int32, (32, n), 0)
        x_s[EMB:XR, :] = jnp.where(rows == DENSE, 1.0, 0.0).astype(BF)
        ones = jnp.where(lax.broadcasted_iota(jnp.int32, (16, n), 0) == 0, 1.0, 0.0).astype(BF)
        hid_s[D : D + 16, :] = ones
        for k in range(NE):
            mid_s[k, FH : FH + 16, :] = ones
        mix_s[2 * EO : 2 * EO + 16, :] = ones
        fg_s[NE * FH + 16 : FG, :] = jnp.zeros((FG - NE * FH - 16, n), BF)
        for ref in (dwa_s, dw1_s, dw2_s, dtw_s, dcol_s, dlog_s):
            ref[...] = jnp.zeros_like(ref)
        gates = []
        for side in range(2):
            base = HALF * FH * side
            at = 0
            for ref in p_refs[side]:
                for c in range(ref.shape[0]):
                    for k in range(HALF):
                        w1_s[ds * at : ds * at + ds, base + FH * k : base + FH * k + FH] = ref[c, k]
                    at += 1
            for k in range(HALF):
                block = w1_s[:, base + FH * k : base + FH * k + FH]
                w1t_s[base + FH * k : base + FH * k + FH, :] = (block.astype(F32).T * 0.5).astype(BF)
            holder = core if side == 0 else 1 - core
            at = 0
            for ref in q_refs[side]:
                for c in range(ref.shape[0]):
                    q_s[tab_ref[1 + at]] = ref[c, :, 0:QD].astype(F32)
                    small = ref[c, :, QA:QD].astype(F32)
                    to = ds * p_order(at, chunks)
                    ga_s[to : to + fs, :] = small
                    ga_s[to + fs : to + ds, :] = pltpu.roll(small, 128 - NE, 1)
                    wat_s[pl.ds(pl.multiple_of(to + holder * fs, fs), fs), :] = ref[c, :, QD : QD + XR]
                    at += 1
            gates.append(swap_halves(ga_s[...].T[GA : GA + NE], second_core))
            w2 = q_s[:, :, 0:QA].reshape(FH, QA) * 0.5
            w2_s[:, QA * side : QA * side + QA] = w2.astype(BF)
            w2t_s[QA * side : QA * side + QA, :] = w2.T.astype(BF)
            b1_s[side] = q_s[:, :, QA:QD].reshape(FH, 128) * 0.5
            last = q_s[:, 0:osz, QA:QD].reshape(EO, 128)
            b2_s[side] = last * 0.5
            tower = last[:, 0:TW]
            rest = jnp.zeros_like(tower)
            both = jnp.concatenate([tower, rest] if side == 0 else [rest, tower], axis=1)
            tw_s[EO * side : EO * side + EO, :] = both.astype(BF)
            tt_s[:, EO * side : EO * side + EO] = (both.T * 0.5).astype(BF)
        gates = jnp.concatenate(gates, axis=0)
        w1t_s[NE * FH : NE * FH + 16, :] = gates.astype(BF)
        pad = jnp.concatenate([gates, jnp.zeros((112, D), F32)], axis=0)
        w1_s[:, NE * FH : FG] = pad.T.astype(BF)
        vecs = [jnp.concatenate([r[...].astype(F32), jnp.zeros((112, 128), F32)], axis=0).T for r in (vec_ref, far_vec_ref)]
        gb_s[...] = jnp.concatenate([swap_halves(v[0:NE, 0:1], second_core) for v in vecs], axis=0)
        b1 = jnp.concatenate([v[0:TW, 1:2] for v in vecs], axis=0)
        head = jnp.concatenate([v[0:TW, 2:3] for v in vecs], axis=0)
        last = jnp.concatenate([v[0:1, 3:4] for v in vecs] * TW, axis=0)
        tcol_s[...] = jnp.concatenate([b1 * 0.5, head, head * 0.5, last], axis=1)
        users = sizes_ref.shape[1]
        counts = sizes_ref[...].astype(F32)
        turned = jnp.concatenate([counts, jnp.zeros((128 - counts.shape[0], users), F32)], axis=0).T
        upto = lax.broadcasted_iota(jnp.int32, (users, users), 1) <= lax.broadcasted_iota(jnp.int32, (users, users), 0)
        ends = mm(jnp.where(upto, 1.0, 0.0).astype(BF), turned.astype(BF))
        starts = ends - turned
        for b in range(counts.shape[0]):
            end_s[b] = jnp.broadcast_to(ends[:, b : b + 1], (users, 128))
            start_s[b] = jnp.broadcast_to(starts[:, b : b + 1], (users, 128))
            inv_s[b] = jnp.broadcast_to(1.0 / turned[:, b : b + 1], (users, 128))

    batch_steps = batch_rows // n
    at_step = core * pl.num_programs(0) + step
    batch = at_step // batch_steps
    first_row = (at_step % batch_steps * n).astype(F32)
    row_weight = []
    for c in range(n // 128):
        row_at = first_row + (lax.broadcasted_iota(jnp.int32, (1, 128), 1) + 128 * c).astype(F32)
        inside = (row_at >= start_s[batch]) & (row_at < end_s[batch])
        row_weight.append(jnp.sum(jnp.where(inside, inv_s[batch], 0.0), axis=0, keepdims=True))
    row_weight = jnp.concatenate(row_weight, axis=1)
    labels = (lab_ref[...].astype(F32), far_lab_ref[...].astype(F32))
    x_s[0:EMB, :] = emb_ref[...]
    x_s[EMB : EMB + DENSE, :] = dense_ref[...]
    x = x_s[...]
    hid = mm(wat_s[...], x).astype(BF)
    hid_s[0:D, :] = hid
    logits = mm(w1t_s[NE * FH : NE * FH + 16, :], hid) + gb_s[...]
    probs = []
    for t in range(2):
        lt = logits[NE * t : NE * t + NE]
        e = jnp.exp(lt - jnp.max(lt, axis=0, keepdims=True))
        probs.append(e / jnp.sum(e, axis=0, keepdims=True))
    mix = [None, None]
    pend = None
    nxt = mm(w1t_s[0:FH, :], hid)
    for k in range(NE + 1):
        h = nxt
        if k < NE - 1:
            nxt = mm(w1t_s[FH * (k + 1) : FH * (k + 2), :], hid)
        if k < NE:
            m, s = act_pair(h + b1_s[k // HALF, :, B1 + k % HALF : B1 + k % HALF + 1])
            mb = m.astype(BF)
            mid_s[k, 0:FH, :] = mb
            sl1_s[FH * k : FH * k + FH, :] = s.astype(BF)
            h2 = mm(w2t_s[EO * k : EO * k + EO, :], mb)
        if pend is not None:
            j = k - 1
            o, s = act_pair(pend + b2_s[j // HALF, :, TW + j % HALF : TW + j % HALF + 1])
            out_s[EO * j : EO * j + EO, :] = o.astype(out_s.dtype)
            sl2_s[EO * j : EO * j + EO, :] = s.astype(sl2_s.dtype)
            for t in range(2):
                term = probs[t][j : j + 1, :] * o
                mix[t] = term if j == 0 else mix[t] + term
        pend = h2
    mix_s[0:EO, :] = mix[0].astype(BF)
    mix_s[EO : 2 * EO, :] = mix[1].astype(BF)
    act, slope = act_pair(mm(tt_s[...], mix_s[0 : 2 * EO, :]) + tcol_s[:, 0:1])
    weighted = act * tcol_s[:, 1:2]
    lgos = []
    for t in range(2):
        logit = jnp.sum(weighted[TW * t : TW * t + TW], axis=0, keepdims=True) + tcol_s[t : t + 1, 3:4]
        lgos.append(row_weight * (0.5 * jnp.tanh(0.5 * logit) + 0.5 - labels[t]))
    lgo = jnp.concatenate([jnp.broadcast_to(lgos[t], (TW, n)) for t in range(2)], axis=0)
    dcol_s[...] += lane_fold(lgo * act)
    dlog_s[...] += lane_fold(jnp.concatenate([jnp.broadcast_to(lgos[t], (8, n)) for t in range(2)], axis=0))
    tg = (lgo * (tcol_s[:, 2:3] * slope)).astype(BF)
    dtw_s[...] += mm_nt(mix_s[...], tg)
    mgh = mm(tw_s[...], tg) * 0.5
    pgs = [[], []]
    mgs = [None] * NE
    for k in range(NE + 2):
        if k < NE:
            o = out_s[EO * k : EO * k + EO, :].astype(F32)
            og = None
            for t in range(2):
                mg = mgh[EO * t : EO * t + EO]
                pgs[t].append(jnp.sum(o * mg, axis=0, keepdims=True))
                term = probs[t][k : k + 1, :] * mg
                og = term if og is None else og + term
            sg = (og * sl2_s[EO * k : EO * k + EO, :].astype(F32)).astype(BF)
            sg_s[EO * k : EO * k + EO, :] = sg
            mgs[k] = mm(w2_s[:, EO * k : EO * k + EO], sg)
        if 1 <= k < NE + 1:
            j = k - 1
            dw2_s[:, EO * j : EO * j + EO] += mm_nt(mid_s[j], sg_s[EO * j : EO * j + EO, :])
            fg = (mgs[j] * sl1_s[FH * j : FH * j + FH, :].astype(F32)).astype(BF)
            fg_s[FH * j : FH * j + FH, :] = fg
        if k >= 2:
            j = k - 2
            dw1_s[:, FH * j : FH * j + FH] += mm_nt(hid_s[...], fg_s[FH * j : FH * j + FH, :])
    lgs = []
    for t in range(2):
        pg = jnp.concatenate(pgs[t], axis=0)
        lgs.append(2.0 * probs[t] * (pg - jnp.sum(probs[t] * pg, axis=0, keepdims=True)))
    fg_s[NE * FH : NE * FH + 16, :] = jnp.concatenate(lgs, axis=0).astype(BF)
    dw1_s[:, NE * FH : FG] += mm_nt(hid_s[...], fg_s[NE * FH : FG, :])
    hg = mm(w1_s[...], fg_s[...]).astype(BF)
    hg_ref[...] = hg
    dwa_s[...] += mm_nt(hg, x)

    @pl.when(step == pl.num_programs(0) - 1)
    def _():
        gate = dw1_s[:, NE * FH : FG].T
        dlog = jnp.sum(dlog_s[...], axis=1, keepdims=True)
        dcol = jnp.sum(dcol_s[...].T, axis=0, keepdims=True)
        for side in range(2):
            ref = dp_refs[side]
            for c in range(chunks):
                for k in range(HALF):
                    base = HALF * FH * side + FH * k
                    ref[c, k] = dw1_s[ds * c : ds * c + ds, base : base + FH].astype(BF)
            own_gate = swap_halves(gate[NE * side : NE * side + NE], second_core)
            gate_rows = jnp.concatenate([own_gate[:, 0:D], jnp.zeros((120, D), F32)], axis=0).T
            b1 = [dw1_s[D : D + 1, FH * k : FH * k + FH] for k in range(HALF * side, HALF * side + HALF)]
            b1 = jnp.concatenate(b1 + [jnp.zeros((124, FH), F32)], axis=0).T
            b2 = [dw2_s[FH : FH + 1, EO * k : EO * k + EO] for k in range(HALF * side, HALF * side + HALF)]
            b2 = jnp.concatenate(b2 + [jnp.zeros((60, EO), F32)], axis=0).T
            tower = dtw_s[EO * side : EO * side + EO, TW * side : TW * side + TW]
            tower = jnp.concatenate([tower, b2], axis=1)
            lanes = slice(TW * side, TW * side + TW)
            blank = jnp.zeros((1, TW), F32)
            lines = [jnp.concatenate([a, blank], axis=1) for a in (dtw_s[2 * EO : 2 * EO + 1, lanes], dcol[:, lanes])]
            gate_b = jnp.sum(jnp.where(lax.broadcasted_iota(jnp.int32, (NE, D + 16), 1) == D, own_gate, 0.0), axis=1, keepdims=True)
            small = jnp.concatenate([gate_b, dlog[8 * side : 8 * side + 8]], axis=0)
            small = jnp.concatenate([jnp.broadcast_to(small, (16, 128)), jnp.zeros((112, 128), F32)], axis=0).T[0:1]
            tail = jnp.concatenate(lines + [small, jnp.zeros((fs - osz - 3, 128), F32)], axis=0)
            b1 = pltpu.roll(b1, B1, 1)
            for c in range(chunks):
                dsm_s[fs * c : fs * c + fs, :] = b1[fs * c : fs * c + fs] + jnp.concatenate([tower[osz * c : osz * c + osz], tail], axis=0)
            ref = dq_refs[side]
            holder = core if side == 0 else 1 - core
            for c in range(chunks):
                where = pl.ds(pl.multiple_of(tab_ref[1 + c] * fs, fs), fs)
                ref[c, :, 0:QA] = dw2_s[where, QA * side : QA * side + QA].astype(BF)
                to = ds * p_order(c, chunks)
                low = pltpu.roll(gate_rows[to : to + fs], GA, 1)
                high = pltpu.roll(gate_rows[to + fs : to + ds], GA + NE, 1)
                ref[c, :, QA:QD] = (dsm_s[where, :] + low + high).astype(BF)
                ref[c, :, QD : QD + XR] = dwa_s[pl.ds(pl.multiple_of(to + holder * fs, fs), fs), :].astype(BF)
                ref[c, :, QD + XR : QC] = jnp.zeros((fs, QC - QD - XR), BF)


def const2(i, c):
    return (0, 0)


def const3(i, c):
    return (0, 0, 0)


def const4(i, c):
    return (0, 0, 0, 0)


def main_call(table, embt, denset, labels, far_labels, sizes, vec, far_vec, p_own, p_other, q_own, q_other):
    rows = embt.shape[1]
    half = rows // 2
    steps = half // TILE
    pieces = len(p_own)
    chunks = sum(a.shape[0] for a in q_own)
    fs, ds = FH // chunks, D // chunks
    batches, users = sizes.shape

    def own(i, c):
        return (0, c[0] * steps + i)

    grads = [(chunks, HALF, ds, FH)] * 2 + [(chunks, fs, QC)] * 2
    spec = pltpu.PrefetchScalarGridSpec(
        num_scalar_prefetch=1,
        grid=(steps,),
        in_specs=[
            pl.BlockSpec((EMB, TILE), own),
            pl.BlockSpec((DENSE, TILE), own),
            pl.BlockSpec((1, TILE), own),
            pl.BlockSpec((1, TILE), own),
        ]
        + [whole()] * (3 + 4 * pieces),
        out_specs=[pl.BlockSpec((D, TILE), lambda i, c: (0, i))] + [whole()] * 5,
        scratch_shapes=[
            pltpu.VMEM((XR, TILE), BF),
            pltpu.VMEM((D + 16, TILE), BF),
            pltpu.VMEM((NE, FH + 16, TILE), BF),
            pltpu.VMEM((NE * FH, TILE), BF),
            pltpu.VMEM((NE * EO, TILE), F32),
            pltpu.VMEM((NE * EO, TILE), F32),
            pltpu.VMEM((NE * EO, TILE), BF),
            pltpu.VMEM((FG, TILE), BF),
            pltpu.VMEM((2 * EO + 16, TILE), BF),
            pltpu.VMEM((D, FG), BF),
            pltpu.VMEM((NE * FH + 16, D), BF),
            pltpu.VMEM((D, 128), F32),
            pltpu.VMEM((NE * EO, FH), BF),
            pltpu.VMEM((FH, NE * EO), BF),
            pltpu.VMEM((2, FH, 128), F32),
            pltpu.VMEM((2, EO, 128), F32),
            pltpu.VMEM((16, 1), F32),
            pltpu.VMEM((2 * TW, 2 * EO), BF),
            pltpu.VMEM((2 * EO, 2 * TW), BF),
            pltpu.VMEM((2 * TW, 4), F32),
            pltpu.VMEM((chunks, fs, QD), F32),
            pltpu.VMEM((batches, users, 128), F32),
            pltpu.VMEM((batches, users, 128), F32),
            pltpu.VMEM((batches, users, 128), F32),
            pltpu.VMEM((D, XR), F32),
            pltpu.VMEM((D + 16, FG), F32),
            pltpu.VMEM((FH + 16, NE * EO), F32),
            pltpu.VMEM((2 * EO + 16, 2 * TW), F32),
            pltpu.VMEM((2 * TW, 128), F32),
            pltpu.VMEM((16, 128), F32),
            pltpu.VMEM((FH, 128), F32),
        ],
    )
    return pl.pallas_call(
        functools.partial(main_kernel, pieces, chunks, rows // batches),
        grid_spec=spec,
        out_shape=[jax.ShapeDtypeStruct((D, half), BF), jax.ShapeDtypeStruct((D, XR), BF)]
        + [jax.ShapeDtypeStruct(a, BF) for a in grads],
        compiler_params=pltpu.CompilerParams(vmem_limit_bytes=48 * 1024 * 1024),
        cost_estimate=pl.CostEstimate(flops=50_000_000_000, bytes_accessed=24_000_000, transcendentals=0),
        name="experts",
    )(table, embt, denset, labels, far_labels, sizes, vec, far_vec, *p_own, *p_other, *q_own, *q_other)


def input_kernel(steps, tab_ref, own_ref, far_ref, wat_ref, token_ref, eg_ref, dg_ref, done_ref, wa_s):
    step = pl.program_id(0)

    @pl.when(step == 0)
    def _():
        done_ref[...] = jnp.zeros_like(done_ref)
        wa_s[...] = wat_ref[...].astype(F32).T.astype(BF)

    def emit(ref):
        eg = mm(wa_s[...], ref[...])
        eg_ref[...] = eg[0:EMB]
        dg_ref[...] = eg[EMB : EMB + DENSE]

    @pl.when(step < steps)
    def _():
        emit(own_ref)

    @pl.when(step >= steps)
    def _():
        emit(far_ref)


def input_call(table, own_hg, far_hg, wat, token):
    half = own_hg.shape[1]
    tile = 2 * TILE
    steps = half // tile

    def place(i, c):
        near = i < steps
        return (0, jnp.where(near, c[0] * steps + i, (1 - c[0]) * steps + i - steps))

    spec = pltpu.PrefetchScalarGridSpec(
        num_scalar_prefetch=1,
        grid=(2 * steps,),
        in_specs=[
            pl.BlockSpec((D, tile), lambda i, c: (0, jnp.minimum(i, steps - 1))),
            pl.BlockSpec((D, tile), lambda i, c: (0, jnp.maximum(i - steps, 0))),
            whole(),
            whole(pl.ANY),
        ],
        out_specs=[pl.BlockSpec((EMB, tile), place), pl.BlockSpec((DENSE, tile), place), pl.BlockSpec((8, 128), const2)],
        scratch_shapes=[pltpu.VMEM((XR, D), BF)],
    )
    return pl.pallas_call(
        functools.partial(input_kernel, steps),
        grid_spec=spec,
        out_shape=[jax.ShapeDtypeStruct((EMB, 2 * half), F32), jax.ShapeDtypeStruct((DENSE, 2 * half), F32), jax.ShapeDtypeStruct((8, 128), F32)],
        compiler_params=pltpu.CompilerParams(vmem_limit_bytes=48 * 1024 * 1024),
        cost_estimate=pl.CostEstimate(flops=6_000_000_000, bytes_accessed=18_000_000, transcendentals=0),
        name="input_grads",
    )(table, own_hg, far_hg, wat, token)


def widen(a):
    return jnp.concatenate([a.astype(F32), jnp.zeros((a.shape[0], 128 - a.shape[1]), F32)], axis=1)


def square(rows):
    count = sum(a.shape[0] for a in rows)
    return jnp.concatenate(rows + [jnp.zeros((128 - count, 128), F32)], axis=0)


def pack_vec(gb_ref, t1_ref, t2_ref, t3_ref):
    return jnp.concatenate([widen(r[...]) for r in (gb_ref, t1_ref, t2_ref, t3_ref)] + [jnp.zeros((12, 128), F32)], axis=0).astype(BF)


def pack_kernel(core_ref, emb_ref, dense_ref, bias_ref, w2_ref, b1_ref, b2_ref, gate_ref, tower_ref, *refs):
    q_ref, vec_ref = refs[4:]
    vec_ref[...] = pack_vec(*refs[:4])
    fs = q_ref.shape[0]
    turned = square([widen(r[...]) for r in (b1_ref, b2_ref, gate_ref, dense_ref, bias_ref)]).T
    lane = lax.broadcasted_iota(jnp.int32, (fs, 128), 1)
    low, high = turned[0:fs], turned[fs : 2 * fs]
    small = jnp.concatenate([widen(tower_ref[...]), jnp.zeros((fs - tower_ref.shape[0], 128), F32)], axis=0)
    small += jnp.where((lane >= TW) & (lane < TW + HALF), pltpu.roll(low, TW - HALF, 1), 0.0)
    small += jnp.where(((lane >= B1) & (lane < B1 + HALF)) | ((lane >= GA) & (lane < GA + NE)), pltpu.roll(low, B1, 1), 0.0)
    small += jnp.where((lane >= GA + NE) & (lane < GA + 2 * NE), pltpu.roll(high, GA, 1), 0.0)
    for k in range(HALF):
        q_ref[:, EO * k : EO * k + EO] = w2_ref[k]
    q_ref[:, QA:QD] = small.astype(BF)
    second_core = core_ref[0] == 1
    lanes = lax.broadcasted_iota(jnp.int32, (2 * fs, 128), 1)
    last = widen(emb_ref[:, 384:EMB]) + jnp.where((lanes >= 32) & (lanes < 33 + DENSE), pltpu.roll(turned[0 : 2 * fs], 16, 1), 0.0)
    for c in range(3):
        block = emb_ref[:, 128 * c : 128 * c + 128]
        q_ref[:, QD + 128 * c : QD + 128 * c + 128] = jnp.where(second_core, block[fs:], block[0:fs])
    q_ref[:, QD + 384 : QC] = jnp.where(second_core, last[fs:], last[0:fs]).astype(BF)


def whole(memory=pltpu.VMEM):
    return pl.BlockSpec(memory_space=memory)


def pack_call(core, *parts):
    fs = parts[3].shape[1]
    return pl.pallas_call(
        pack_kernel,
        in_specs=[whole(pltpu.SMEM)] + [whole() for _ in parts],
        out_specs=[whole(), whole()],
        out_shape=[jax.ShapeDtypeStruct((fs, QC), BF), jax.ShapeDtypeStruct((16, 128), BF)],
        name="pack",
    )(core, *parts)


def sum_kernel(groups, count, *refs):
    ins, outs = refs[:count], refs[-len(groups) :]
    for group, out in zip(groups, outs):
        total = None
        for number, at in group:
            term = (ins[number][...] if at is None else ins[number][at]).astype(F32)
            total = term if total is None else total + term
        out[...] = total.astype(out.dtype)


def sum_call(name, arrays, groups, shapes, token=None, dtype=BF):
    shapes = [jax.ShapeDtypeStruct(a, dtype) for a in shapes]
    extra = [] if token is None else [token]
    return pl.pallas_call(
        functools.partial(sum_kernel, groups, len(arrays)),
        in_specs=[whole() for _ in arrays] + [whole(pl.ANY) for _ in extra],
        out_specs=[whole() for _ in shapes],
        out_shape=shapes,
        compiler_params=pltpu.CompilerParams(vmem_limit_bytes=32 * 1024 * 1024),
        name=name,
    )(*arrays, *extra)


def finish_kernel(scale, core_ref, far_ref, *refs):
    tp, tq = [sum(r[...].astype(F32) for r in refs[4 * j : 4 * j + 4]) * scale for j in range(2)]
    own_part, far_part = tq[:, QD : QD + XR], far_ref[...] * scale
    second_core = core_ref[0] == 1
    ta = jnp.concatenate([jnp.where(second_core, far_part, own_part), jnp.where(second_core, own_part, far_part)], axis=0)
    emb_ref, dense_ref, bias_ref, w1_ref, b1_ref, w2_ref, b2_ref, gate_ref, gb_ref, tower_ref, t1_ref, t2_ref, t3_ref = refs[8:]
    fs = tq.shape[0]
    osz = tower_ref.shape[0]
    w1_ref[...] = tp
    for k in range(HALF):
        w2_ref[k] = tq[:, EO * k : EO * k + EO]
    small = tq[:, QA:QD]
    turned = square([small]).T
    b1_ref[...] = turned[B1 : B1 + HALF, 0:fs]
    b2_ref[...] = turned[TW : TW + HALF, 0:osz]
    gates = turned[GA : GA + NE] + pltpu.roll(turned[GA + NE : GA + 2 * NE], fs, 1)
    gate_ref[...] = gates[:, 0 : 2 * fs]
    tower_ref[...] = small[0:osz, 0:TW]
    t1_ref[...] = small[osz : osz + 1, 0:TW]
    t2_ref[...] = small[osz + 1 : osz + 2, 0:TW]
    gb_ref[...] = small[osz + 2 : osz + 3, 0:NE]
    t3_ref[...] = small[osz + 2 : osz + 3, NE : NE + 1]
    emb_ref[...] = ta[:, 0:EMB]
    last = square([widen(ta[:, 384:XR])]).T
    dense_ref[...] = last[32 : 32 + DENSE, 0 : 2 * fs]
    bias_ref[...] = last[32 + DENSE : 33 + DENSE, 0 : 2 * fs]


def last_kernel(*refs):
    refs[4][...] = sum(r[:, QD : QD + XR].astype(F32) for r in refs[:4])


def last_call(arrays):
    return pl.pallas_call(
        last_kernel,
        in_specs=[whole() for _ in arrays],
        out_specs=whole(),
        out_shape=jax.ShapeDtypeStruct((arrays[0].shape[0], XR), F32),
        name="sum_last",
    )(*arrays)


def finish_call(scale, core, far, arrays, ds, fs, osz):
    shapes = [
        (ds, EMB), (DENSE, ds), (1, ds), (HALF, ds, FH), (HALF, fs), (HALF, fs, EO), (HALF, osz), (NE, ds), (1, NE),
        (osz, TW), (1, TW), (1, TW), (1, 1),
    ]
    return pl.pallas_call(
        functools.partial(finish_kernel, scale),
        in_specs=[whole(pltpu.SMEM), whole()] + [whole() for _ in arrays],
        out_specs=[whole() for _ in shapes],
        out_shape=[jax.ShapeDtypeStruct(a, F32) for a in shapes],
        name="finish",
    )(core, far, *arrays)


def join_kernel(*refs):
    ins, (p_ref, q_ref) = refs[:8], refs[8:]
    for j in range(4):
        p_ref[j] = ins[j][...]
        q_ref[j] = ins[4 + j][...]


def join_call(parts_p, parts_q):
    return pl.pallas_call(
        join_kernel,
        in_specs=[whole() for _ in range(8)],
        out_specs=[whole(), whole()],
        out_shape=[jax.ShapeDtypeStruct((4, *a[0].shape), BF) for a in (parts_p, parts_q)],
        name="join",
    )(*parts_p, *parts_q)


def hop(a, mask, size):
    return lax.ppermute(a, "rows", [(i, i ^ mask) for i in range(size)])


def partner(a):
    return lax.ppermute(a, "task", [(0, 1), (1, 0)])


def add_wide(a, b):
    return a.astype(F32) + b.astype(F32)


def pad_to(a, rows, cols):
    return jnp.pad(a, ((0, rows - a.shape[0]), (0, cols - a.shape[1])))


def body(
    emb, dense, group_sizes, labels, w_emb, w_dense, b_in, expert_w1, expert_b1, expert_w2, expert_b2,
    gate_w, gate_b, tower_w1, tower_b1, tower_w2, tower_b2,
):
    size = lax.axis_size("rows")
    core = lax.axis_index("task")
    place = lax.axis_index("rows")
    user_count = group_sizes.shape[1] * group_sizes.shape[0] * size
    ds, fs, osz = D // size, FH // size, EO // size
    fast = size == 16
    far_labels = partner(labels)
    smalls = (gate_b, tower_b1, tower_w2, tower_b2[None])

    if fast:
        one_core = core[None].astype(jnp.int32)
        gate_t = jnp.transpose(gate_w, (0, 2, 1))[0]
        q_shard, vec = pack_call(
            one_core, w_emb.T, w_dense, b_in[None], expert_w2, expert_b1, expert_b2, gate_t, tower_w1[0], *smalls
        )
        near_p = [expert_w1] + [hop(expert_w1, 4 * a, size) for a in range(1, 4)]
        near_q = [q_shard] + [hop(q_shard, b, size) for b in range(1, 4)]
        zp, zq = join_call(near_p, near_q)
        p_own = [zp] + [hop(zp, b, size) for b in range(1, 4)]
        q_own = [zq] + [hop(zq, 4 * a, size) for a in range(1, 4)]
        order = place ^ jnp.arange(16, dtype=jnp.int32)
    else:
        gather = functools.partial(lax.all_gather, axis_name="rows", axis=0, tiled=True)
        proj = jnp.concatenate([w_emb.T, w_dense.T, b_in[:, None], jnp.zeros((ds, 82), BF)], axis=1)
        w2_all = gather(jnp.transpose(expert_w2, (1, 0, 2)).reshape(fs, QA))
        o_all = gather(jnp.concatenate([tower_w1[0], expert_b2.T], axis=1))
        b1_all, g_all, proj_all = gather(expert_b1.T), gather(gate_w[0]), gather(proj)
        small = jnp.concatenate([pad_to(o_all, FH, B1), pad_to(b1_all, FH, GA - B1), g_all[0:FH], g_all[FH:], jnp.zeros((FH, 32), BF)], axis=1)
        part = jnp.where(core == 0, proj_all[0:FH], proj_all[FH:])
        q_own = [jnp.concatenate([w2_all, small, part], axis=1)[None]]
        p_own = [lax.all_gather(expert_w1, "rows", axis=1, tiled=True)[None]]
        order = jnp.zeros((1,), jnp.int32)
        vec = jnp.concatenate([pad_to(a, 1, 128) for a in smalls] + [jnp.zeros((12, 128), BF)], axis=0)
    p_other = [partner(a) for a in p_own]
    q_other = [partner(a) for a in q_own]
    table = jnp.concatenate([core[None].astype(jnp.int32), order])

    hg, wat, dp_own, dp_far, dq_own, dq_far = main_call(
        table, emb.T, dense.T, labels, far_labels, group_sizes, vec, partner(vec), p_own, p_other, q_own, q_other
    )
    dp_far, dq_far = partner(dp_far), partner(dq_far)
    far_hg = partner(hg)
    scale = 1.0 / user_count
    if fast:
        p_shape, q_shape = (HALF, ds, FH), (fs, QC)
        groups = [[(j, slice(4 * b, 4 * b + 4)), (j + 1, slice(4 * b, 4 * b + 4))] for j in (0, 2) for b in range(1, 4)]
        sums = sum_call("sum_cores", [dp_own, dp_far, dq_own, dq_far], groups, [(4, *p_shape)] * 3 + [(4, *q_shape)] * 3)
        got_p = [hop(sums[b - 1], b, size) for b in range(1, 4)]
        got_q = [hop(sums[2 + a], 4 * a, size) for a in range(1, 4)]
        eg, dg, token = input_call(table, hg, far_hg, wat, sums[0])
        groups = [[(j, k) for j in range(start, start + 5)] for start in (0, 5) for k in range(4)]
        arrays = [dp_own, dp_far, *got_p, dq_own, dq_far, *got_q]
        sums = sum_call("sum_first", arrays, groups, [p_shape] * 4 + [q_shape] * 4, token)
        parts_p = [sums[0]] + [hop(sums[a], 4 * a, size) for a in range(1, 4)]
        parts_q = [sums[4]] + [hop(sums[4 + b], b, size) for b in range(1, 4)]
        far_input = partner(last_call(parts_q))
        out = finish_call(scale, one_core, far_input, parts_p + parts_q, ds, fs, osz)
        g_emb, g_dense, g_bias, g_w1, g_b1, g_w2, g_b2, g_gate, g_gb, g_tower, g_t1, g_t2, g_t3 = out
        return (
            eg.T, dg.T, g_emb.T, g_dense, g_bias[0], g_w1, g_b1, g_w2, g_b2, g_gate.T[None], g_gb, g_tower[None], g_t1, g_t2, g_t3[0],
        )
    eg, dg, _ = input_call(table, hg, far_hg, wat, dp_far)
    scatter = functools.partial(lax.psum_scatter, axis_name="rows", scatter_dimension=0, tiled=True)
    dp, wide = add_wide(dp_own[0], dp_far[0]), add_wide(dq_own[0], dq_far[0])
    small = wide[:, QA:QD]
    near, far = wide[:, QD : QD + XR], partner(wide[:, QD : QD + XR])
    ta = scatter(jnp.concatenate([jnp.where(core == 0, near, far), jnp.where(core == 0, far, near)], axis=0)) * scale
    tp = lax.psum_scatter(dp, "rows", scatter_dimension=1, tiled=True) * scale
    tw2, to, tb1 = scatter(wide[:, 0:QA]) * scale, scatter(small[0:EO, 0:B1]) * scale, scatter(small[:, B1 : B1 + HALF]) * scale
    tg = scatter(jnp.concatenate([small[:, GA : GA + NE], small[:, GA + NE : GA + 2 * NE]], axis=0)) * scale
    ts = lax.psum(small[EO : EO + 3], "rows") * scale
    return (
        eg.T,
        dg.T,
        ta[:, 0:EMB].T,
        ta[:, EMB : EMB + DENSE].T,
        ta[:, EMB + DENSE],
        tp,
        tb1.T,
        jnp.transpose(tw2.reshape(fs, HALF, EO), (1, 0, 2)),
        to[:, TW : TW + HALF].T,
        tg[None],
        ts[2:3, 0:NE],
        to[:, 0:TW][None],
        ts[0:1, 0:TW],
        ts[1:2, 0:TW],
        ts[2, NE : NE + 1],
    )


def solution(mesh):
    in_specs = (
        P("rows", None),
        P("rows", None),
        P("rows", None),
        P("task", "rows"),
        P(None, "rows"),
        P(None, "rows"),
        P("rows"),
        P("task", "rows", None),
        P("task", "rows"),
        P("task", "rows", None),
        P("task", "rows"),
        P("task", "rows", None),
        P("task", None),
        P("task", "rows", None),
        P("task", None),
        P("task", None),
        P("task"),
    )
    out_specs = (
        P("rows", None),
        P("rows", None),
        P(None, "rows"),
        P(None, "rows"),
        P("rows"),
        P("task", "rows", None),
        P("task", "rows"),
        P("task", "rows", None),
        P("task", "rows"),
        P("task", "rows", None),
        P("task", None),
        P("task", "rows", None),
        P("task", None),
        P("task", None),
        P("task"),
    )
    return jax.shard_map(body, mesh=mesh, in_specs=in_specs, out_specs=out_specs, check_vma=False)
```

```python
import functools

import jax
import jax.numpy as jnp
from jax import lax
from jax.experimental import pallas as pl
from jax.experimental.pallas import tpu as pltpu
from jax.sharding import PartitionSpec as P

F32 = jnp.float32
BF = jnp.bfloat16
NT = (((1,), (1,)), ((), ()))
D, FH, EO, TW, NE = 512, 256, 128, 64, 8
HALF = NE // 2
EMB, DENSE = 416, 13
XR = 448
QA = HALF * FH
QS = QA + HALF * EO
UC = QS + 128
B1, GA = 72, 80
FG = NE * FH + 128
TILE = 512


def mm(a, b):
    return jnp.dot(a, b, preferred_element_type=F32)


def mm_nt(a, b):
    return lax.dot_general(a, b, NT, preferred_element_type=F32)


def act_pair(half):
    t = jnp.tanh(half)
    q = 1.0 + t
    m = half * q
    return m, q + m * (1.0 - t)


def swap_halves(a, flag):
    return jnp.where(flag, jnp.concatenate([a[HALF:NE], a[0:HALF]], axis=0), a)


def lane_fold(a):
    total = a[:, 0:128]
    for c in range(1, a.shape[1] // 128):
        total = total + a[:, 128 * c : 128 * c + 128]
    return total


def chunk_at(n, chunks, flag):
    if chunks == 1 or n // 4 in (0, 3):
        return n
    return n + 4 * flag if n // 4 == 1 else n - 4 * flag


def main_kernel(pieces, chunks, tab_ref, *refs):
    emb_ref, dense_ref, lab_ref, far_lab_ref, row_ref, vec_ref, far_vec_ref = refs[:7]
    u_refs = (refs[7 : 7 + pieces], refs[7 + pieces : 7 + 2 * pieces])
    hg_ref, wat_s, *du_refs = refs[7 + 2 * pieces : 11 + 2 * pieces]
    (
        x_s, hid_s, mid_s, sl1_s, out_s, sl2_s, sg_s, fg_s, mix_s,
        w1_s, w1t_s, ga_s, w2t_s, w2_s, b1_s, b2_s, gb_s, tt_s, tw_s, tcol_s, q_s,
        dwa_s, dw1_s, dw2_s, dtw_s, dcol_s, dlog_s, dsm_s, u_s, sem,
    ) = refs[11 + 2 * pieces :]
    n = emb_ref.shape[1]
    fs, osz, ds = FH // chunks, EO // chunks, D // chunks
    step = pl.program_id(0)
    core = tab_ref[0]
    second_core = core == 1

    @pl.when(step == 0)
    def _():
        copies = [[], []]
        for side in range(2):
            at = 0
            for j, ref in enumerate(u_refs[side]):
                copies[side].append(pltpu.make_async_copy(ref, u_s.at[side, pl.ds(at, ref.shape[0])], sem.at[pieces * side + j]))
                copies[side][-1].start()
                at += ref.shape[0]
        rows = lax.broadcasted_iota(jnp.int32, (32, n), 0)
        x_s[EMB:XR, :] = jnp.where(rows == DENSE, 1.0, 0.0).astype(BF)
        ones = jnp.where(lax.broadcasted_iota(jnp.int32, (16, n), 0) == 0, 1.0, 0.0).astype(BF)
        hid_s[D : D + 16, :] = ones
        for k in range(NE):
            mid_s[k, FH : FH + 16, :] = ones
        mix_s[2 * EO : 2 * EO + 16, :] = ones
        fg_s[NE * FH + 16 : FG, :] = jnp.zeros((FG - NE * FH - 16, n), BF)
        for ref in (dwa_s, dw1_s, dw2_s, dtw_s, dcol_s, dlog_s):
            ref[...] = jnp.zeros_like(ref)
        gates = []
        for side in range(2):
            for copy in copies[side]:
                copy.wait()
            base = HALF * FH * side
            holder = core if side == 0 else 1 - core
            for c in range(chunks):
                at = chunk_at(c, chunks, holder)
                to = pl.multiple_of(ds * at, ds)
                w1_s[pl.ds(to, ds), base : base + QA] = u_s[side, c, :, 0:QA]
                q_s[tab_ref[1 + at]] = u_s[side, c, 0:fs, QA:UC].astype(F32)
                small = u_s[side, c, 0:fs, QS:UC].astype(F32)
                ga_s[pl.ds(to, fs), :] = small
                ga_s[pl.ds(pl.multiple_of(to + fs, fs), fs), :] = pltpu.roll(small, 128 - NE, 1)
                wat_s[pl.ds(pl.multiple_of(to + holder * fs, fs), fs), :] = u_s[side, c, fs:ds, QA : QA + XR]
            for k in range(HALF):
                block = w1_s[:, base + FH * k : base + FH * k + FH]
                w1t_s[base + FH * k : base + FH * k + FH, :] = (block.astype(F32).T * 0.5).astype(BF)
            gates.append(swap_halves(ga_s[...].T[GA : GA + NE], second_core))
            cols = HALF * EO
            w2 = q_s[:, :, 0:cols].reshape(FH, cols) * 0.5
            w2_s[:, cols * side : cols * side + cols] = w2.astype(BF)
            w2t_s[cols * side : cols * side + cols, :] = w2.T.astype(BF)
            b1_s[side] = q_s[:, :, cols : cols + 128].reshape(FH, 128) * 0.5
            last = q_s[:, 0:osz, cols : cols + 128].reshape(EO, 128)
            b2_s[side] = last * 0.5
            tower = last[:, 0:TW]
            rest = jnp.zeros_like(tower)
            both = jnp.concatenate([tower, rest] if side == 0 else [rest, tower], axis=1)
            tw_s[EO * side : EO * side + EO, :] = both.astype(BF)
            tt_s[:, EO * side : EO * side + EO] = (both.T * 0.5).astype(BF)
        gates = jnp.concatenate(gates, axis=0)
        w1t_s[NE * FH : NE * FH + 16, :] = gates.astype(BF)
        pad = jnp.concatenate([gates, jnp.zeros((112, D), F32)], axis=0)
        w1_s[:, NE * FH : FG] = pad.T.astype(BF)
        vecs = [jnp.concatenate([r[...].astype(F32), jnp.zeros((112, 128), F32)], axis=0).T for r in (vec_ref, far_vec_ref)]
        gb_s[...] = jnp.concatenate([swap_halves(v[0:NE, 0:1], second_core) for v in vecs], axis=0)
        b1 = jnp.concatenate([v[0:TW, 1:2] for v in vecs], axis=0)
        head = jnp.concatenate([v[0:TW, 2:3] for v in vecs], axis=0)
        last = jnp.concatenate([v[0:1, 3:4] for v in vecs] * TW, axis=0)
        tcol_s[...] = jnp.concatenate([b1 * 0.5, head, head * 0.5, last], axis=1)

    row_weight = row_ref[...]
    labels = (lab_ref[...].astype(F32), far_lab_ref[...].astype(F32))
    x_s[0:EMB, :] = emb_ref[...]
    x_s[EMB : EMB + DENSE, :] = dense_ref[...]
    x = x_s[...]
    hid = mm(wat_s[...], x).astype(BF)
    hid_s[0:D, :] = hid
    logits = mm(w1t_s[NE * FH : NE * FH + 16, :], hid) + gb_s[...]
    probs = []
    for t in range(2):
        lt = logits[NE * t : NE * t + NE]
        e = jnp.exp(lt - jnp.max(lt, axis=0, keepdims=True))
        probs.append(e / jnp.sum(e, axis=0, keepdims=True))
    mix = [None, None]
    pend = None
    nxt = mm(w1t_s[0:FH, :], hid)
    for k in range(NE + 1):
        h = nxt
        if k < NE - 1:
            nxt = mm(w1t_s[FH * (k + 1) : FH * (k + 2), :], hid)
        if k < NE:
            m, s = act_pair(h + b1_s[k // HALF, :, B1 + k % HALF : B1 + k % HALF + 1])
            mb = m.astype(BF)
            mid_s[k, 0:FH, :] = mb
            sl1_s[FH * k : FH * k + FH, :] = s.astype(BF)
            h2 = mm(w2t_s[EO * k : EO * k + EO, :], mb)
        if pend is not None:
            j = k - 1
            o, s = act_pair(pend + b2_s[j // HALF, :, TW + j % HALF : TW + j % HALF + 1])
            out_s[EO * j : EO * j + EO, :] = o.astype(out_s.dtype)
            sl2_s[EO * j : EO * j + EO, :] = s.astype(sl2_s.dtype)
            for t in range(2):
                term = probs[t][j : j + 1, :] * o
                mix[t] = term if j == 0 else mix[t] + term
        pend = h2
    mix_s[0:EO, :] = mix[0].astype(BF)
    mix_s[EO : 2 * EO, :] = mix[1].astype(BF)
    act, slope = act_pair(mm(tt_s[...], mix_s[0 : 2 * EO, :]) + tcol_s[:, 0:1])
    weighted = act * tcol_s[:, 1:2]
    lgos = []
    for t in range(2):
        logit = jnp.sum(weighted[TW * t : TW * t + TW], axis=0, keepdims=True) + tcol_s[t : t + 1, 3:4]
        lgos.append(row_weight * (0.5 * jnp.tanh(0.5 * logit) + 0.5 - labels[t]))
    lgo = jnp.concatenate([jnp.broadcast_to(lgos[t], (TW, n)) for t in range(2)], axis=0)
    dcol_s[...] += lane_fold(lgo * act)
    dlog_s[...] += lane_fold(jnp.concatenate([jnp.broadcast_to(lgos[t], (8, n)) for t in range(2)], axis=0))
    tg = (lgo * (tcol_s[:, 2:3] * slope)).astype(BF)
    dtw_s[...] += mm_nt(mix_s[...], tg)
    mgh = mm(tw_s[...], tg) * 0.5
    pgs = [[], []]
    mgs = [None] * NE
    for k in range(NE + 2):
        if k < NE:
            o = out_s[EO * k : EO * k + EO, :].astype(F32)
            og = None
            for t in range(2):
                mg = mgh[EO * t : EO * t + EO]
                pgs[t].append(jnp.sum(o * mg, axis=0, keepdims=True))
                term = probs[t][k : k + 1, :] * mg
                og = term if og is None else og + term
            sg = (og * sl2_s[EO * k : EO * k + EO, :].astype(F32)).astype(BF)
            sg_s[EO * k : EO * k + EO, :] = sg
            mgs[k] = mm(w2_s[:, EO * k : EO * k + EO], sg)
        if 1 <= k < NE + 1:
            j = k - 1
            dw2_s[:, EO * j : EO * j + EO] += mm_nt(mid_s[j], sg_s[EO * j : EO * j + EO, :])
            fg = (mgs[j] * sl1_s[FH * j : FH * j + FH, :].astype(F32)).astype(BF)
            fg_s[FH * j : FH * j + FH, :] = fg
        if k >= 2:
            j = k - 2
            dw1_s[:, FH * j : FH * j + FH] += mm_nt(hid_s[...], fg_s[FH * j : FH * j + FH, :])
    lgs = []
    for t in range(2):
        pg = jnp.concatenate(pgs[t], axis=0)
        lgs.append(2.0 * probs[t] * (pg - jnp.sum(probs[t] * pg, axis=0, keepdims=True)))
    fg_s[NE * FH : NE * FH + 16, :] = jnp.concatenate(lgs, axis=0).astype(BF)
    dw1_s[:, NE * FH : FG] += mm_nt(hid_s[...], fg_s[NE * FH : FG, :])
    hg = mm(w1_s[...], fg_s[...]).astype(BF)
    hg_ref[...] = hg
    dwa_s[...] += mm_nt(hg, x)

    @pl.when(step == pl.num_programs(0) - 1)
    def _():
        gate = dw1_s[:, NE * FH : FG].T
        dlog = jnp.sum(dlog_s[...], axis=1, keepdims=True)
        dcol = jnp.sum(dcol_s[...].T, axis=0, keepdims=True)
        for side in range(2):
            own_gate = swap_halves(gate[NE * side : NE * side + NE], second_core)
            ga_s[...] = jnp.concatenate([own_gate[:, 0:D], jnp.zeros((120, D), F32)], axis=0).T
            b1 = [dw1_s[D : D + 1, FH * k : FH * k + FH] for k in range(HALF * side, HALF * side + HALF)]
            b1 = jnp.concatenate(b1 + [jnp.zeros((124, FH), F32)], axis=0).T
            b2 = [dw2_s[FH : FH + 1, EO * k : EO * k + EO] for k in range(HALF * side, HALF * side + HALF)]
            b2 = jnp.concatenate(b2 + [jnp.zeros((60, EO), F32)], axis=0).T
            tower = dtw_s[EO * side : EO * side + EO, TW * side : TW * side + TW]
            tower = jnp.concatenate([tower, b2], axis=1)
            lanes = slice(TW * side, TW * side + TW)
            blank = jnp.zeros((1, TW), F32)
            lines = [jnp.concatenate([a, blank], axis=1) for a in (dtw_s[2 * EO : 2 * EO + 1, lanes], dcol[:, lanes])]
            gate_b = jnp.sum(jnp.where(lax.broadcasted_iota(jnp.int32, (NE, D + 16), 1) == D, own_gate, 0.0), axis=1, keepdims=True)
            small = jnp.concatenate([gate_b, dlog[8 * side : 8 * side + 8]], axis=0)
            small = jnp.concatenate([jnp.broadcast_to(small, (16, 128)), jnp.zeros((112, 128), F32)], axis=0).T[0:1]
            tail = jnp.concatenate(lines + [small, jnp.zeros((fs - osz - 3, 128), F32)], axis=0)
            b1 = pltpu.roll(b1, B1, 1)
            for c in range(chunks):
                dsm_s[fs * c : fs * c + fs, :] = b1[fs * c : fs * c + fs] + jnp.concatenate([tower[osz * c : osz * c + osz], tail], axis=0)
            ref = du_refs[side]
            holder = core if side == 0 else 1 - core
            cols = HALF * EO
            for c in range(chunks):
                at = chunk_at(c, chunks, holder)
                to = pl.multiple_of(ds * at, ds)
                where = pl.ds(pl.multiple_of(tab_ref[1 + at] * fs, fs), fs)
                ref[c, :, 0:QA] = dw1_s[pl.ds(to, ds), QA * side : QA * side + QA].astype(BF)
                ref[c, 0:fs, QA:QS] = dw2_s[where, cols * side : cols * side + cols].astype(BF)
                low = pltpu.roll(ga_s[pl.ds(to, fs), :], GA, 1)
                high = pltpu.roll(ga_s[pl.ds(pl.multiple_of(to + fs, fs), fs), :], GA + NE, 1)
                ref[c, 0:fs, QS:UC] = (dsm_s[where, :] + low + high).astype(BF)
                lower = dwa_s[pl.ds(pl.multiple_of(to + holder * fs, fs), fs), :]
                ref[c, fs:ds, QA:UC] = jnp.concatenate([lower, jnp.zeros((fs, UC - QA - XR), F32)], axis=1).astype(BF)


def weight_kernel(batch_rows, tab_ref, sizes_ref, token_ref, out_ref, start_s, end_s, inv_s):
    users = sizes_ref.shape[1]
    counts = sizes_ref[...].astype(F32)
    turned = jnp.concatenate([counts, jnp.zeros((128 - counts.shape[0], users), F32)], axis=0).T
    upto = lax.broadcasted_iota(jnp.int32, (users, users), 1) <= lax.broadcasted_iota(jnp.int32, (users, users), 0)
    ends = mm(jnp.where(upto, 1.0, 0.0).astype(BF), turned.astype(BF))
    starts = ends - turned
    for b in range(counts.shape[0]):
        end_s[b] = jnp.broadcast_to(ends[:, b : b + 1], (users, 128))
        start_s[b] = jnp.broadcast_to(starts[:, b : b + 1], (users, 128))
        inv_s[b] = jnp.broadcast_to(1.0 / turned[:, b : b + 1], (users, 128))
    steps = out_ref.shape[1] // TILE
    for step in range(steps):
        at_step = tab_ref[0] * steps + step
        batch = at_step // (batch_rows // TILE)
        first_row = (at_step % (batch_rows // TILE) * TILE).astype(F32)
        for c in range(TILE // 128):
            row_at = first_row + (lax.broadcasted_iota(jnp.int32, (1, 128), 1) + 128 * c).astype(F32)
            inside = (row_at >= start_s[batch]) & (row_at < end_s[batch])
            at = TILE * step + 128 * c
            out_ref[:, at : at + 128] = jnp.sum(jnp.where(inside, inv_s[batch], 0.0), axis=0, keepdims=True)


def weight_call(table, sizes, rows, token):
    batches, users = sizes.shape
    return pl.pallas_call(
        functools.partial(weight_kernel, rows // batches),
        in_specs=[whole(pltpu.SMEM), whole(), whole(pl.ANY)],
        out_specs=whole(),
        out_shape=jax.ShapeDtypeStruct((1, rows // 2), F32),
        scratch_shapes=[pltpu.VMEM((batches, users, 128), F32)] * 3,
        cost_estimate=pl.CostEstimate(flops=3_000_000_000, bytes_accessed=1_000_000, transcendentals=0),
        name="row_weights",
    )(table, sizes, token)


def const2(i, c):
    return (0, 0)


def main_call(table, embt, denset, labels, far_labels, row_weights, vec, far_vec, own_u, far_u):
    rows = embt.shape[1]
    half = rows // 2
    steps = half // TILE
    pieces = len(own_u)
    chunks = sum(a.shape[0] for a in own_u)
    fs, ds = FH // chunks, D // chunks

    def own(i, c):
        return (0, c[0] * steps + i)

    grads = [(chunks, ds, UC)] * 2
    spec = pltpu.PrefetchScalarGridSpec(
        num_scalar_prefetch=1,
        grid=(steps,),
        in_specs=[
            pl.BlockSpec((EMB, TILE), own),
            pl.BlockSpec((DENSE, TILE), own),
            pl.BlockSpec((1, TILE), own),
            pl.BlockSpec((1, TILE), own),
            pl.BlockSpec((1, TILE), lambda i, c: (0, i)),
            whole(),
            whole(),
        ]
        + [whole(pl.ANY) for _ in (*own_u, *far_u)],
        out_specs=[pl.BlockSpec((D, TILE), lambda i, c: (0, i))] + [whole()] * 3,
        scratch_shapes=[
            pltpu.VMEM((XR, TILE), BF),
            pltpu.VMEM((D + 16, TILE), BF),
            pltpu.VMEM((NE, FH + 16, TILE), BF),
            pltpu.VMEM((NE * FH, TILE), BF),
            pltpu.VMEM((NE * EO, TILE), F32),
            pltpu.VMEM((NE * EO, TILE), F32),
            pltpu.VMEM((NE * EO, TILE), BF),
            pltpu.VMEM((FG, TILE), BF),
            pltpu.VMEM((2 * EO + 16, TILE), BF),
            pltpu.VMEM((D, FG), BF),
            pltpu.VMEM((NE * FH + 16, D), BF),
            pltpu.VMEM((D, 128), F32),
            pltpu.VMEM((NE * EO, FH), BF),
            pltpu.VMEM((FH, NE * EO), BF),
            pltpu.VMEM((2, FH, 128), F32),
            pltpu.VMEM((2, EO, 128), F32),
            pltpu.VMEM((16, 1), F32),
            pltpu.VMEM((2 * TW, 2 * EO), BF),
            pltpu.VMEM((2 * EO, 2 * TW), BF),
            pltpu.VMEM((2 * TW, 4), F32),
            pltpu.VMEM((chunks, fs, UC - QA), F32),
            pltpu.VMEM((D, XR), F32),
            pltpu.VMEM((D + 16, FG), F32),
            pltpu.VMEM((FH + 16, NE * EO), F32),
            pltpu.VMEM((2 * EO + 16, 2 * TW), F32),
            pltpu.VMEM((2 * TW, 128), F32),
            pltpu.VMEM((16, 128), F32),
            pltpu.VMEM((FH, 128), F32),
            pltpu.VMEM((2, chunks, ds, UC), BF),
            pltpu.SemaphoreType.DMA((2 * pieces,)),
        ],
    )
    return pl.pallas_call(
        functools.partial(main_kernel, pieces, chunks),
        grid_spec=spec,
        out_shape=[jax.ShapeDtypeStruct((D, half), BF), jax.ShapeDtypeStruct((D, XR), BF)]
        + [jax.ShapeDtypeStruct(a, BF) for a in grads],
        compiler_params=pltpu.CompilerParams(vmem_limit_bytes=48 * 1024 * 1024),
        cost_estimate=pl.CostEstimate(flops=50_000_000_000, bytes_accessed=24_000_000, transcendentals=0),
        name="experts",
    )(table, embt, denset, labels, far_labels, row_weights, vec, far_vec, *own_u, *far_u)


def input_kernel(tab_ref, hg_ref, wat_ref, *refs):
    eg_ref, dg_ref, done_ref, wa_s = refs[-4:]

    @pl.when(pl.program_id(0) == 0)
    def _():
        wa_s[...] = wat_ref[...].astype(F32).T.astype(BF)
        done_ref[...] = jnp.zeros_like(done_ref)

    eg = mm(wa_s[...], hg_ref[...])
    eg_ref[...] = eg[0:EMB]
    dg_ref[...] = eg[EMB : EMB + DENSE]


def input_call(table, hg, wat, token, other, name):
    half = hg.shape[1]
    tile = 2 * TILE
    steps = half // tile

    def place(i, c):
        return (0, (c[0] if other is None else 1 - c[0]) * steps + i)

    extra = [token] + (list(other) if other is not None else [])
    spec = pltpu.PrefetchScalarGridSpec(
        num_scalar_prefetch=1,
        grid=(steps,),
        in_specs=[pl.BlockSpec((D, tile), lambda i, c: (0, i)), pl.BlockSpec((D, XR), const2, pipeline_mode=pl.Buffered(1))]
        + [whole(pl.ANY) for _ in extra],
        out_specs=[pl.BlockSpec((EMB, tile), place), pl.BlockSpec((DENSE, tile), place), pl.BlockSpec((8, 128), const2)],
        scratch_shapes=[pltpu.VMEM((XR, D), BF)],
    )
    return pl.pallas_call(
        input_kernel,
        grid_spec=spec,
        out_shape=[jax.ShapeDtypeStruct((EMB, 2 * half), F32), jax.ShapeDtypeStruct((DENSE, 2 * half), F32), jax.ShapeDtypeStruct((8, 128), F32)],
        input_output_aliases={} if other is None else {4: 0, 5: 1},
        compiler_params=pltpu.CompilerParams(vmem_limit_bytes=32 * 1024 * 1024),
        cost_estimate=pl.CostEstimate(flops=4_000_000_000, bytes_accessed=9_000_000, transcendentals=0),
        name=name,
    )(table, hg, wat, *extra)


def widen(a):
    return jnp.concatenate([a.astype(F32), jnp.zeros((a.shape[0], 128 - a.shape[1]), F32)], axis=1)


def square(rows):
    count = sum(a.shape[0] for a in rows)
    return jnp.concatenate(rows + [jnp.zeros((128 - count, 128), F32)], axis=0)


def pack_vec(gb_ref, t1_ref, t2_ref, t3_ref):
    return jnp.concatenate([widen(r[...]) for r in (gb_ref, t1_ref, t2_ref, t3_ref)] + [jnp.zeros((12, 128), F32)], axis=0).astype(BF)


def pack_kernel(core_ref, emb_ref, dense_ref, bias_ref, w1_ref, w2_ref, b1_ref, b2_ref, gate_ref, tower_ref, *refs):
    u_ref, vec_ref = refs[4:]
    vec_ref[...] = pack_vec(*refs[:4])
    fs = u_ref.shape[0] // 2
    turned = square([widen(r[...]) for r in (b1_ref, b2_ref, gate_ref, dense_ref, bias_ref)]).T
    lane = lax.broadcasted_iota(jnp.int32, (fs, 128), 1)
    low, high = turned[0:fs], turned[fs : 2 * fs]
    small = jnp.concatenate([widen(tower_ref[...]), jnp.zeros((fs - tower_ref.shape[0], 128), F32)], axis=0)
    small += jnp.where((lane >= TW) & (lane < TW + HALF), pltpu.roll(low, TW - HALF, 1), 0.0)
    small += jnp.where(((lane >= B1) & (lane < B1 + HALF)) | ((lane >= GA) & (lane < GA + NE)), pltpu.roll(low, B1, 1), 0.0)
    small += jnp.where((lane >= GA + NE) & (lane < GA + 2 * NE), pltpu.roll(high, GA, 1), 0.0)
    for k in range(HALF):
        u_ref[:, FH * k : FH * k + FH] = w1_ref[k]
        u_ref[0:fs, QA + EO * k : QA + EO * k + EO] = w2_ref[k]
    u_ref[0:fs, QS:UC] = small.astype(BF)
    second_core = core_ref[0] == 1
    lanes = lax.broadcasted_iota(jnp.int32, (2 * fs, 128), 1)
    last = widen(emb_ref[:, 384:EMB]) + jnp.where((lanes >= 32) & (lanes < 33 + DENSE), pltpu.roll(turned[0 : 2 * fs], 16, 1), 0.0)
    for c in range(3):
        block = emb_ref[:, 128 * c : 128 * c + 128]
        u_ref[fs:, QA + 128 * c : QA + 128 * c + 128] = jnp.where(second_core, block[fs:], block[0:fs])
    u_ref[fs:, QA + 384 : QA + 512] = jnp.where(second_core, last[fs:], last[0:fs]).astype(BF)
    u_ref[fs:, QA + 512 : UC] = jnp.zeros((fs, UC - QA - 512), BF)


def whole(memory=pltpu.VMEM):
    return pl.BlockSpec(memory_space=memory)


def pack_call(core, *parts):
    ds = parts[3].shape[1]
    return pl.pallas_call(
        pack_kernel,
        in_specs=[whole(pltpu.SMEM)] + [whole() for _ in parts],
        out_specs=[whole(), whole()],
        out_shape=[jax.ShapeDtypeStruct((ds, UC), BF), jax.ShapeDtypeStruct((16, 128), BF)],
        name="pack",
    )(core, *parts)


def sum_kernel(groups, count, *refs):
    ins, outs = refs[:count], refs[-len(groups) :]
    for group, out in zip(groups, outs):
        total = None
        for number, at in group:
            term = ins[number][at].astype(F32)
            total = term if total is None else total + term
        out[...] = total.astype(out.dtype)


def sum_call(name, arrays, groups, shapes, token=None, through=None):
    extra = [a for a in (token, through) if a is not None]
    lead = [] if through is None else [through]
    return pl.pallas_call(
        functools.partial(sum_kernel, groups, len(arrays)),
        in_specs=[whole() for _ in arrays] + [whole(pl.ANY) for _ in extra],
        out_specs=[whole(pl.ANY) for _ in lead] + [whole() for _ in shapes],
        out_shape=[jax.ShapeDtypeStruct(a.shape, a.dtype) for a in lead] + [jax.ShapeDtypeStruct(a, BF) for a in shapes],
        input_output_aliases={len(arrays) + len(extra) - 1: 0} if lead else {},
        compiler_params=pltpu.CompilerParams(vmem_limit_bytes=32 * 1024 * 1024),
        name=name,
    )(*arrays, *extra)


def finish_kernel(scale, core_ref, token_ref, far_ref, *refs):
    total = sum(r[...].astype(F32) for r in refs[:4]) * scale
    ds = total.shape[0]
    fs = ds // 2
    own_part, far_part = total[fs:, QA : QA + XR], far_ref[...] * scale
    second_core = core_ref[0] == 1
    ta = jnp.concatenate([jnp.where(second_core, far_part, own_part), jnp.where(second_core, own_part, far_part)], axis=0)
    emb_ref, dense_ref, bias_ref, w1_ref, b1_ref, w2_ref, b2_ref, gate_ref, gb_ref, tower_ref, t1_ref, t2_ref, t3_ref = refs[4:]
    osz = tower_ref.shape[0]
    for k in range(HALF):
        w1_ref[k] = total[:, FH * k : FH * k + FH]
        w2_ref[k] = total[0:fs, QA + EO * k : QA + EO * k + EO]
    small = total[0:fs, QS:UC]
    turned = square([small]).T
    b1_ref[...] = turned[B1 : B1 + HALF, 0:fs]
    b2_ref[...] = turned[TW : TW + HALF, 0:osz]
    gates = turned[GA : GA + NE] + pltpu.roll(turned[GA + NE : GA + 2 * NE], fs, 1)
    gate_ref[...] = gates[:, 0 : 2 * fs]
    tower_ref[...] = small[0:osz, 0:TW]
    t1_ref[...] = small[osz : osz + 1, 0:TW]
    t2_ref[...] = small[osz + 1 : osz + 2, 0:TW]
    gb_ref[...] = small[osz + 2 : osz + 3, 0:NE]
    t3_ref[...] = small[osz + 2 : osz + 3, NE : NE + 1]
    emb_ref[...] = ta[:, 0:EMB]
    last = square([widen(ta[:, 384:XR])]).T
    dense_ref[...] = last[32 : 32 + DENSE, 0 : 2 * fs]
    bias_ref[...] = last[32 + DENSE : 33 + DENSE, 0 : 2 * fs]


def last_kernel(*refs):
    fs = refs[4].shape[0]
    refs[4][...] = sum(r[fs:, QA : QA + XR].astype(F32) for r in refs[:4])


def last_call(arrays):
    return pl.pallas_call(
        last_kernel,
        in_specs=[whole() for _ in arrays],
        out_specs=whole(),
        out_shape=jax.ShapeDtypeStruct((arrays[0].shape[0] // 2, XR), F32),
        name="sum_last",
    )(*arrays)


def finish_call(scale, core, token, far, arrays, ds, fs, osz):
    shapes = [
        (ds, EMB), (DENSE, ds), (1, ds), (HALF, ds, FH), (HALF, fs), (HALF, fs, EO), (HALF, osz), (NE, ds), (1, NE),
        (osz, TW), (1, TW), (1, TW), (1, 1),
    ]
    return pl.pallas_call(
        functools.partial(finish_kernel, scale),
        in_specs=[whole(pltpu.SMEM), whole(pl.ANY), whole()] + [whole() for _ in arrays],
        out_specs=[whole() for _ in shapes],
        out_shape=[jax.ShapeDtypeStruct(a, F32) for a in shapes],
        name="finish",
    )(core, token, far, *arrays)


def join_kernel(token_ref, *refs):
    for j in range(4):
        refs[4][j] = refs[j][...]


def join_call(parts, token):
    return pl.pallas_call(
        join_kernel,
        in_specs=[whole(pl.ANY)] + [whole() for _ in parts],
        out_specs=whole(),
        out_shape=jax.ShapeDtypeStruct((4, *parts[0].shape), BF),
        name="join",
    )(token, *parts)


def hop(a, mask, size):
    return lax.ppermute(a, "rows", [(i, i ^ mask) for i in range(size)])


def cross(a, masks, size):
    pairs = [(2 * i + t, 2 * (i ^ masks[t]) + t) for i in range(size) for t in range(2)]
    return lax.ppermute(a, ("rows", "task"), pairs)


def partner(a):
    return lax.ppermute(a, "task", [(0, 1), (1, 0)])


def add_wide(a, b):
    return a.astype(F32) + b.astype(F32)


def pad_to(a, rows, cols):
    return jnp.pad(a, ((0, rows - a.shape[0]), (0, cols - a.shape[1])))


def body(
    emb, dense, group_sizes, labels, w_emb, w_dense, b_in, expert_w1, expert_b1, expert_w2, expert_b2,
    gate_w, gate_b, tower_w1, tower_b1, tower_w2, tower_b2,
):
    size = lax.axis_size("rows")
    core = lax.axis_index("task")
    place = lax.axis_index("rows")
    user_count = group_sizes.shape[1] * group_sizes.shape[0] * size
    ds, fs, osz = D // size, FH // size, EO // size
    fast = size == 16
    far_labels = partner(labels)
    smalls = (gate_b, tower_b1, tower_w2, tower_b2[None])

    if fast:
        one_core = core[None].astype(jnp.int32)
        gate_t = jnp.transpose(gate_w, (0, 2, 1))[0]
        shard, vec = pack_call(
            one_core, w_emb.T, w_dense, b_in[None], expert_w1, expert_w2, expert_b1, expert_b2, gate_t, tower_w1[0], *smalls
        )
        row_weights = weight_call(one_core, group_sizes, emb.shape[0], vec)
        near = join_call([shard] + [hop(shard, 4 * a, size) for a in range(1, 4)], row_weights)
        near = jnp.concatenate([near, cross(near, (1, 2), size)], axis=0)
        own_u = [near, cross(near, (2, 1), size)]
        steps = jnp.arange(16, dtype=jnp.int32)
        order = place ^ (steps % 4 * 4 + steps // 4)
    else:
        gather = functools.partial(lax.all_gather, axis_name="rows", axis=0, tiled=True)
        proj = jnp.concatenate([w_emb.T, w_dense.T, b_in[:, None], jnp.zeros((ds, 82), BF)], axis=1)
        w1_all = gather(jnp.transpose(expert_w1, (1, 0, 2)).reshape(ds, QA))
        w2_all = gather(jnp.transpose(expert_w2, (1, 0, 2)).reshape(fs, HALF * EO))
        o_all = gather(jnp.concatenate([tower_w1[0], expert_b2.T], axis=1))
        b1_all, g_all, proj_all = gather(expert_b1.T), gather(gate_w[0]), gather(proj)
        small = jnp.concatenate([pad_to(o_all, FH, B1), pad_to(b1_all, FH, GA - B1), g_all[0:FH], g_all[FH:], jnp.zeros((FH, 32), BF)], axis=1)
        part = jnp.where(core == 0, proj_all[0:FH], proj_all[FH:])
        lower = jnp.concatenate([part, jnp.zeros((FH, UC - QA - 512), BF)], axis=1)
        own_u = [jnp.concatenate([w1_all, jnp.concatenate([jnp.concatenate([w2_all, small], axis=1), lower], axis=0)], axis=1)[None]]
        order = jnp.zeros((1,), jnp.int32)
        vec = jnp.concatenate([pad_to(a, 1, 128) for a in smalls] + [jnp.zeros((12, 128), BF)], axis=0)
        row_weights = weight_call(core[None].astype(jnp.int32), group_sizes, emb.shape[0], vec)
    far_u = [partner(a) for a in own_u]
    table = jnp.concatenate([core[None].astype(jnp.int32), order])

    hg, wat, du_own, du_far = main_call(table, emb.T, dense.T, labels, far_labels, row_weights, vec, partner(vec), own_u, far_u)
    du_far = partner(du_far)
    scale = 1.0 / user_count
    if fast:
        hg, part = sum_call("sum_cores", [du_own, du_far], [[(0, slice(8, 16)), (1, slice(8, 16))]], [(8, ds, UC)], through=hg)
        got = cross(part, (2, 1), size)
        eg, dg, token = input_call(table, hg, wat, part, None, "input_own")
        far_hg = partner(hg)
        groups = [[(j, slice(4 * b, 4 * b + 4)) for j in range(3)] for b in (1, 0)]
        part, rest = sum_call("sum_first", [du_own, du_far, got], groups, [(4, ds, UC)] * 2, token)
        got = cross(part, (1, 2), size)
        eg, dg, token = input_call(table, far_hg, wat, part, (eg, dg), "input_far")
        sums = sum_call("sum_second", [rest, got], [[(0, k), (1, k)] for k in range(4)], [(ds, UC)] * 4, token)
        parts = [sums[0]] + [hop(sums[a], 4 * a, size) for a in range(1, 4)]
        far_input = partner(last_call(parts))
        out = finish_call(scale, one_core, sums[0], far_input, parts, ds, fs, osz)
        g_emb, g_dense, g_bias, g_w1, g_b1, g_w2, g_b2, g_gate, g_gb, g_tower, g_t1, g_t2, g_t3 = out
        return (
            eg.T, dg.T, g_emb.T, g_dense, g_bias[0], g_w1, g_b1, g_w2, g_b2, g_gate.T[None], g_gb, g_tower[None], g_t1, g_t2, g_t3[0],
        )
    eg, dg, token = input_call(table, hg, wat, du_far, None, "input_own")
    eg, dg, _ = input_call(table, partner(hg), wat, token, (eg, dg), "input_far")
    scatter = functools.partial(lax.psum_scatter, axis_name="rows", scatter_dimension=0, tiled=True)
    wide = add_wide(du_own[0], du_far[0])
    upper, near = wide[0:FH, QA:UC], wide[FH:, QA : QA + XR]
    far, small = partner(near), upper[:, HALF * EO :]
    ta = scatter(jnp.concatenate([jnp.where(core == 0, near, far), jnp.where(core == 0, far, near)], axis=0)) * scale
    tp = jnp.transpose((scatter(wide[:, 0:QA]) * scale).reshape(ds, HALF, FH), (1, 0, 2))
    tw2, to, tb1 = scatter(upper[:, 0 : HALF * EO]) * scale, scatter(small[0:EO, 0:B1]) * scale, scatter(small[:, B1 : B1 + HALF]) * scale
    tg = scatter(jnp.concatenate([small[:, GA : GA + NE], small[:, GA + NE : GA + 2 * NE]], axis=0)) * scale
    ts = lax.psum(small[EO : EO + 3], "rows") * scale
    return (
        eg.T,
        dg.T,
        ta[:, 0:EMB].T,
        ta[:, EMB : EMB + DENSE].T,
        ta[:, EMB + DENSE],
        tp,
        tb1.T,
        jnp.transpose(tw2.reshape(fs, HALF, EO), (1, 0, 2)),
        to[:, TW : TW + HALF].T,
        tg[None],
        ts[2:3, 0:NE],
        to[:, 0:TW][None],
        ts[0:1, 0:TW],
        ts[1:2, 0:TW],
        ts[2, NE : NE + 1],
    )


def solution(mesh):
    in_specs = (
        P("rows", None),
        P("rows", None),
        P("rows", None),
        P("task", "rows"),
        P(None, "rows"),
        P(None, "rows"),
        P("rows"),
        P("task", "rows", None),
        P("task", "rows"),
        P("task", "rows", None),
        P("task", "rows"),
        P("task", "rows", None),
        P("task", None),
        P("task", "rows", None),
        P("task", None),
        P("task", None),
        P("task"),
    )
    out_specs = (
        P("rows", None),
        P("rows", None),
        P(None, "rows"),
        P(None, "rows"),
        P("rows"),
        P("task", "rows", None),
        P("task", "rows"),
        P("task", "rows", None),
        P("task", "rows"),
        P("task", "rows", None),
        P("task", None),
        P("task", "rows", None),
        P("task", None),
        P("task", None),
        P("task"),
    )
    return jax.shard_map(body, mesh=mesh, in_specs=in_specs, out_specs=out_specs, check_vma=False)
```

```python
import functools

import jax
import jax.numpy as jnp
from jax import lax
from jax.experimental import pallas as pl
from jax.experimental.pallas import tpu as pltpu
from jax.sharding import PartitionSpec as P

F32 = jnp.float32
BF = jnp.bfloat16
NT = (((1,), (1,)), ((), ()))
D, FH, EO, TW, NE = 512, 256, 128, 64, 8
HALF = NE // 2
EMB, DENSE = 416, 13
XR = 448
QA = HALF * FH
QS = QA + HALF * EO
UC = QS + 128
B1, GA = 72, 80
FG = NE * FH + 128
TILE = 1024
SUB = 512


def mm(a, b):
    return jnp.dot(a, b, preferred_element_type=F32)


def mm_nt(a, b):
    return lax.dot_general(a, b, NT, preferred_element_type=F32)


def act_narrow(half):
    return act_pair(half.astype(BF))


def act_pair(half):
    t = jnp.tanh(half)
    q = 1.0 + t
    m = half * q
    return m, q + m * (1.0 - t)


def swap_halves(a, flag):
    return jnp.where(flag, jnp.concatenate([a[HALF:NE], a[0:HALF]], axis=0), a)


def lane_fold(a):
    total = a[:, 0:128]
    for c in range(1, a.shape[1] // 128):
        total = total + a[:, 128 * c : 128 * c + 128]
    return total


def chunk_at(n, chunks, flag):
    if chunks == 1 or n // 4 in (0, 3):
        return n
    return n + 4 * flag if n // 4 == 1 else n - 4 * flag


LAG = 4


def take_turns(chains, lag):
    going = [(chain, lag * j) for j, chain in enumerate(chains)]
    while going:
        left = []
        for chain, wait in going:
            if wait > 0:
                left.append((chain, wait - 1))
            elif next(chain, True) is None:
                left.append((chain, 0))
        going = left


def main_kernel(pieces, chunks, tab_ref, *refs):
    emb_ref, dense_ref, lab_ref, far_lab_ref, row_ref, vec_ref, far_vec_ref = refs[:7]
    u_refs = (refs[7 : 7 + pieces], refs[7 + pieces : 7 + 2 * pieces])
    hg_ref, wat_s, du_own_ref, *du_far_refs = refs[7 + 2 * pieces : 12 + 2 * pieces]
    (
        x_s, hid_s, mid_s, sl1_s, out_s, sl2_s, sg_s, fg_s, mix_s,
        w1_s, w1t_s, ga_s, w2t_s, w2_s, b1_s, b2_s, gb_s, tt_s, tw_s, tcol_s, q_s,
        dwa_s, dw1_s, dw2_s, dtw_s, dcol_s, dlog_s, dsm_s, u_s, sem,
    ) = refs[12 + 2 * pieces :]
    n = SUB
    fs, osz, ds = FH // chunks, EO // chunks, D // chunks
    step = pl.program_id(0)
    core = tab_ref[0]
    second_core = core == 1

    @pl.when(step == 0)
    def _():
        copies = [[], []]
        for side in range(2):
            at = 0
            for j, ref in enumerate(u_refs[side]):
                copies[side].append(pltpu.make_async_copy(ref, u_s.at[side, pl.ds(at, ref.shape[0])], sem.at[pieces * side + j]))
                copies[side][-1].start()
                at += ref.shape[0]
        rows = lax.broadcasted_iota(jnp.int32, (32, n), 0)
        ones = jnp.where(lax.broadcasted_iota(jnp.int32, (16, n), 0) == 0, 1.0, 0.0).astype(BF)
        for h in range(TILE // SUB):
            x_s[h, EMB:XR, :] = jnp.where(rows == DENSE, 1.0, 0.0).astype(BF)
            hid_s[h, D : D + 16, :] = ones
            for k in range(NE):
                mid_s[h, k, FH : FH + 16, :] = ones
            mix_s[h, 2 * EO : 2 * EO + 16, :] = ones
            fg_s[h, NE * FH + 16 : FG, :] = jnp.zeros((FG - NE * FH - 16, n), BF)
        for ref in (dwa_s, dw1_s, dw2_s, dtw_s, dcol_s, dlog_s):
            ref[...] = jnp.zeros_like(ref)
        gates = []
        for side in range(2):
            for copy in copies[side]:
                copy.wait()
            base = HALF * FH * side
            holder = core if side == 0 else 1 - core
            for c in range(chunks):
                at = chunk_at(c, chunks, holder)
                to = pl.multiple_of(ds * at, ds)
                w1_s[pl.ds(to, ds), base : base + QA] = u_s[side, c, :, 0:QA]
                q_s[tab_ref[1 + at]] = u_s[side, c, 0:fs, QA:UC].astype(F32)
                small = u_s[side, c, 0:fs, QS:UC].astype(F32)
                ga_s[pl.ds(to, fs), :] = small
                ga_s[pl.ds(pl.multiple_of(to + fs, fs), fs), :] = pltpu.roll(small, 128 - NE, 1)
                wat_s[pl.ds(pl.multiple_of(to + holder * fs, fs), fs), :] = u_s[side, c, fs:ds, QA : QA + XR]
            for k in range(HALF):
                block = w1_s[:, base + FH * k : base + FH * k + FH]
                w1t_s[base + FH * k : base + FH * k + FH, :] = (block.astype(F32).T * 0.5).astype(BF)
            gates.append(swap_halves(ga_s[...].T[GA : GA + NE], second_core))
            cols = HALF * EO
            w2 = q_s[:, :, 0:cols].reshape(FH, cols) * 0.5
            w2_s[:, cols * side : cols * side + cols] = w2.astype(BF)
            w2t_s[cols * side : cols * side + cols, :] = w2.T.astype(BF)
            b1_s[side] = q_s[:, :, cols : cols + 128].reshape(FH, 128) * 0.5
            last = q_s[:, 0:osz, cols : cols + 128].reshape(EO, 128)
            b2_s[side] = last * 0.5
            tower = last[:, 0:TW]
            rest = jnp.zeros_like(tower)
            both = jnp.concatenate([tower, rest] if side == 0 else [rest, tower], axis=1)
            tw_s[EO * side : EO * side + EO, :] = both.astype(BF)
            tt_s[:, EO * side : EO * side + EO] = (both.T * 0.5).astype(BF)
        gates = jnp.concatenate(gates, axis=0)
        w1t_s[NE * FH : NE * FH + 16, :] = gates.astype(BF)
        pad = jnp.concatenate([gates, jnp.zeros((112, D), F32)], axis=0)
        w1_s[:, NE * FH : FG] = pad.T.astype(BF)
        vecs = [jnp.concatenate([r[...].astype(F32), jnp.zeros((112, 128), F32)], axis=0).T for r in (vec_ref, far_vec_ref)]
        gb_s[...] = jnp.concatenate([swap_halves(v[0:NE, 0:1], second_core) for v in vecs], axis=0)
        b1 = jnp.concatenate([v[0:TW, 1:2] for v in vecs], axis=0)
        head = jnp.concatenate([v[0:TW, 2:3] for v in vecs], axis=0)
        last = jnp.concatenate([v[0:1, 3:4] for v in vecs] * TW, axis=0)
        tcol_s[...] = jnp.concatenate([b1 * 0.5, head, head * 0.5, last], axis=1)

    def chain(h):
        at = slice(SUB * h, SUB * h + SUB)
        x_s[h, 0:EMB, :] = emb_ref[:, at]
        x_s[h, EMB : EMB + DENSE, :] = dense_ref[:, at]
        hid = mm(wat_s[...], x_s[h]).astype(BF)
        hid_s[h, 0:D, :] = hid
        yield
        logits = mm(w1t_s[NE * FH : NE * FH + 16, :], hid) + gb_s[...]
        probs = []
        for t in range(2):
            lt = logits[NE * t : NE * t + NE]
            e = jnp.exp(lt - jnp.max(lt, axis=0, keepdims=True))
            probs.append(e / jnp.sum(e, axis=0, keepdims=True))
        mix = [None, None]
        pend = None
        nxt = mm(w1t_s[0:FH, :], hid)
        yield
        for k in range(NE + 1):
            pre = nxt
            if k < NE - 1:
                nxt = mm(w1t_s[FH * (k + 1) : FH * (k + 2), :], hid)
            if k < NE:
                m, s = act_narrow(pre + b1_s[k // HALF, :, B1 + k % HALF : B1 + k % HALF + 1])
                mid_s[h, k, 0:FH, :] = m
                sl1_s[h, FH * k : FH * k + FH, :] = s
                pre2 = mm(w2t_s[EO * k : EO * k + EO, :], m)
            if pend is not None:
                j = k - 1
                o, s = act_narrow(pend + b2_s[j // HALF, :, TW + j % HALF : TW + j % HALF + 1])
                out_s[h, EO * j : EO * j + EO, :] = o
                sl2_s[h, EO * j : EO * j + EO, :] = s
                o = o.astype(F32)
                for t in range(2):
                    term = probs[t][j : j + 1, :] * o
                    mix[t] = term if j == 0 else mix[t] + term
            pend = pre2
            yield
        mix_s[h, 0:EO, :] = mix[0].astype(BF)
        mix_s[h, EO : 2 * EO, :] = mix[1].astype(BF)
        act, slope = act_pair(mm(tt_s[...], mix_s[h, 0 : 2 * EO, :]) + tcol_s[:, 0:1])
        weighted = act * tcol_s[:, 1:2]
        lgos = []
        for t in range(2):
            logit = jnp.sum(weighted[TW * t : TW * t + TW], axis=0, keepdims=True) + tcol_s[t : t + 1, 3:4]
            label = (lab_ref, far_lab_ref)[t][:, at].astype(F32)
            lgos.append(row_ref[:, at] * (0.5 * jnp.tanh(0.5 * logit) + 0.5 - label))
        lgo = jnp.concatenate([jnp.broadcast_to(lgos[t], (TW, SUB)) for t in range(2)], axis=0)
        dcol_s[...] += lane_fold(lgo * act)
        dlog_s[...] += lane_fold(jnp.concatenate([jnp.broadcast_to(lgos[t], (8, SUB)) for t in range(2)], axis=0))
        tg = (lgo * (tcol_s[:, 2:3] * slope)).astype(BF)
        yield
        dtw_s[...] += mm_nt(mix_s[h], tg)
        mgh = mm(tw_s[...], tg) * 0.5
        yield
        pgs = [[], []]
        mgs = [None] * NE
        for k in range(NE + 2):
            if k < NE:
                o = out_s[h, EO * k : EO * k + EO, :]
                og = None
                for t in range(2):
                    mg = mgh[EO * t : EO * t + EO]
                    pgs[t].append(jnp.sum((o * mg.astype(BF)).astype(F32), axis=0, keepdims=True))
                    term = probs[t][k : k + 1, :] * mg
                    og = term if og is None else og + term
                sg = og.astype(BF) * sl2_s[h, EO * k : EO * k + EO, :]
                sg_s[h, EO * (k % 2) : EO * (k % 2) + EO, :] = sg
                mgs[k] = mm(w2_s[:, EO * k : EO * k + EO], sg)
            if 1 <= k < NE + 1:
                j = k - 1
                dw2_s[:, EO * j : EO * j + EO] += mm_nt(mid_s[h, j], sg_s[h, EO * (j % 2) : EO * (j % 2) + EO, :])
                fg = mgs[j].astype(BF) * sl1_s[h, FH * j : FH * j + FH, :]
                fg_s[h, FH * j : FH * j + FH, :] = fg
            if k >= 2:
                j = k - 2
                dw1_s[:, FH * j : FH * j + FH] += mm_nt(hid_s[h], fg_s[h, FH * j : FH * j + FH, :])
            yield
        lgs = []
        for t in range(2):
            pg = jnp.concatenate(pgs[t], axis=0)
            lgs.append(2.0 * probs[t] * (pg - jnp.sum(probs[t] * pg, axis=0, keepdims=True)))
        fg_s[h, NE * FH : NE * FH + 16, :] = jnp.concatenate(lgs, axis=0).astype(BF)
        yield
        dw1_s[:, NE * FH : FG] += mm_nt(hid_s[h], fg_s[h, NE * FH : FG, :])
        hg = mm(w1_s[...], fg_s[h]).astype(BF)
        hg_ref[:, at] = hg
        yield
        dwa_s[...] += mm_nt(hg, x_s[h])
        yield

    take_turns([chain(h) for h in range(TILE // SUB)], LAG)

    @pl.when(step == pl.num_programs(0) - 1)
    def _():
        gate = dw1_s[:, NE * FH : FG].T
        dlog = jnp.sum(dlog_s[...], axis=1, keepdims=True)
        dcol = jnp.sum(dcol_s[...].T, axis=0, keepdims=True)
        for side in range(2):
            own_gate = swap_halves(gate[NE * side : NE * side + NE], second_core)
            ga_s[...] = jnp.concatenate([own_gate[:, 0:D], jnp.zeros((120, D), F32)], axis=0).T
            b1 = [dw1_s[D : D + 1, FH * k : FH * k + FH] for k in range(HALF * side, HALF * side + HALF)]
            b1 = jnp.concatenate(b1 + [jnp.zeros((124, FH), F32)], axis=0).T
            b2 = [dw2_s[FH : FH + 1, EO * k : EO * k + EO] for k in range(HALF * side, HALF * side + HALF)]
            b2 = jnp.concatenate(b2 + [jnp.zeros((60, EO), F32)], axis=0).T
            tower = dtw_s[EO * side : EO * side + EO, TW * side : TW * side + TW]
            tower = jnp.concatenate([tower, b2], axis=1)
            lanes = slice(TW * side, TW * side + TW)
            blank = jnp.zeros((1, TW), F32)
            lines = [jnp.concatenate([a, blank], axis=1) for a in (dtw_s[2 * EO : 2 * EO + 1, lanes], dcol[:, lanes])]
            gate_b = jnp.sum(jnp.where(lax.broadcasted_iota(jnp.int32, (NE, D + 16), 1) == D, own_gate, 0.0), axis=1, keepdims=True)
            small = jnp.concatenate([gate_b, dlog[8 * side : 8 * side + 8]], axis=0)
            small = jnp.concatenate([jnp.broadcast_to(small, (16, 128)), jnp.zeros((112, 128), F32)], axis=0).T[0:1]
            tail = jnp.concatenate(lines + [small, jnp.zeros((fs - osz - 3, 128), F32)], axis=0)
            b1 = pltpu.roll(b1, B1, 1)
            for c in range(chunks):
                dsm_s[fs * c : fs * c + fs, :] = b1[fs * c : fs * c + fs] + jnp.concatenate([tower[osz * c : osz * c + osz], tail], axis=0)
            holder = core if side == 0 else 1 - core
            cols = HALF * EO
            for n in range(chunks):
                ref, c = du_own_ref, n
                if side == 1:
                    ref, c = du_far_refs[n * 2 // chunks], n % max(chunks // 2, 1)
                at = chunk_at(n, chunks, holder)
                to = pl.multiple_of(ds * at, ds)
                where = pl.ds(pl.multiple_of(tab_ref[1 + at] * fs, fs), fs)
                ref[c, :, 0:QA] = dw1_s[pl.ds(to, ds), QA * side : QA * side + QA].astype(BF)
                ref[c, 0:fs, QA:QS] = dw2_s[where, cols * side : cols * side + cols].astype(BF)
                low = pltpu.roll(ga_s[pl.ds(to, fs), :], GA, 1)
                high = pltpu.roll(ga_s[pl.ds(pl.multiple_of(to + fs, fs), fs), :], GA + NE, 1)
                ref[c, 0:fs, QS:UC] = (dsm_s[where, :] + low + high).astype(BF)
                lower = dwa_s[pl.ds(pl.multiple_of(to + holder * fs, fs), fs), :]
                ref[c, fs:ds, QA:UC] = jnp.concatenate([lower, jnp.zeros((fs, UC - QA - XR), F32)], axis=1).astype(BF)


def weight_kernel(batch_rows, tab_ref, sizes_ref, token_ref, out_ref, start_s):
    batches, users = sizes_ref.shape
    counts = jnp.concatenate([sizes_ref[...].astype(F32), jnp.zeros((16 - batches, users), F32)], axis=0)
    turned = jnp.concatenate([counts, jnp.zeros((112, users), F32)], axis=0).T
    before = lax.broadcasted_iota(jnp.int32, (users, users), 1) < lax.broadcasted_iota(jnp.int32, (users, users), 0)
    starts = mm(jnp.where(before, 1.0, 0.0).astype(BF), turned.astype(BF))
    for b in range(batches):
        start_s[b] = jnp.broadcast_to(starts[:, b : b + 1], (users, 128))
    first = lax.broadcasted_iota(jnp.int32, counts.shape, 1) == 0
    rises = counts - jnp.where(first, 0.0, pltpu.roll(counts, 1, 1))
    line = lax.broadcasted_iota(jnp.int32, counts.shape, 0)
    steps = out_ref.shape[1] // SUB
    for step in range(steps):
        at_step = tab_ref[0] * steps + step
        batch = at_step // (batch_rows // SUB)
        first_row = (at_step % (batch_rows // SUB) * SUB).astype(F32)
        begins = start_s[batch]
        places = first_row + lax.broadcasted_iota(jnp.int32, (1, 128), 1).astype(F32)
        begun = [jnp.where(begins <= places + 128.0 * c, 1.0, 0.0).astype(BF) for c in range(SUB // 128)]
        rise = jnp.where(line == batch, rises, 0.0).astype(BF)
        size = jnp.sum(mm(rise, jnp.concatenate(begun, axis=1)), axis=0, keepdims=True)
        out_ref[:, SUB * step : SUB * step + SUB] = 1.0 / size


def weight_call(table, sizes, rows, token):
    batches, users = sizes.shape
    return pl.pallas_call(
        functools.partial(weight_kernel, rows // batches),
        in_specs=[whole(pltpu.SMEM), whole(), whole(pl.ANY)],
        out_specs=whole(),
        out_shape=jax.ShapeDtypeStruct((1, rows // 2), F32),
        scratch_shapes=[pltpu.VMEM((batches, users, 128), F32)],
        cost_estimate=pl.CostEstimate(flops=3_000_000_000, bytes_accessed=1_000_000, transcendentals=0),
        name="row_weights",
    )(table, sizes, token)


def const2(i, c):
    return (0, 0)


def main_call(table, embt, denset, labels, far_labels, row_weights, vec, far_vec, own_u, far_u):
    rows = embt.shape[1]
    half = rows // 2
    steps = half // TILE
    pieces = len(own_u)
    chunks = sum(a.shape[0] for a in own_u)
    fs, ds = FH // chunks, D // chunks

    def own(i, c):
        return (0, c[0] * steps + i)

    grads = [(chunks, ds, UC)] + [(max(chunks // 2, 1), ds, UC)] * 2
    parts = TILE // SUB
    spec = pltpu.PrefetchScalarGridSpec(
        num_scalar_prefetch=1,
        grid=(steps,),
        in_specs=[
            pl.BlockSpec((EMB, TILE), own),
            pl.BlockSpec((DENSE, TILE), own),
            pl.BlockSpec((1, TILE), own),
            pl.BlockSpec((1, TILE), own),
            pl.BlockSpec((1, TILE), lambda i, c: (0, i)),
            whole(),
            whole(),
        ]
        + [whole(pltpu.HBM) for _ in (*own_u, *far_u)],
        out_specs=[pl.BlockSpec((D, TILE), lambda i, c: (0, i))] + [whole()] * 4,
        scratch_shapes=[
            pltpu.VMEM((parts, XR, SUB), BF),
            pltpu.VMEM((parts, D + 16, SUB), BF),
            pltpu.VMEM((parts, NE, FH + 16, SUB), BF),
            pltpu.VMEM((parts, NE * FH, SUB), BF),
            pltpu.VMEM((parts, NE * EO, SUB), BF),
            pltpu.VMEM((parts, NE * EO, SUB), BF),
            pltpu.VMEM((parts, 2 * EO, SUB), BF),
            pltpu.VMEM((parts, FG, SUB), BF),
            pltpu.VMEM((parts, 2 * EO + 16, SUB), BF),
            pltpu.VMEM((D, FG), BF),
            pltpu.VMEM((NE * FH + 16, D), BF),
            pltpu.VMEM((D, 128), F32),
            pltpu.VMEM((NE * EO, FH), BF),
            pltpu.VMEM((FH, NE * EO), BF),
            pltpu.VMEM((2, FH, 128), F32),
            pltpu.VMEM((2, EO, 128), F32),
            pltpu.VMEM((16, 1), F32),
            pltpu.VMEM((2 * TW, 2 * EO), BF),
            pltpu.VMEM((2 * EO, 2 * TW), BF),
            pltpu.VMEM((2 * TW, 4), F32),
            pltpu.VMEM((chunks, fs, UC - QA), F32),
            pltpu.VMEM((D, XR), F32),
            pltpu.VMEM((D + 16, FG), F32),
            pltpu.VMEM((FH + 16, NE * EO), F32),
            pltpu.VMEM((2 * EO + 16, 2 * TW), F32),
            pltpu.VMEM((2 * TW, 128), F32),
            pltpu.VMEM((16, 128), F32),
            pltpu.VMEM((FH, 128), F32),
            pltpu.VMEM((2, chunks, ds, UC), BF),
            pltpu.SemaphoreType.DMA((2 * pieces,)),
        ],
    )
    return pl.pallas_call(
        functools.partial(main_kernel, pieces, chunks),
        grid_spec=spec,
        out_shape=[jax.ShapeDtypeStruct((D, half), BF), jax.ShapeDtypeStruct((D, XR), BF)]
        + [jax.ShapeDtypeStruct(a, BF) for a in grads],
        compiler_params=pltpu.CompilerParams(vmem_limit_bytes=48 * 1024 * 1024),
        cost_estimate=pl.CostEstimate(flops=50_000_000_000, bytes_accessed=24_000_000, transcendentals=0),
        name="experts",
    )(table, embt, denset, labels, far_labels, row_weights, vec, far_vec, *own_u, *far_u)


def input_kernel(tab_ref, hg_ref, wat_ref, *refs):
    eg_ref, dg_ref, done_ref, wa_s = refs[-4:]

    @pl.when(pl.program_id(0) == 0)
    def _():
        wa_s[...] = wat_ref[...].astype(F32).T.astype(BF)
        done_ref[...] = jnp.zeros_like(done_ref)

    eg = mm(wa_s[...], hg_ref[...])
    eg_ref[...] = eg[0:EMB]
    dg_ref[...] = eg[EMB : EMB + DENSE]


def input_call(table, hg, wat, token, other, name):
    half = hg.shape[1]
    tile = TILE
    steps = half // tile

    def place(i, c):
        return (0, (c[0] if other is None else 1 - c[0]) * steps + i)

    extra = [token] + (list(other) if other is not None else [])
    spec = pltpu.PrefetchScalarGridSpec(
        num_scalar_prefetch=1,
        grid=(steps,),
        in_specs=[pl.BlockSpec((D, tile), lambda i, c: (0, i)), pl.BlockSpec((D, XR), const2, pipeline_mode=pl.Buffered(1))]
        + [whole(pl.ANY) for _ in extra],
        out_specs=[pl.BlockSpec((EMB, tile), place), pl.BlockSpec((DENSE, tile), place), pl.BlockSpec((8, 128), const2)],
        scratch_shapes=[pltpu.VMEM((XR, D), BF)],
    )
    return pl.pallas_call(
        input_kernel,
        grid_spec=spec,
        out_shape=[jax.ShapeDtypeStruct((EMB, 2 * half), F32), jax.ShapeDtypeStruct((DENSE, 2 * half), F32), jax.ShapeDtypeStruct((8, 128), F32)],
        input_output_aliases={} if other is None else {4: 0, 5: 1},
        compiler_params=pltpu.CompilerParams(vmem_limit_bytes=32 * 1024 * 1024),
        cost_estimate=pl.CostEstimate(flops=4_000_000_000, bytes_accessed=9_000_000, transcendentals=0),
        name=name,
    )(table, hg, wat, *extra)


def widen(a):
    return jnp.concatenate([a.astype(F32), jnp.zeros((a.shape[0], 128 - a.shape[1]), F32)], axis=1)


def square(rows):
    count = sum(a.shape[0] for a in rows)
    return jnp.concatenate(rows + [jnp.zeros((128 - count, 128), F32)], axis=0)


def pack_vec(gb_ref, t1_ref, t2_ref, t3_ref):
    return jnp.concatenate([widen(r[...]) for r in (gb_ref, t1_ref, t2_ref, t3_ref)] + [jnp.zeros((12, 128), F32)], axis=0).astype(BF)


def pack_kernel(core_ref, emb_ref, dense_ref, bias_ref, w1_ref, w2_ref, b1_ref, b2_ref, gate_ref, tower_ref, *refs):
    u_ref, vec_ref = refs[4:]
    vec_ref[...] = pack_vec(*refs[:4])
    fs = u_ref.shape[0] // 2
    turned = square([widen(r[...]) for r in (b1_ref, b2_ref, gate_ref, dense_ref, bias_ref)]).T
    lane = lax.broadcasted_iota(jnp.int32, (fs, 128), 1)
    low, high = turned[0:fs], turned[fs : 2 * fs]
    small = jnp.concatenate([widen(tower_ref[...]), jnp.zeros((fs - tower_ref.shape[0], 128), F32)], axis=0)
    small += jnp.where((lane >= TW) & (lane < TW + HALF), pltpu.roll(low, TW - HALF, 1), 0.0)
    small += jnp.where(((lane >= B1) & (lane < B1 + HALF)) | ((lane >= GA) & (lane < GA + NE)), pltpu.roll(low, B1, 1), 0.0)
    small += jnp.where((lane >= GA + NE) & (lane < GA + 2 * NE), pltpu.roll(high, GA, 1), 0.0)
    for k in range(HALF):
        u_ref[:, FH * k : FH * k + FH] = w1_ref[k]
        u_ref[0:fs, QA + EO * k : QA + EO * k + EO] = w2_ref[k]
    u_ref[0:fs, QS:UC] = small.astype(BF)
    second_core = core_ref[0] == 1
    lanes = lax.broadcasted_iota(jnp.int32, (2 * fs, 128), 1)
    last = widen(emb_ref[:, 384:EMB]) + jnp.where((lanes >= 32) & (lanes < 33 + DENSE), pltpu.roll(turned[0 : 2 * fs], 16, 1), 0.0)
    for c in range(3):
        block = emb_ref[:, 128 * c : 128 * c + 128]
        u_ref[fs:, QA + 128 * c : QA + 128 * c + 128] = jnp.where(second_core, block[fs:], block[0:fs])
    u_ref[fs:, QA + 384 : QA + 512] = jnp.where(second_core, last[fs:], last[0:fs]).astype(BF)
    u_ref[fs:, QA + 512 : UC] = jnp.zeros((fs, UC - QA - 512), BF)


def whole(memory=pltpu.VMEM):
    return pl.BlockSpec(memory_space=memory)


def pack_call(core, *parts):
    ds = parts[3].shape[1]
    return pl.pallas_call(
        pack_kernel,
        in_specs=[whole(pltpu.SMEM)] + [whole() for _ in parts],
        out_specs=[whole(), whole()],
        out_shape=[jax.ShapeDtypeStruct((ds, UC), BF), jax.ShapeDtypeStruct((16, 128), BF)],
        name="pack",
    )(core, *parts)


def sum_kernel(groups, count, *refs):
    ins, outs = refs[:count], refs[-len(groups) :]
    for group, out in zip(groups, outs):
        total = None
        for number, at in group:
            term = ins[number][at].astype(F32)
            total = term if total is None else total + term
        out[...] = total.astype(out.dtype)


def sum_call(name, arrays, groups, shapes, token=None, through=None):
    extra = [a for a in (token, through) if a is not None]
    lead = [] if through is None else [through]
    return pl.pallas_call(
        functools.partial(sum_kernel, groups, len(arrays)),
        in_specs=[whole() for _ in arrays] + [whole(pl.ANY) for _ in extra],
        out_specs=[whole(pl.ANY) for _ in lead] + [whole() for _ in shapes],
        out_shape=[jax.ShapeDtypeStruct(a.shape, a.dtype) for a in lead] + [jax.ShapeDtypeStruct(a, BF) for a in shapes],
        input_output_aliases={len(arrays) + len(extra) - 1: 0} if lead else {},
        compiler_params=pltpu.CompilerParams(vmem_limit_bytes=32 * 1024 * 1024),
        name=name,
    )(*arrays, *extra)


def finish_kernel(scale, core_ref, token_ref, *refs):
    total = sum(r[...].astype(F32) for r in refs[:4]) * scale
    ds = total.shape[0]
    fs = ds // 2
    own_part = total[fs:, QA : QA + XR]
    far_part = sum(r[...].astype(F32) for r in refs[4:8])[:, 0:XR] * scale
    second_core = core_ref[0] == 1
    ta = jnp.concatenate([jnp.where(second_core, far_part, own_part), jnp.where(second_core, own_part, far_part)], axis=0)
    emb_ref, dense_ref, bias_ref, w1_ref, b1_ref, w2_ref, b2_ref, gate_ref, gb_ref, tower_ref, t1_ref, t2_ref, t3_ref = refs[8:]
    osz = tower_ref.shape[0]
    for k in range(HALF):
        w1_ref[k] = total[:, FH * k : FH * k + FH]
        w2_ref[k] = total[0:fs, QA + EO * k : QA + EO * k + EO]
    small = total[0:fs, QS:UC]
    turned = square([small]).T
    b1_ref[...] = turned[B1 : B1 + HALF, 0:fs]
    b2_ref[...] = turned[TW : TW + HALF, 0:osz]
    gates = turned[GA : GA + NE] + pltpu.roll(turned[GA + NE : GA + 2 * NE], fs, 1)
    gate_ref[...] = gates[:, 0 : 2 * fs]
    tower_ref[...] = small[0:osz, 0:TW]
    t1_ref[...] = small[osz : osz + 1, 0:TW]
    t2_ref[...] = small[osz + 1 : osz + 2, 0:TW]
    gb_ref[...] = small[osz + 2 : osz + 3, 0:NE]
    t3_ref[...] = small[osz + 2 : osz + 3, NE : NE + 1]
    emb_ref[...] = ta[:, 0:EMB]
    last = square([widen(ta[:, 384:XR])]).T
    dense_ref[...] = last[32 : 32 + DENSE, 0 : 2 * fs]
    bias_ref[...] = last[32 + DENSE : 33 + DENSE, 0 : 2 * fs]


def finish_call(scale, core, token, arrays, ds, fs, osz):
    shapes = [
        (ds, EMB), (DENSE, ds), (1, ds), (HALF, ds, FH), (HALF, fs), (HALF, fs, EO), (HALF, osz), (NE, ds), (1, NE),
        (osz, TW), (1, TW), (1, TW), (1, 1),
    ]
    return pl.pallas_call(
        functools.partial(finish_kernel, scale),
        in_specs=[whole(pltpu.SMEM), whole(pl.ANY)] + [whole() for _ in arrays],
        out_specs=[whole() for _ in shapes],
        out_shape=[jax.ShapeDtypeStruct(a, F32) for a in shapes],
        name="finish",
    )(core, token, *arrays)


def hop(a, mask, size):
    return lax.ppermute(a, "rows", [(i, i ^ mask) for i in range(size)])


def cross(a, masks, size):
    pairs = [(2 * i + t, 2 * (i ^ masks[t]) + t) for i in range(size) for t in range(2)]
    return lax.ppermute(a, ("rows", "task"), pairs)


def partner(a):
    return lax.ppermute(a, "task", [(0, 1), (1, 0)])


def add_wide(a, b):
    return a.astype(F32) + b.astype(F32)


def pad_to(a, rows, cols):
    return jnp.pad(a, ((0, rows - a.shape[0]), (0, cols - a.shape[1])))


def body(
    emb, dense, group_sizes, labels, w_emb, w_dense, b_in, expert_w1, expert_b1, expert_w2, expert_b2,
    gate_w, gate_b, tower_w1, tower_b1, tower_w2, tower_b2,
):
    size = lax.axis_size("rows")
    core = lax.axis_index("task")
    place = lax.axis_index("rows")
    user_count = group_sizes.shape[1] * group_sizes.shape[0] * size
    ds, fs, osz = D // size, FH // size, EO // size
    fast = size == 16
    far_labels = partner(labels)
    smalls = (gate_b, tower_b1, tower_w2, tower_b2[None])

    if fast:
        one_core = core[None].astype(jnp.int32)
        gate_t = jnp.transpose(gate_w, (0, 2, 1))[0]
        shard, vec = pack_call(
            one_core, w_emb.T, w_dense, b_in[None], expert_w1, expert_w2, expert_b1, expert_b2, gate_t, tower_w1[0], *smalls
        )
        row_weights = weight_call(one_core, group_sizes, emb.shape[0], vec)
        near = jnp.stack([shard] + [hop(shard, 4 * a, size) for a in range(1, 4)])
        once = cross(near, (1, 2), size)
        own_u = [near, once, cross(near, (2, 1), size), cross(once, (2, 1), size)]
        steps = jnp.arange(16, dtype=jnp.int32)
        order = place ^ (steps % 4 * 4 + steps // 4)
    else:
        gather = functools.partial(lax.all_gather, axis_name="rows", axis=0, tiled=True)
        proj = jnp.concatenate([w_emb.T, w_dense.T, b_in[:, None], jnp.zeros((ds, 82), BF)], axis=1)
        w1_all = gather(jnp.transpose(expert_w1, (1, 0, 2)).reshape(ds, QA))
        w2_all = gather(jnp.transpose(expert_w2, (1, 0, 2)).reshape(fs, HALF * EO))
        o_all = gather(jnp.concatenate([tower_w1[0], expert_b2.T], axis=1))
        b1_all, g_all, proj_all = gather(expert_b1.T), gather(gate_w[0]), gather(proj)
        small = jnp.concatenate([pad_to(o_all, FH, B1), pad_to(b1_all, FH, GA - B1), g_all[0:FH], g_all[FH:], jnp.zeros((FH, 32), BF)], axis=1)
        part = jnp.where(core == 0, proj_all[0:FH], proj_all[FH:])
        lower = jnp.concatenate([part, jnp.zeros((FH, UC - QA - 512), BF)], axis=1)
        own_u = [jnp.concatenate([w1_all, jnp.concatenate([jnp.concatenate([w2_all, small], axis=1), lower], axis=0)], axis=1)[None]]
        order = jnp.zeros((1,), jnp.int32)
        vec = jnp.concatenate([pad_to(a, 1, 128) for a in smalls] + [jnp.zeros((12, 128), BF)], axis=0)
        row_weights = weight_call(core[None].astype(jnp.int32), group_sizes, emb.shape[0], vec)
    far_u = [partner(a) for a in own_u]
    table = jnp.concatenate([core[None].astype(jnp.int32), order])

    hg, wat, du_own, du_low, du_high = main_call(table, emb.T, dense.T, labels, far_labels, row_weights, vec, partner(vec), own_u, far_u)
    du_high = partner(du_high)
    scale = 1.0 / user_count
    if fast:
        hg, part = sum_call("sum_cores", [du_own, du_high], [[(0, slice(8, 16)), (1, slice(0, 8))]], [(8, ds, UC)], through=hg)
        got = cross(part, (2, 1), size)
        du_low, far_hg = partner(du_low), partner(hg)
        eg, dg, token = input_call(table, hg, wat, part, None, "input_own")
        groups = [[(j, slice(4 * b, 4 * b + 4)) for j in range(3)] for b in (1, 0)]
        part, rest = sum_call("sum_first", [du_own, du_low, got], groups, [(4, ds, UC)] * 2, token)
        got = cross(part, (1, 2), size)
        eg, dg, token = input_call(table, far_hg, wat, part, (eg, dg), "input_far")
        sums = sum_call("sum_second", [rest, got], [[(0, k), (1, k)] for k in range(4)], [(ds, UC)] * 4, token)
        parts = [sums[0]] + [hop(sums[a], 4 * a, size) for a in range(1, 4)]
        parts += [partner(a[fs:, QA : QA + 512]) for a in parts]
        out = finish_call(scale, one_core, sums[0], parts, ds, fs, osz)
        g_emb, g_dense, g_bias, g_w1, g_b1, g_w2, g_b2, g_gate, g_gb, g_tower, g_t1, g_t2, g_t3 = out
        return (
            eg.T, dg.T, g_emb.T, g_dense, g_bias[0], g_w1, g_b1, g_w2, g_b2, g_gate.T[None], g_gb, g_tower[None], g_t1, g_t2, g_t3[0],
        )
    eg, dg, token = input_call(table, hg, wat, du_high, None, "input_own")
    eg, dg, _ = input_call(table, partner(hg), wat, token, (eg, dg), "input_far")
    scatter = functools.partial(lax.psum_scatter, axis_name="rows", scatter_dimension=0, tiled=True)
    wide = add_wide(du_own[0], partner(du_low)[0])
    upper, near = wide[0:FH, QA:UC], wide[FH:, QA : QA + XR]
    far, small = partner(near), upper[:, HALF * EO :]
    ta = scatter(jnp.concatenate([jnp.where(core == 0, near, far), jnp.where(core == 0, far, near)], axis=0)) * scale
    tp = jnp.transpose((scatter(wide[:, 0:QA]) * scale).reshape(ds, HALF, FH), (1, 0, 2))
    tw2, to, tb1 = scatter(upper[:, 0 : HALF * EO]) * scale, scatter(small[0:EO, 0:B1]) * scale, scatter(small[:, B1 : B1 + HALF]) * scale
    tg = scatter(jnp.concatenate([small[:, GA : GA + NE], small[:, GA + NE : GA + 2 * NE]], axis=0)) * scale
    ts = lax.psum(small[EO : EO + 3], "rows") * scale
    return (
        eg.T,
        dg.T,
        ta[:, 0:EMB].T,
        ta[:, EMB : EMB + DENSE].T,
        ta[:, EMB + DENSE],
        tp,
        tb1.T,
        jnp.transpose(tw2.reshape(fs, HALF, EO), (1, 0, 2)),
        to[:, TW : TW + HALF].T,
        tg[None],
        ts[2:3, 0:NE],
        to[:, 0:TW][None],
        ts[0:1, 0:TW],
        ts[1:2, 0:TW],
        ts[2, NE : NE + 1],
    )


def solution(mesh):
    in_specs = (
        P("rows", None),
        P("rows", None),
        P("rows", None),
        P("task", "rows"),
        P(None, "rows"),
        P(None, "rows"),
        P("rows"),
        P("task", "rows", None),
        P("task", "rows"),
        P("task", "rows", None),
        P("task", "rows"),
        P("task", "rows", None),
        P("task", None),
        P("task", "rows", None),
        P("task", None),
        P("task", None),
        P("task"),
    )
    out_specs = (
        P("rows", None),
        P("rows", None),
        P(None, "rows"),
        P(None, "rows"),
        P("rows"),
        P("task", "rows", None),
        P("task", "rows"),
        P("task", "rows", None),
        P("task", "rows"),
        P("task", "rows", None),
        P("task", None),
        P("task", "rows", None),
        P("task", None),
        P("task", None),
        P("task"),
    )
    return jax.shard_map(body, mesh=mesh, in_specs=in_specs, out_specs=out_specs, check_vma=False)
```

```python
import functools

import jax
import jax.numpy as jnp
from jax import lax
from jax.experimental import pallas as pl
from jax.experimental.pallas import tpu as pltpu
from jax.sharding import PartitionSpec as P

F32 = jnp.float32
BF = jnp.bfloat16
NT = (((1,), (1,)), ((), ()))
D, FH, EO, TW, NE = 512, 256, 128, 64, 8
HALF = NE // 2
EMB, DENSE = 416, 13
XR = 448
QA = HALF * FH
QS = QA + HALF * EO
UC = QS + 128
B1, GA = 72, 80
FG = NE * FH + 128
TILE = 1024
SUB = 512


def mm(a, b):
    return jnp.dot(a, b, preferred_element_type=F32)


def mm_nt(a, b):
    return lax.dot_general(a, b, NT, preferred_element_type=F32)


def act_narrow(half):
    return act_pair(half.astype(BF))


def act_pair(half):
    t = jnp.tanh(half)
    q = 1.0 + t
    m = half * q
    return m, q + m * (1.0 - t)


def swap_halves(a, flag):
    return jnp.where(flag, jnp.concatenate([a[HALF:NE], a[0:HALF]], axis=0), a)


def lane_fold(a):
    total = a[:, 0:128]
    for c in range(1, a.shape[1] // 128):
        total = total + a[:, 128 * c : 128 * c + 128]
    return total


def chunk_at(n, chunks, flag):
    if chunks == 1 or n // 4 in (0, 3):
        return n
    return n + 4 * flag if n // 4 == 1 else n - 4 * flag


LAG = 4


def take_turns(chains, lag):
    going = [(chain, lag * j) for j, chain in enumerate(chains)]
    while going:
        left = []
        for chain, wait in going:
            if wait > 0:
                left.append((chain, wait - 1))
            elif next(chain, True) is None:
                left.append((chain, 0))
        going = left


def main_kernel(pieces, chunks, rows, batch_rows, tab_ref, *refs):
    emb_ref, dense_ref, line_ref, far_line_ref = refs[:4]
    u_refs = (refs[4 : 4 + pieces], refs[4 + pieces : 4 + 2 * pieces])
    hg_ref, wat_s, *du_refs = refs[4 + 2 * pieces : 10 + 2 * pieces]
    (
        x_s, hid_s, mid_s, sl1_s, out_s, sl2_s, sg_s, fg_s, mix_s,
        w1_s, w1t_s, ga_s, w2t_s, w2_s, b1_s, b2_s, gb_s, tt_s, tw_s, tcol_s, q_s,
        dwa_s, dw1_s, dw2_s, dtw_s, dcol_s, dlog_s, dsm_s, dense_s, start_s, row_s, sem,
    ) = refs[10 + 2 * pieces :]
    n = SUB
    fs, osz, ds = FH // chunks, EO // chunks, D // chunks
    step = pl.program_id(0)
    core = tab_ref[0]
    second_core = core == 1

    @pl.when(step == 0)
    def _():
        half = dense_s.shape[1]
        mine = dense_ref.at[:, pl.ds(pl.multiple_of(core * half, half), half)]
        dense_copy = pltpu.make_async_copy(mine, dense_s, sem)
        dense_copy.start()
        row_number = lax.broadcasted_iota(jnp.int32, (32, n), 0)
        ones = jnp.where(lax.broadcasted_iota(jnp.int32, (16, n), 0) == 0, 1.0, 0.0).astype(BF)
        for h in range(TILE // SUB):
            x_s[h, EMB:XR, :] = jnp.where(row_number == DENSE, 1.0, 0.0).astype(BF)
            hid_s[h, D : D + 16, :] = ones
            for k in range(NE):
                mid_s[h, k, FH : FH + 16, :] = ones
            mix_s[h, 2 * EO : 2 * EO + 16, :] = ones
            fg_s[h, NE * FH + 16 : FG, :] = jnp.zeros((FG - NE * FH - 16, n), BF)
        for ref in (dwa_s, dw1_s, dw2_s, dtw_s, dcol_s, dlog_s):
            ref[...] = jnp.zeros_like(ref)
        users = start_s.shape[1]
        sizes = [line_ref[:, rows + 512 + users * b : rows + 512 + users * b + users] for b in range(start_s.shape[0])]
        fill_weights(core, batch_rows, jnp.concatenate(sizes, axis=0), start_s, row_s)
        dense_copy.wait()
        gates = []
        for side in range(2):
            base = HALF * FH * side
            holder = core if side == 0 else 1 - core
            for c in range(chunks):
                ref, c_in = u_refs[side][c * pieces // chunks], c % (chunks // pieces)
                at = chunk_at(c, chunks, holder)
                to = pl.multiple_of(ds * at, ds)
                w1_s[pl.ds(to, ds), base : base + QA] = ref[c_in, :, 0:QA]
                q_s[tab_ref[1 + at]] = ref[c_in, 0:fs, QA:UC].astype(F32)
                small = ref[c_in, 0:fs, QS:UC].astype(F32)
                ga_s[pl.ds(to, fs), :] = small
                ga_s[pl.ds(pl.multiple_of(to + fs, fs), fs), :] = pltpu.roll(small, 128 - NE, 1)
                wat_s[pl.ds(pl.multiple_of(to + holder * fs, fs), fs), :] = ref[c_in, fs:ds, QA : QA + XR]
            for k in range(HALF):
                block = w1_s[:, base + FH * k : base + FH * k + FH]
                w1t_s[base + FH * k : base + FH * k + FH, :] = (block.astype(F32).T * 0.5).astype(BF)
            gates.append(swap_halves(ga_s[...].T[GA : GA + NE], second_core))
            cols = HALF * EO
            w2 = q_s[:, :, 0:cols].reshape(FH, cols) * 0.5
            w2_s[:, cols * side : cols * side + cols] = w2.astype(BF)
            w2t_s[cols * side : cols * side + cols, :] = w2.T.astype(BF)
            b1_s[side] = q_s[:, :, cols : cols + 128].reshape(FH, 128) * 0.5
            last = q_s[:, 0:osz, cols : cols + 128].reshape(EO, 128)
            b2_s[side] = last * 0.5
            tower = last[:, 0:TW]
            rest = jnp.zeros_like(tower)
            both = jnp.concatenate([tower, rest] if side == 0 else [rest, tower], axis=1)
            tw_s[EO * side : EO * side + EO, :] = both.astype(BF)
            tt_s[:, EO * side : EO * side + EO] = (both.T * 0.5).astype(BF)
        gates = jnp.concatenate(gates, axis=0)
        w1t_s[NE * FH : NE * FH + 16, :] = gates.astype(BF)
        pad = jnp.concatenate([gates, jnp.zeros((112, D), F32)], axis=0)
        w1_s[:, NE * FH : FG] = pad.T.astype(BF)
        vecs = [square([r[:, rows + 128 * j : rows + 128 * j + 128] for j in range(4)]).T for r in (line_ref, far_line_ref)]
        gb_s[...] = jnp.concatenate([swap_halves(v[0:NE, 0:1], second_core) for v in vecs], axis=0)
        b1 = jnp.concatenate([v[0:TW, 1:2] for v in vecs], axis=0)
        head = jnp.concatenate([v[0:TW, 2:3] for v in vecs], axis=0)
        last = jnp.concatenate([v[0:1, 3:4] for v in vecs] * TW, axis=0)
        tcol_s[...] = jnp.concatenate([b1 * 0.5, head, head * 0.5, last], axis=1)

    def chain(h):
        at = slice(SUB * h, SUB * h + SUB)
        x_s[h, 0:EMB, :] = emb_ref[:, at]
        x_s[h, EMB : EMB + DENSE, :] = dense_s[:, pl.ds(pl.multiple_of(step * TILE + SUB * h, SUB), SUB)]
        hid = mm(wat_s[...], x_s[h]).astype(BF)
        hid_s[h, 0:D, :] = hid
        yield
        logits = mm(w1t_s[NE * FH : NE * FH + 16, :], hid) + gb_s[...]
        probs = []
        for t in range(2):
            lt = logits[NE * t : NE * t + NE]
            e = jnp.exp(lt - jnp.max(lt, axis=0, keepdims=True))
            probs.append(e / jnp.sum(e, axis=0, keepdims=True))
        mix = [None, None]
        pend = None
        nxt = mm(w1t_s[0:FH, :], hid)
        yield
        for k in range(NE + 1):
            pre = nxt
            if k < NE - 1:
                nxt = mm(w1t_s[FH * (k + 1) : FH * (k + 2), :], hid)
            if k < NE:
                m, s = act_narrow(pre + b1_s[k // HALF, :, B1 + k % HALF : B1 + k % HALF + 1])
                mid_s[h, k, 0:FH, :] = m
                sl1_s[h, FH * k : FH * k + FH, :] = s
                pre2 = mm(w2t_s[EO * k : EO * k + EO, :], m)
            if pend is not None:
                j = k - 1
                o, s = act_narrow(pend + b2_s[j // HALF, :, TW + j % HALF : TW + j % HALF + 1])
                out_s[h, EO * j : EO * j + EO, :] = o
                sl2_s[h, EO * j : EO * j + EO, :] = s
                o = o.astype(F32)
                for t in range(2):
                    term = probs[t][j : j + 1, :] * o
                    mix[t] = term if j == 0 else mix[t] + term
            pend = pre2
            yield
        mix_s[h, 0:EO, :] = mix[0].astype(BF)
        mix_s[h, EO : 2 * EO, :] = mix[1].astype(BF)
        act, slope = act_pair(mm(tt_s[...], mix_s[h, 0 : 2 * EO, :]) + tcol_s[:, 0:1])
        weighted = act * tcol_s[:, 1:2]
        lgos = []
        for t in range(2):
            logit = jnp.sum(weighted[TW * t : TW * t + TW], axis=0, keepdims=True) + tcol_s[t : t + 1, 3:4]
            label = (line_ref, far_line_ref)[t][:, pl.ds(pl.multiple_of((core * pl.num_programs(0) + step) * TILE + SUB * h, SUB), SUB)]
            lgos.append(row_s[:, pl.ds(pl.multiple_of(step * TILE + SUB * h, SUB), SUB)] * (0.5 * jnp.tanh(0.5 * logit) + 0.5 - label))
        lgo = jnp.concatenate([jnp.broadcast_to(lgos[t], (TW, SUB)) for t in range(2)], axis=0)
        dcol_s[...] += lane_fold(lgo * act)
        dlog_s[...] += lane_fold(jnp.concatenate([jnp.broadcast_to(lgos[t], (8, SUB)) for t in range(2)], axis=0))
        tg = (lgo * (tcol_s[:, 2:3] * slope)).astype(BF)
        yield
        dtw_s[...] += mm_nt(mix_s[h], tg)
        mgh = mm(tw_s[...], tg) * 0.5
        yield
        pgs = [[], []]
        mgs = [None] * NE
        for k in range(NE + 2):
            if k < NE:
                o = out_s[h, EO * k : EO * k + EO, :]
                og = None
                for t in range(2):
                    mg = mgh[EO * t : EO * t + EO]
                    pgs[t].append(jnp.sum((o * mg.astype(BF)).astype(F32), axis=0, keepdims=True))
                    term = probs[t][k : k + 1, :] * mg
                    og = term if og is None else og + term
                sg = og.astype(BF) * sl2_s[h, EO * k : EO * k + EO, :]
                sg_s[h, EO * (k % 2) : EO * (k % 2) + EO, :] = sg
                mgs[k] = mm(w2_s[:, EO * k : EO * k + EO], sg)
            if 1 <= k < NE + 1:
                j = k - 1
                dw2_s[:, EO * j : EO * j + EO] += mm_nt(mid_s[h, j], sg_s[h, EO * (j % 2) : EO * (j % 2) + EO, :])
                fg = mgs[j].astype(BF) * sl1_s[h, FH * j : FH * j + FH, :]
                fg_s[h, FH * j : FH * j + FH, :] = fg
            if k >= 2:
                j = k - 2
                dw1_s[:, FH * j : FH * j + FH] += mm_nt(hid_s[h], fg_s[h, FH * j : FH * j + FH, :])
            yield
        lgs = []
        for t in range(2):
            pg = jnp.concatenate(pgs[t], axis=0)
            lgs.append(2.0 * probs[t] * (pg - jnp.sum(probs[t] * pg, axis=0, keepdims=True)))
        fg_s[h, NE * FH : NE * FH + 16, :] = jnp.concatenate(lgs, axis=0).astype(BF)
        yield
        dw1_s[:, NE * FH : FG] += mm_nt(hid_s[h], fg_s[h, NE * FH : FG, :])
        hg = mm(w1_s[...], fg_s[h]).astype(BF)
        hg_ref[:, at] = hg
        yield
        dwa_s[...] += mm_nt(hg, x_s[h])
        yield

    take_turns([chain(h) for h in range(TILE // SUB)], LAG)

    @pl.when(step == pl.num_programs(0) - 1)
    def _():
        gate = dw1_s[:, NE * FH : FG].T
        dlog = jnp.sum(dlog_s[...], axis=1, keepdims=True)
        dcol = jnp.sum(dcol_s[...].T, axis=0, keepdims=True)
        for side in range(2):
            own_gate = swap_halves(gate[NE * side : NE * side + NE], second_core)
            ga_s[...] = jnp.concatenate([own_gate[:, 0:D], jnp.zeros((120, D), F32)], axis=0).T
            b1 = [dw1_s[D : D + 1, FH * k : FH * k + FH] for k in range(HALF * side, HALF * side + HALF)]
            b1 = jnp.concatenate(b1 + [jnp.zeros((124, FH), F32)], axis=0).T
            b2 = [dw2_s[FH : FH + 1, EO * k : EO * k + EO] for k in range(HALF * side, HALF * side + HALF)]
            b2 = jnp.concatenate(b2 + [jnp.zeros((60, EO), F32)], axis=0).T
            tower = dtw_s[EO * side : EO * side + EO, TW * side : TW * side + TW]
            tower = jnp.concatenate([tower, b2], axis=1)
            lanes = slice(TW * side, TW * side + TW)
            blank = jnp.zeros((1, TW), F32)
            lines = [jnp.concatenate([a, blank], axis=1) for a in (dtw_s[2 * EO : 2 * EO + 1, lanes], dcol[:, lanes])]
            gate_b = jnp.sum(jnp.where(lax.broadcasted_iota(jnp.int32, (NE, D + 16), 1) == D, own_gate, 0.0), axis=1, keepdims=True)
            small = jnp.concatenate([gate_b, dlog[8 * side : 8 * side + 8]], axis=0)
            small = jnp.concatenate([jnp.broadcast_to(small, (16, 128)), jnp.zeros((112, 128), F32)], axis=0).T[0:1]
            tail = jnp.concatenate(lines + [small, jnp.zeros((fs - osz - 3, 128), F32)], axis=0)
            b1 = pltpu.roll(b1, B1, 1)
            for c in range(chunks):
                dsm_s[fs * c : fs * c + fs, :] = b1[fs * c : fs * c + fs] + jnp.concatenate([tower[osz * c : osz * c + osz], tail], axis=0)
            holder = core if side == 0 else 1 - core
            cols = HALF * EO
            for n in range(chunks):
                ref, c = du_refs[2 * side + n * 2 // chunks], n % max(chunks // 2, 1)
                at = chunk_at(n, chunks, holder)
                to = pl.multiple_of(ds * at, ds)
                where = pl.ds(pl.multiple_of(tab_ref[1 + at] * fs, fs), fs)
                ref[c, :, 0:QA] = dw1_s[pl.ds(to, ds), QA * side : QA * side + QA].astype(BF)
                ref[c, 0:fs, QA:QS] = dw2_s[where, cols * side : cols * side + cols].astype(BF)
                low = pltpu.roll(ga_s[pl.ds(to, fs), :], GA, 1)
                high = pltpu.roll(ga_s[pl.ds(pl.multiple_of(to + fs, fs), fs), :], GA + NE, 1)
                ref[c, 0:fs, QS:UC] = (dsm_s[where, :] + low + high).astype(BF)
                lower = dwa_s[pl.ds(pl.multiple_of(to + holder * fs, fs), fs), :]
                ref[c, fs:ds, QA:UC] = jnp.concatenate([lower, jnp.zeros((fs, UC - QA - XR), F32)], axis=1).astype(BF)


def fill_weights(core, batch_rows, sizes, start_s, out_ref):
    batches, users = sizes.shape
    counts = jnp.concatenate([sizes.astype(F32), jnp.zeros((16 - batches, users), F32)], axis=0)
    turned = jnp.concatenate([counts, jnp.zeros((112, users), F32)], axis=0).T
    before = lax.broadcasted_iota(jnp.int32, (users, users), 1) < lax.broadcasted_iota(jnp.int32, (users, users), 0)
    starts = mm(jnp.where(before, 1.0, 0.0).astype(BF), turned.astype(BF))
    for b in range(batches):
        start_s[b] = jnp.broadcast_to(starts[:, b : b + 1], (users, 128))
    first = lax.broadcasted_iota(jnp.int32, counts.shape, 1) == 0
    rises = counts - jnp.where(first, 0.0, pltpu.roll(counts, 1, 1))
    line = lax.broadcasted_iota(jnp.int32, counts.shape, 0)
    steps = out_ref.shape[1] // SUB
    for step in range(steps):
        at_step = core * steps + step
        batch = at_step // (batch_rows // SUB)
        first_row = (at_step % (batch_rows // SUB) * SUB).astype(F32)
        begins = start_s[batch]
        places = first_row + lax.broadcasted_iota(jnp.int32, (1, 128), 1).astype(F32)
        begun = [jnp.where(begins <= places + 128.0 * c, 1.0, 0.0).astype(BF) for c in range(SUB // 128)]
        rise = jnp.where(line == batch, rises, 0.0).astype(BF)
        size = jnp.sum(mm(rise, jnp.concatenate(begun, axis=1)), axis=0, keepdims=True)
        out_ref[:, SUB * step : SUB * step + SUB] = 1.0 / size


def const2(i, c):
    return (0, 0)


def main_call(table, embt, denset, line, far_line, sizes_shape, own_u, far_u):
    rows = embt.shape[1]
    half = rows // 2
    steps = half // TILE
    pieces = len(own_u)
    chunks = sum(a.shape[0] for a in own_u)
    fs, ds = FH // chunks, D // chunks

    def own(i, c):
        return (0, c[0] * steps + i)

    grads = [(max(chunks // 2, 1), ds, UC)] * 4
    parts = TILE // SUB
    spec = pltpu.PrefetchScalarGridSpec(
        num_scalar_prefetch=1,
        grid=(steps,),
        in_specs=[
            pl.BlockSpec((EMB, TILE), own),
            whole(pltpu.HBM),
            whole(),
            whole(),
        ]
        + [whole() for _ in (*own_u, *far_u)],
        out_specs=[pl.BlockSpec((D, TILE), lambda i, c: (0, i))] + [whole()] * 5,
        scratch_shapes=[
            pltpu.VMEM((parts, XR, SUB), BF),
            pltpu.VMEM((parts, D + 16, SUB), BF),
            pltpu.VMEM((parts, NE, FH + 16, SUB), BF),
            pltpu.VMEM((parts, NE * FH, SUB), BF),
            pltpu.VMEM((parts, NE * EO, SUB), BF),
            pltpu.VMEM((parts, NE * EO, SUB), BF),
            pltpu.VMEM((parts, 2 * EO, SUB), BF),
            pltpu.VMEM((parts, FG, SUB), BF),
            pltpu.VMEM((parts, 2 * EO + 16, SUB), BF),
            pltpu.VMEM((D, FG), BF),
            pltpu.VMEM((NE * FH + 16, D), BF),
            pltpu.VMEM((D, 128), F32),
            pltpu.VMEM((NE * EO, FH), BF),
            pltpu.VMEM((FH, NE * EO), BF),
            pltpu.VMEM((2, FH, 128), F32),
            pltpu.VMEM((2, EO, 128), F32),
            pltpu.VMEM((16, 1), F32),
            pltpu.VMEM((2 * TW, 2 * EO), BF),
            pltpu.VMEM((2 * EO, 2 * TW), BF),
            pltpu.VMEM((2 * TW, 4), F32),
            pltpu.VMEM((chunks, fs, UC - QA), F32),
            pltpu.VMEM((D, XR), F32),
            pltpu.VMEM((D + 16, FG), F32),
            pltpu.VMEM((FH + 16, NE * EO), F32),
            pltpu.VMEM((2 * EO + 16, 2 * TW), F32),
            pltpu.VMEM((2 * TW, 128), F32),
            pltpu.VMEM((16, 128), F32),
            pltpu.VMEM((FH, 128), F32),
            pltpu.VMEM((DENSE, half), BF),
            pltpu.VMEM((*sizes_shape, 128), F32),
            pltpu.VMEM((1, half), F32),
            pltpu.SemaphoreType.DMA(()),
        ],
    )
    return pl.pallas_call(
        functools.partial(main_kernel, pieces, chunks, rows, rows // sizes_shape[0]),
        grid_spec=spec,
        out_shape=[jax.ShapeDtypeStruct((D, half), BF), jax.ShapeDtypeStruct((D, XR), BF)]
        + [jax.ShapeDtypeStruct(a, BF) for a in grads],
        compiler_params=pltpu.CompilerParams(vmem_limit_bytes=48 * 1024 * 1024),
        cost_estimate=pl.CostEstimate(flops=50_000_000_000, bytes_accessed=24_000_000, transcendentals=0),
        name="experts",
    )(table, embt, denset, line, far_line, *own_u, *far_u)


def input_kernel(tab_ref, hg_ref, wat_ref, *refs):
    eg_ref, dg_ref, done_ref, wa_s = refs[-4:]

    @pl.when(pl.program_id(0) == 0)
    def _():
        wa_s[...] = wat_ref[...].astype(F32).T.astype(BF)
        done_ref[...] = jnp.zeros_like(done_ref)

    eg = mm(wa_s[...], hg_ref[...])
    eg_ref[...] = eg[0:EMB]
    dg_ref[...] = eg[EMB : EMB + DENSE]


def input_call(table, hg, wat, token, other, name):
    half = hg.shape[1]
    tile = TILE
    steps = half // tile

    def place(i, c):
        return (0, (c[0] if other is None else 1 - c[0]) * steps + i)

    extra = [token] + (list(other) if other is not None else [])
    spec = pltpu.PrefetchScalarGridSpec(
        num_scalar_prefetch=1,
        grid=(steps,),
        in_specs=[pl.BlockSpec((D, tile), lambda i, c: (0, i)), pl.BlockSpec((D, XR), const2, pipeline_mode=pl.Buffered(1))]
        + [whole(pl.ANY) for _ in extra],
        out_specs=[pl.BlockSpec((EMB, tile), place), pl.BlockSpec((DENSE, tile), place), pl.BlockSpec((8, 128), const2)],
        scratch_shapes=[pltpu.VMEM((XR, D), BF)],
    )
    return pl.pallas_call(
        input_kernel,
        grid_spec=spec,
        out_shape=[jax.ShapeDtypeStruct((EMB, 2 * half), F32), jax.ShapeDtypeStruct((DENSE, 2 * half), F32), jax.ShapeDtypeStruct((8, 128), F32)],
        input_output_aliases={} if other is None else {4: 0, 5: 1},
        compiler_params=pltpu.CompilerParams(vmem_limit_bytes=32 * 1024 * 1024),
        cost_estimate=pl.CostEstimate(flops=4_000_000_000, bytes_accessed=9_000_000, transcendentals=0),
        name=name,
    )(table, hg, wat, *extra)


def widen(a):
    return jnp.concatenate([a.astype(F32), jnp.zeros((a.shape[0], 128 - a.shape[1]), F32)], axis=1)


def square(rows):
    count = sum(a.shape[0] for a in rows)
    return jnp.concatenate(rows + [jnp.zeros((128 - count, 128), F32)], axis=0)


def pack_kernel(core_ref, emb_ref, dense_ref, bias_ref, w1_ref, w2_ref, b1_ref, b2_ref, gate_ref, tower_ref, *refs):
    sizes_ref, label_ref, u_ref, line_ref = refs[4:]
    rows = label_ref.shape[1]
    line_ref[:, 0:rows] = label_ref[...].astype(F32)
    for j in range(4):
        line_ref[:, rows + 128 * j : rows + 128 * j + 128] = widen(refs[j][...])
    users = sizes_ref.shape[1]
    for b in range(sizes_ref.shape[0]):
        line_ref[:, rows + 512 + users * b : rows + 512 + users * b + users] = sizes_ref[b : b + 1, :].astype(F32)
    fs = u_ref.shape[0] // 2
    turned = square([widen(r[...]) for r in (b1_ref, b2_ref, gate_ref, dense_ref, bias_ref)]).T
    lane = lax.broadcasted_iota(jnp.int32, (fs, 128), 1)
    low, high = turned[0:fs], turned[fs : 2 * fs]
    small = jnp.concatenate([widen(tower_ref[...]), jnp.zeros((fs - tower_ref.shape[0], 128), F32)], axis=0)
    small += jnp.where((lane >= TW) & (lane < TW + HALF), pltpu.roll(low, TW - HALF, 1), 0.0)
    small += jnp.where(((lane >= B1) & (lane < B1 + HALF)) | ((lane >= GA) & (lane < GA + NE)), pltpu.roll(low, B1, 1), 0.0)
    small += jnp.where((lane >= GA + NE) & (lane < GA + 2 * NE), pltpu.roll(high, GA, 1), 0.0)
    for k in range(HALF):
        u_ref[:, FH * k : FH * k + FH] = w1_ref[k]
        u_ref[0:fs, QA + EO * k : QA + EO * k + EO] = w2_ref[k]
    u_ref[0:fs, QS:UC] = small.astype(BF)
    second_core = core_ref[0] == 1
    lanes = lax.broadcasted_iota(jnp.int32, (2 * fs, 128), 1)
    last = widen(emb_ref[:, 384:EMB]) + jnp.where((lanes >= 32) & (lanes < 33 + DENSE), pltpu.roll(turned[0 : 2 * fs], 16, 1), 0.0)
    for c in range(3):
        block = emb_ref[:, 128 * c : 128 * c + 128]
        u_ref[fs:, QA + 128 * c : QA + 128 * c + 128] = jnp.where(second_core, block[fs:], block[0:fs])
    u_ref[fs:, QA + 384 : QA + 512] = jnp.where(second_core, last[fs:], last[0:fs]).astype(BF)
    u_ref[fs:, QA + 512 : UC] = jnp.zeros((fs, UC - QA - 512), BF)


def whole(memory=pltpu.VMEM):
    return pl.BlockSpec(memory_space=memory)


def pack_call(core, *parts):
    ds = parts[3].shape[1]
    return pl.pallas_call(
        pack_kernel,
        in_specs=[whole(pltpu.SMEM)] + [whole() for _ in parts],
        out_specs=[whole(), whole()],
        out_shape=[jax.ShapeDtypeStruct((ds, UC), BF), jax.ShapeDtypeStruct((1, parts[-1].shape[1] + 512 + parts[-2].size), F32)],
        name="pack",
    )(core, *parts)


def sum_kernel(groups, count, *refs):
    ins, outs = refs[:count], refs[-len(groups) :]
    for group, out in zip(groups, outs):
        total = None
        for number, at in group:
            term = ins[number][at].astype(F32)
            total = term if total is None else total + term
        out[...] = total.astype(out.dtype)


def sum_call(name, arrays, groups, shapes, token=None, through=None):
    extra = [a for a in (token, through) if a is not None]
    lead = [] if through is None else [through]
    return pl.pallas_call(
        functools.partial(sum_kernel, groups, len(arrays)),
        in_specs=[whole() for _ in arrays] + [whole(pl.ANY) for _ in extra],
        out_specs=[whole(pl.ANY) for _ in lead] + [whole() for _ in shapes],
        out_shape=[jax.ShapeDtypeStruct(a.shape, a.dtype) for a in lead] + [jax.ShapeDtypeStruct(a, BF) for a in shapes],
        input_output_aliases={len(arrays) + len(extra) - 1: 0} if lead else {},
        compiler_params=pltpu.CompilerParams(vmem_limit_bytes=16 * 1024 * 1024),
        name=name,
    )(*arrays, *extra)


def finish_kernel(scale, core_ref, token_ref, *refs):
    total = sum(r[...].astype(F32) for r in refs[:4]) * scale
    ds = total.shape[0]
    fs = ds // 2
    own_part = total[fs:, QA : QA + XR]
    far_part = sum(r[...].astype(F32) for r in refs[4:8])[:, 0:XR] * scale
    second_core = core_ref[0] == 1
    ta = jnp.concatenate([jnp.where(second_core, far_part, own_part), jnp.where(second_core, own_part, far_part)], axis=0)
    emb_ref, dense_ref, bias_ref, w1_ref, b1_ref, w2_ref, b2_ref, gate_ref, gb_ref, tower_ref, t1_ref, t2_ref, t3_ref = refs[8:]
    osz = tower_ref.shape[0]
    for k in range(HALF):
        w1_ref[k] = total[:, FH * k : FH * k + FH]
        w2_ref[k] = total[0:fs, QA + EO * k : QA + EO * k + EO]
    small = total[0:fs, QS:UC]
    turned = square([small]).T
    b1_ref[...] = turned[B1 : B1 + HALF, 0:fs]
    b2_ref[...] = turned[TW : TW + HALF, 0:osz]
    gates = turned[GA : GA + NE] + pltpu.roll(turned[GA + NE : GA + 2 * NE], fs, 1)
    gate_ref[...] = gates[:, 0 : 2 * fs]
    tower_ref[...] = small[0:osz, 0:TW]
    t1_ref[...] = small[osz : osz + 1, 0:TW]
    t2_ref[...] = small[osz + 1 : osz + 2, 0:TW]
    gb_ref[...] = small[osz + 2 : osz + 3, 0:NE]
    t3_ref[...] = small[osz + 2 : osz + 3, NE : NE + 1]
    emb_ref[...] = ta[:, 0:EMB]
    last = square([widen(ta[:, 384:XR])]).T
    dense_ref[...] = last[32 : 32 + DENSE, 0 : 2 * fs]
    bias_ref[...] = last[32 + DENSE : 33 + DENSE, 0 : 2 * fs]


def finish_call(scale, core, token, arrays, ds, fs, osz):
    shapes = [
        (ds, EMB), (DENSE, ds), (1, ds), (HALF, ds, FH), (HALF, fs), (HALF, fs, EO), (HALF, osz), (NE, ds), (1, NE),
        (osz, TW), (1, TW), (1, TW), (1, 1),
    ]
    return pl.pallas_call(
        functools.partial(finish_kernel, scale),
        in_specs=[whole(pltpu.SMEM), whole(pl.ANY)] + [whole() for _ in arrays],
        out_specs=[whole() for _ in shapes],
        out_shape=[jax.ShapeDtypeStruct(a, F32) for a in shapes],
        compiler_params=pltpu.CompilerParams(vmem_limit_bytes=8 * 1024 * 1024),
        name="finish",
    )(core, token, *arrays)


def hop(a, mask, size):
    return lax.ppermute(a, "rows", [(i, i ^ mask) for i in range(size)])


def cross(a, masks, size):
    pairs = [(2 * i + t, 2 * (i ^ masks[t]) + t) for i in range(size) for t in range(2)]
    return lax.ppermute(a, ("rows", "task"), pairs)


def partner(a):
    return lax.ppermute(a, "task", [(0, 1), (1, 0)])


def add_wide(a, b):
    return a.astype(F32) + b.astype(F32)


def pad_to(a, rows, cols):
    return jnp.pad(a, ((0, rows - a.shape[0]), (0, cols - a.shape[1])))


def body(
    emb, dense, group_sizes, labels, w_emb, w_dense, b_in, expert_w1, expert_b1, expert_w2, expert_b2,
    gate_w, gate_b, tower_w1, tower_b1, tower_w2, tower_b2,
):
    size = lax.axis_size("rows")
    core = lax.axis_index("task")
    place = lax.axis_index("rows")
    user_count = group_sizes.shape[1] * group_sizes.shape[0] * size
    ds, fs, osz = D // size, FH // size, EO // size
    fast = size == 16
    smalls = (gate_b, tower_b1, tower_w2, tower_b2[None])

    if fast:
        one_core = core[None].astype(jnp.int32)
        gate_t = jnp.transpose(gate_w, (0, 2, 1))[0]
        shard, line = pack_call(
            one_core, w_emb.T, w_dense, b_in[None], expert_w1, expert_w2, expert_b1, expert_b2, gate_t, tower_w1[0], *smalls, group_sizes, labels
        )
        near = jnp.stack([shard] + [hop(shard, 4 * a, size) for a in range(1, 4)])
        once = cross(near, (1, 2), size)
        own_u = [near, once, cross(near, (2, 1), size), cross(once, (2, 1), size)]
        steps = jnp.arange(16, dtype=jnp.int32)
        order = place ^ (steps % 4 * 4 + steps // 4)
    else:
        gather = functools.partial(lax.all_gather, axis_name="rows", axis=0, tiled=True)
        proj = jnp.concatenate([w_emb.T, w_dense.T, b_in[:, None], jnp.zeros((ds, 82), BF)], axis=1)
        w1_all = gather(jnp.transpose(expert_w1, (1, 0, 2)).reshape(ds, QA))
        w2_all = gather(jnp.transpose(expert_w2, (1, 0, 2)).reshape(fs, HALF * EO))
        o_all = gather(jnp.concatenate([tower_w1[0], expert_b2.T], axis=1))
        b1_all, g_all, proj_all = gather(expert_b1.T), gather(gate_w[0]), gather(proj)
        small = jnp.concatenate([pad_to(o_all, FH, B1), pad_to(b1_all, FH, GA - B1), g_all[0:FH], g_all[FH:], jnp.zeros((FH, 32), BF)], axis=1)
        part = jnp.where(core == 0, proj_all[0:FH], proj_all[FH:])
        lower = jnp.concatenate([part, jnp.zeros((FH, UC - QA - 512), BF)], axis=1)
        own_u = [jnp.concatenate([w1_all, jnp.concatenate([jnp.concatenate([w2_all, small], axis=1), lower], axis=0)], axis=1)[None]]
        order = jnp.zeros((1,), jnp.int32)
        line = [labels.astype(F32)] + [pad_to(a, 1, 128).astype(F32) for a in smalls]
        line = jnp.concatenate(line + [group_sizes.astype(F32).reshape(1, -1)], axis=1)
    far_u = [partner(a) for a in own_u]
    table = jnp.concatenate([core[None].astype(jnp.int32), order])

    hg, wat, own_low, own_high, du_low, du_high = main_call(table, emb.T, dense.T, line, partner(line), group_sizes.shape, own_u, far_u)
    du_high = partner(du_high)
    scale = 1.0 / user_count
    if fast:
        hg, part = sum_call("sum_cores", [own_high, du_high], [[(0, slice(0, 8)), (1, slice(0, 8))]], [(8, ds, UC)], through=hg)
        got = cross(part, (2, 1), size)
        du_low, far_hg = partner(du_low), partner(hg)
        eg, dg, token = input_call(table, hg, wat, part, None, "input_own")
        groups = [[(j, slice(4 * b, 4 * b + 4)) for j in range(3)] for b in (1, 0)]
        part, rest = sum_call("sum_first", [own_low, du_low, got], groups, [(4, ds, UC)] * 2, token)
        got = cross(part, (1, 2), size)
        eg, dg, token = input_call(table, far_hg, wat, part, (eg, dg), "input_far")
        sums = sum_call("sum_second", [rest, got], [[(0, k), (1, k)] for k in range(4)], [(ds, UC)] * 4, token)
        parts = [sums[0]] + [hop(sums[a], 4 * a, size) for a in range(1, 4)]
        parts += [partner(a[fs:, QA : QA + 512]) for a in parts]
        out = finish_call(scale, one_core, sums[0], parts, ds, fs, osz)
        g_emb, g_dense, g_bias, g_w1, g_b1, g_w2, g_b2, g_gate, g_gb, g_tower, g_t1, g_t2, g_t3 = out
        return (
            eg.T, dg.T, g_emb.T, g_dense, g_bias[0], g_w1, g_b1, g_w2, g_b2, g_gate.T[None], g_gb, g_tower[None], g_t1, g_t2, g_t3[0],
        )
    eg, dg, token = input_call(table, hg, wat, du_high, None, "input_own")
    eg, dg, _ = input_call(table, partner(hg), wat, token, (eg, dg), "input_far")
    scatter = functools.partial(lax.psum_scatter, axis_name="rows", scatter_dimension=0, tiled=True)
    wide = add_wide(own_low[0], partner(du_low)[0])
    upper, near = wide[0:FH, QA:UC], wide[FH:, QA : QA + XR]
    far, small = partner(near), upper[:, HALF * EO :]
    ta = scatter(jnp.concatenate([jnp.where(core == 0, near, far), jnp.where(core == 0, far, near)], axis=0)) * scale
    tp = jnp.transpose((scatter(wide[:, 0:QA]) * scale).reshape(ds, HALF, FH), (1, 0, 2))
    tw2, to, tb1 = scatter(upper[:, 0 : HALF * EO]) * scale, scatter(small[0:EO, 0:B1]) * scale, scatter(small[:, B1 : B1 + HALF]) * scale
    tg = scatter(jnp.concatenate([small[:, GA : GA + NE], small[:, GA + NE : GA + 2 * NE]], axis=0)) * scale
    ts = lax.psum(small[EO : EO + 3], "rows") * scale
    return (
        eg.T,
        dg.T,
        ta[:, 0:EMB].T,
        ta[:, EMB : EMB + DENSE].T,
        ta[:, EMB + DENSE],
        tp,
        tb1.T,
        jnp.transpose(tw2.reshape(fs, HALF, EO), (1, 0, 2)),
        to[:, TW : TW + HALF].T,
        tg[None],
        ts[2:3, 0:NE],
        to[:, 0:TW][None],
        ts[0:1, 0:TW],
        ts[1:2, 0:TW],
        ts[2, NE : NE + 1],
    )


def solution(mesh):
    in_specs = (
        P("rows", None),
        P("rows", None),
        P("rows", None),
        P("task", "rows"),
        P(None, "rows"),
        P(None, "rows"),
        P("rows"),
        P("task", "rows", None),
        P("task", "rows"),
        P("task", "rows", None),
        P("task", "rows"),
        P("task", "rows", None),
        P("task", None),
        P("task", "rows", None),
        P("task", None),
        P("task", None),
        P("task"),
    )
    out_specs = (
        P("rows", None),
        P("rows", None),
        P(None, "rows"),
        P(None, "rows"),
        P("rows"),
        P("task", "rows", None),
        P("task", "rows"),
        P("task", "rows", None),
        P("task", "rows"),
        P("task", "rows", None),
        P("task", None),
        P("task", "rows", None),
        P("task", None),
        P("task", None),
        P("task"),
    )
    return jax.shard_map(body, mesh=mesh, in_specs=in_specs, out_specs=out_specs, check_vma=False)
```

```python
import functools

import jax
import jax.numpy as jnp
from jax import lax
from jax.experimental import pallas as pl
from jax.experimental.pallas import tpu as pltpu
from jax.sharding import PartitionSpec as P

F32 = jnp.float32
BF = jnp.bfloat16
NT = (((1,), (1,)), ((), ()))
D, FH, EO, TW, NE = 512, 256, 128, 64, 8
HALF = NE // 2
EMB, DENSE = 416, 13
XR = 448
QA = HALF * FH
QS = QA + HALF * EO
UC = QS + 128
B1, GA = 72, 80
FG = NE * FH + 128
TILE = 1024
SUB = 512


def mm(a, b):
    return jnp.dot(a, b, preferred_element_type=F32)


def mm_nt(a, b):
    return lax.dot_general(a, b, NT, preferred_element_type=F32)


def act_narrow(half):
    return act_pair(half.astype(BF))


def act_pair(half):
    t = jnp.tanh(half)
    q = 1.0 + t
    m = half * q
    return m, q + m * (1.0 - t)


def swap_halves(a, flag):
    return jnp.where(flag, jnp.concatenate([a[HALF:NE], a[0:HALF]], axis=0), a)


def lane_fold(a):
    total = a[:, 0:128]
    for c in range(1, a.shape[1] // 128):
        total = total + a[:, 128 * c : 128 * c + 128]
    return total


def chunk_at(n, chunks, flag):
    if chunks == 1 or n // 4 in (0, 3):
        return n
    return n + 4 * flag if n // 4 == 1 else n - 4 * flag


LAG = 4


def take_turns(chains, lag):
    going = [(chain, lag * j) for j, chain in enumerate(chains)]
    while going:
        left = []
        for chain, wait in going:
            if wait > 0:
                left.append((chain, wait - 1))
            elif next(chain, True) is None:
                left.append((chain, 0))
        going = left


def main_kernel(pieces, chunks, batch_rows, tab_ref, *refs):
    emb_ref, dense_ref, line_ref, far_line_ref = refs[:4]
    u_refs = (refs[4 : 4 + pieces], refs[4 + pieces : 4 + 2 * pieces])
    hg_ref, wat_s, *du_refs = refs[4 + 2 * pieces : 10 + 2 * pieces]
    (
        x_s, hid_s, mid_s, sl1_s, out_s, sl2_s, sg_s, fg_s, mix_s,
        w1_s, w1t_s, ga_s, w2t_s, w2_s, b1_s, b2_s, gb_s, tt_s, tw_s, tcol_s, q_s,
        dwa_s, dw1_s, dw2_s, dtw_s, dcol_s, dlog_s, dsm_s, start_s, row_s,
    ) = refs[10 + 2 * pieces :]
    n = SUB
    fs, osz, ds = FH // chunks, EO // chunks, D // chunks
    step = pl.program_id(0)
    core = tab_ref[0]
    second_core = core == 1

    @pl.when(step == 0)
    def _():
        row_number = lax.broadcasted_iota(jnp.int32, (32, n), 0)
        ones = jnp.where(lax.broadcasted_iota(jnp.int32, (16, n), 0) == 0, 1.0, 0.0).astype(BF)
        for h in range(TILE // SUB):
            x_s[h, EMB:XR, :] = jnp.where(row_number == DENSE, 1.0, 0.0).astype(BF)
            hid_s[h, D : D + 16, :] = ones
            for k in range(NE):
                mid_s[h, k, FH : FH + 16, :] = ones
            mix_s[h, 2 * EO : 2 * EO + 16, :] = ones
            fg_s[h, NE * FH + 16 : FG, :] = jnp.zeros((FG - NE * FH - 16, n), BF)
        for ref in (dwa_s, dw1_s, dw2_s, dtw_s, dcol_s, dlog_s):
            ref[...] = jnp.zeros_like(ref)
        users = start_s.shape[1]
        after = row_s.shape[1] + 512
        sizes = [line_ref[:, after + users * b : after + users * b + users] for b in range(start_s.shape[0])]
        fill_weights(core, batch_rows, jnp.concatenate(sizes, axis=0), start_s, row_s)
        gates = []
        for side in range(2):
            base = HALF * FH * side
            holder = core if side == 0 else 1 - core
            for c in range(chunks):
                ref, c_in = u_refs[side][c * pieces // chunks], c % (chunks // pieces)
                at = chunk_at(c, chunks, holder)
                to = pl.multiple_of(ds * at, ds)
                w1_s[pl.ds(to, ds), base : base + QA] = ref[c_in, :, 0:QA]
                q_s[tab_ref[1 + at]] = ref[c_in, 0:fs, QA:UC].astype(F32)
                small = ref[c_in, 0:fs, QS:UC].astype(F32)
                ga_s[pl.ds(to, fs), :] = small
                ga_s[pl.ds(pl.multiple_of(to + fs, fs), fs), :] = pltpu.roll(small, 128 - NE, 1)
                wat_s[pl.ds(pl.multiple_of(to + holder * fs, fs), fs), :] = ref[c_in, fs:ds, QA : QA + XR]
            for k in range(HALF):
                block = w1_s[:, base + FH * k : base + FH * k + FH]
                w1t_s[base + FH * k : base + FH * k + FH, :] = (block.astype(F32).T * 0.5).astype(BF)
            gates.append(swap_halves(ga_s[...].T[GA : GA + NE], second_core))
            cols = HALF * EO
            w2 = q_s[:, :, 0:cols].reshape(FH, cols) * 0.5
            w2_s[:, cols * side : cols * side + cols] = w2.astype(BF)
            w2t_s[cols * side : cols * side + cols, :] = w2.T.astype(BF)
            b1_s[side] = q_s[:, :, cols : cols + 128].reshape(FH, 128) * 0.5
            last = q_s[:, 0:osz, cols : cols + 128].reshape(EO, 128)
            b2_s[side] = last * 0.5
            tower = last[:, 0:TW]
            rest = jnp.zeros_like(tower)
            both = jnp.concatenate([tower, rest] if side == 0 else [rest, tower], axis=1)
            tw_s[EO * side : EO * side + EO, :] = both.astype(BF)
            tt_s[:, EO * side : EO * side + EO] = (both.T * 0.5).astype(BF)
        gates = jnp.concatenate(gates, axis=0)
        w1t_s[NE * FH : NE * FH + 16, :] = gates.astype(BF)
        pad = jnp.concatenate([gates, jnp.zeros((112, D), F32)], axis=0)
        w1_s[:, NE * FH : FG] = pad.T.astype(BF)
        half = row_s.shape[1]
        vecs = [square([r[:, half + 128 * j : half + 128 * j + 128] for j in range(4)]).T for r in (line_ref, far_line_ref)]
        gb_s[...] = jnp.concatenate([swap_halves(v[0:NE, 0:1], second_core) for v in vecs], axis=0)
        b1 = jnp.concatenate([v[0:TW, 1:2] for v in vecs], axis=0)
        head = jnp.concatenate([v[0:TW, 2:3] for v in vecs], axis=0)
        last = jnp.concatenate([v[0:1, 3:4] for v in vecs] * TW, axis=0)
        tcol_s[...] = jnp.concatenate([b1 * 0.5, head, head * 0.5, last], axis=1)

    def chain(h):
        at = slice(SUB * h, SUB * h + SUB)
        x_s[h, 0:EMB, :] = emb_ref[:, at]
        x_s[h, EMB : EMB + DENSE, :] = dense_ref[:, pl.ds(pl.multiple_of(step * TILE + SUB * h, SUB), SUB)]
        hid = mm(wat_s[...], x_s[h]).astype(BF)
        hid_s[h, 0:D, :] = hid
        yield
        logits = mm(w1t_s[NE * FH : NE * FH + 16, :], hid) + gb_s[...]
        probs = []
        for t in range(2):
            lt = logits[NE * t : NE * t + NE]
            e = jnp.exp(lt - jnp.max(lt, axis=0, keepdims=True))
            probs.append(e / jnp.sum(e, axis=0, keepdims=True))
        mix = [None, None]
        pend = None
        nxt = mm(w1t_s[0:FH, :], hid)
        yield
        for k in range(NE + 1):
            pre = nxt
            if k < NE - 1:
                nxt = mm(w1t_s[FH * (k + 1) : FH * (k + 2), :], hid)
            if k < NE:
                m, s = act_narrow(pre + b1_s[k // HALF, :, B1 + k % HALF : B1 + k % HALF + 1])
                mid_s[h, k, 0:FH, :] = m
                sl1_s[h, FH * k : FH * k + FH, :] = s
                pre2 = mm(w2t_s[EO * k : EO * k + EO, :], m)
            if pend is not None:
                j = k - 1
                o, s = act_narrow(pend + b2_s[j // HALF, :, TW + j % HALF : TW + j % HALF + 1])
                out_s[h, EO * j : EO * j + EO, :] = o
                sl2_s[h, EO * j : EO * j + EO, :] = s
                o = o.astype(F32)
                for t in range(2):
                    term = probs[t][j : j + 1, :] * o
                    mix[t] = term if j == 0 else mix[t] + term
            pend = pre2
            yield
        mix_s[h, 0:EO, :] = mix[0].astype(BF)
        mix_s[h, EO : 2 * EO, :] = mix[1].astype(BF)
        act, slope = act_pair(mm(tt_s[...], mix_s[h, 0 : 2 * EO, :]) + tcol_s[:, 0:1])
        weighted = act * tcol_s[:, 1:2]
        lgos = []
        for t in range(2):
            logit = jnp.sum(weighted[TW * t : TW * t + TW], axis=0, keepdims=True) + tcol_s[t : t + 1, 3:4]
            label = (line_ref, far_line_ref)[t][:, pl.ds(pl.multiple_of(step * TILE + SUB * h, SUB), SUB)]
            lgos.append(row_s[:, pl.ds(pl.multiple_of(step * TILE + SUB * h, SUB), SUB)] * (0.5 * jnp.tanh(0.5 * logit) + 0.5 - label))
        lgo = jnp.concatenate([jnp.broadcast_to(lgos[t], (TW, SUB)) for t in range(2)], axis=0)
        dcol_s[...] += lane_fold(lgo * act)
        dlog_s[...] += lane_fold(jnp.concatenate([jnp.broadcast_to(lgos[t], (8, SUB)) for t in range(2)], axis=0))
        tg = (lgo * (tcol_s[:, 2:3] * slope)).astype(BF)
        yield
        dtw_s[...] += mm_nt(mix_s[h], tg)
        mgh = mm(tw_s[...], tg) * 0.5
        yield
        pgs = [[], []]
        mgs = [None] * NE
        for k in range(NE + 2):
            if k < NE:
                o = out_s[h, EO * k : EO * k + EO, :]
                og = None
                for t in range(2):
                    mg = mgh[EO * t : EO * t + EO]
                    pgs[t].append(jnp.sum((o * mg.astype(BF)).astype(F32), axis=0, keepdims=True))
                    term = probs[t][k : k + 1, :] * mg
                    og = term if og is None else og + term
                sg = og.astype(BF) * sl2_s[h, EO * k : EO * k + EO, :]
                sg_s[h, EO * (k % 2) : EO * (k % 2) + EO, :] = sg
                mgs[k] = mm(w2_s[:, EO * k : EO * k + EO], sg)
            if 1 <= k < NE + 1:
                j = k - 1
                dw2_s[:, EO * j : EO * j + EO] += mm_nt(mid_s[h, j], sg_s[h, EO * (j % 2) : EO * (j % 2) + EO, :])
                fg = mgs[j].astype(BF) * sl1_s[h, FH * j : FH * j + FH, :]
                fg_s[h, FH * j : FH * j + FH, :] = fg
            if k >= 2:
                j = k - 2
                dw1_s[:, FH * j : FH * j + FH] += mm_nt(hid_s[h], fg_s[h, FH * j : FH * j + FH, :])
            yield
        lgs = []
        for t in range(2):
            pg = jnp.concatenate(pgs[t], axis=0)
            lgs.append(2.0 * probs[t] * (pg - jnp.sum(probs[t] * pg, axis=0, keepdims=True)))
        fg_s[h, NE * FH : NE * FH + 16, :] = jnp.concatenate(lgs, axis=0).astype(BF)
        yield
        dw1_s[:, NE * FH : FG] += mm_nt(hid_s[h], fg_s[h, NE * FH : FG, :])
        hg = mm(w1_s[...], fg_s[h]).astype(BF)
        hg_ref[:, at] = hg
        yield
        dwa_s[...] += mm_nt(hg, x_s[h])
        yield

    take_turns([chain(h) for h in range(TILE // SUB)], LAG)

    @pl.when(step == pl.num_programs(0) - 1)
    def _():
        gate = dw1_s[:, NE * FH : FG].T
        dlog = jnp.sum(dlog_s[...], axis=1, keepdims=True)
        dcol = jnp.sum(dcol_s[...].T, axis=0, keepdims=True)
        for side in range(2):
            own_gate = swap_halves(gate[NE * side : NE * side + NE], second_core)
            ga_s[...] = jnp.concatenate([own_gate[:, 0:D], jnp.zeros((120, D), F32)], axis=0).T
            b1 = [dw1_s[D : D + 1, FH * k : FH * k + FH] for k in range(HALF * side, HALF * side + HALF)]
            b1 = jnp.concatenate(b1 + [jnp.zeros((124, FH), F32)], axis=0).T
            b2 = [dw2_s[FH : FH + 1, EO * k : EO * k + EO] for k in range(HALF * side, HALF * side + HALF)]
            b2 = jnp.concatenate(b2 + [jnp.zeros((60, EO), F32)], axis=0).T
            tower = dtw_s[EO * side : EO * side + EO, TW * side : TW * side + TW]
            tower = jnp.concatenate([tower, b2], axis=1)
            lanes = slice(TW * side, TW * side + TW)
            blank = jnp.zeros((1, TW), F32)
            lines = [jnp.concatenate([a, blank], axis=1) for a in (dtw_s[2 * EO : 2 * EO + 1, lanes], dcol[:, lanes])]
            gate_b = jnp.sum(jnp.where(lax.broadcasted_iota(jnp.int32, (NE, D + 16), 1) == D, own_gate, 0.0), axis=1, keepdims=True)
            small = jnp.concatenate([gate_b, dlog[8 * side : 8 * side + 8]], axis=0)
            small = jnp.concatenate([jnp.broadcast_to(small, (16, 128)), jnp.zeros((112, 128), F32)], axis=0).T[0:1]
            tail = jnp.concatenate(lines + [small, jnp.zeros((fs - osz - 3, 128), F32)], axis=0)
            b1 = pltpu.roll(b1, B1, 1)
            for c in range(chunks):
                dsm_s[fs * c : fs * c + fs, :] = b1[fs * c : fs * c + fs] + jnp.concatenate([tower[osz * c : osz * c + osz], tail], axis=0)
            holder = core if side == 0 else 1 - core
            cols = HALF * EO
            for n in range(chunks):
                ref, c = du_refs[2 * side + n * 2 // chunks], n % max(chunks // 2, 1)
                at = chunk_at(n, chunks, holder)
                to = pl.multiple_of(ds * at, ds)
                where = pl.ds(pl.multiple_of(tab_ref[1 + at] * fs, fs), fs)
                ref[c, :, 0:QA] = dw1_s[pl.ds(to, ds), QA * side : QA * side + QA].astype(BF)
                ref[c, 0:fs, QA:QS] = dw2_s[where, cols * side : cols * side + cols].astype(BF)
                low = pltpu.roll(ga_s[pl.ds(to, fs), :], GA, 1)
                high = pltpu.roll(ga_s[pl.ds(pl.multiple_of(to + fs, fs), fs), :], GA + NE, 1)
                ref[c, 0:fs, QS:UC] = (dsm_s[where, :] + low + high).astype(BF)
                lower = dwa_s[pl.ds(pl.multiple_of(to + holder * fs, fs), fs), :]
                ref[c, fs:ds, QA:UC] = jnp.concatenate([lower, jnp.zeros((fs, UC - QA - XR), F32)], axis=1).astype(BF)


def fill_weights(core, batch_rows, sizes, start_s, out_ref):
    batches, users = sizes.shape
    counts = jnp.concatenate([sizes.astype(F32), jnp.zeros((16 - batches, users), F32)], axis=0)
    turned = jnp.concatenate([counts, jnp.zeros((112, users), F32)], axis=0).T
    before = lax.broadcasted_iota(jnp.int32, (users, users), 1) < lax.broadcasted_iota(jnp.int32, (users, users), 0)
    starts = mm(jnp.where(before, 1.0, 0.0).astype(BF), turned.astype(BF))
    for b in range(batches):
        start_s[b] = jnp.broadcast_to(starts[:, b : b + 1], (users, 128))
    first = lax.broadcasted_iota(jnp.int32, counts.shape, 1) == 0
    rises = counts - jnp.where(first, 0.0, pltpu.roll(counts, 1, 1))
    line = lax.broadcasted_iota(jnp.int32, counts.shape, 0)
    steps = out_ref.shape[1] // SUB
    for step in range(steps):
        at_step = core * steps + step
        batch = at_step // (batch_rows // SUB)
        first_row = (at_step % (batch_rows // SUB) * SUB).astype(F32)
        begins = start_s[batch]
        places = first_row + lax.broadcasted_iota(jnp.int32, (1, 128), 1).astype(F32)
        begun = [jnp.where(begins <= places + 128.0 * c, 1.0, 0.0).astype(BF) for c in range(SUB // 128)]
        rise = jnp.where(line == batch, rises, 0.0).astype(BF)
        size = jnp.sum(mm(rise, jnp.concatenate(begun, axis=1)), axis=0, keepdims=True)
        out_ref[:, SUB * step : SUB * step + SUB] = 1.0 / size


def const2(i, c):
    return (0, 0)


def main_call(table, embt, denset, line, far_line, sizes_shape, own_u, far_u):
    rows = embt.shape[1]
    half = rows // 2
    steps = half // TILE
    pieces = len(own_u)
    chunks = sum(a.shape[0] for a in own_u)
    fs, ds = FH // chunks, D // chunks

    def own(i, c):
        return (0, c[0] * steps + i)

    grads = [(max(chunks // 2, 1), ds, UC)] * 4
    parts = TILE // SUB
    spec = pltpu.PrefetchScalarGridSpec(
        num_scalar_prefetch=1,
        grid=(steps,),
        in_specs=[
            pl.BlockSpec((EMB, TILE), own),
            whole(),
            whole(),
            whole(),
        ]
        + [whole() for _ in (*own_u, *far_u)],
        out_specs=[pl.BlockSpec((D, TILE), lambda i, c: (0, i))] + [whole()] * 5,
        scratch_shapes=[
            pltpu.VMEM((parts, XR, SUB), BF),
            pltpu.VMEM((parts, D + 16, SUB), BF),
            pltpu.VMEM((parts, NE, FH + 16, SUB), BF),
            pltpu.VMEM((parts, NE * FH, SUB), BF),
            pltpu.VMEM((parts, NE * EO, SUB), BF),
            pltpu.VMEM((parts, NE * EO, SUB), BF),
            pltpu.VMEM((parts, 2 * EO, SUB), BF),
            pltpu.VMEM((parts, FG, SUB), BF),
            pltpu.VMEM((parts, 2 * EO + 16, SUB), BF),
            pltpu.VMEM((D, FG), BF),
            pltpu.VMEM((NE * FH + 16, D), BF),
            pltpu.VMEM((D, 128), F32),
            pltpu.VMEM((NE * EO, FH), BF),
            pltpu.VMEM((FH, NE * EO), BF),
            pltpu.VMEM((2, FH, 128), F32),
            pltpu.VMEM((2, EO, 128), F32),
            pltpu.VMEM((16, 1), F32),
            pltpu.VMEM((2 * TW, 2 * EO), BF),
            pltpu.VMEM((2 * EO, 2 * TW), BF),
            pltpu.VMEM((2 * TW, 4), F32),
            pltpu.VMEM((chunks, fs, UC - QA), F32),
            pltpu.VMEM((D, XR), F32),
            pltpu.VMEM((D + 16, FG), F32),
            pltpu.VMEM((FH + 16, NE * EO), F32),
            pltpu.VMEM((2 * EO + 16, 2 * TW), F32),
            pltpu.VMEM((2 * TW, 128), F32),
            pltpu.VMEM((16, 128), F32),
            pltpu.VMEM((FH, 128), F32),
            pltpu.VMEM((*sizes_shape, 128), F32),
            pltpu.VMEM((1, half), F32),
        ],
    )
    return pl.pallas_call(
        functools.partial(main_kernel, pieces, chunks, rows // sizes_shape[0]),
        grid_spec=spec,
        out_shape=[jax.ShapeDtypeStruct((D, half), BF), jax.ShapeDtypeStruct((D, XR), BF)]
        + [jax.ShapeDtypeStruct(a, BF) for a in grads],
        compiler_params=pltpu.CompilerParams(vmem_limit_bytes=48 * 1024 * 1024),
        cost_estimate=pl.CostEstimate(flops=50_000_000_000, bytes_accessed=24_000_000, transcendentals=0),
        name="experts",
    )(table, embt, denset, line, far_line, *own_u, *far_u)


def input_kernel(tab_ref, hg_ref, wat_ref, *refs):
    eg_ref, dg_ref, done_ref, wa_s = refs[-4:]

    @pl.when(pl.program_id(0) == 0)
    def _():
        wa_s[...] = wat_ref[...].astype(F32).T.astype(BF)
        done_ref[...] = jnp.zeros_like(done_ref)

    eg = mm(wa_s[...], hg_ref[...])
    eg_ref[...] = eg[0:EMB]
    dg_ref[...] = eg[EMB : EMB + DENSE]


def input_call(table, hg, wat, token, other, name):
    half = hg.shape[1]
    tile = TILE
    steps = half // tile

    def place(i, c):
        return (0, (c[0] if other is None else 1 - c[0]) * steps + i)

    extra = [token] + (list(other) if other is not None else [])
    spec = pltpu.PrefetchScalarGridSpec(
        num_scalar_prefetch=1,
        grid=(steps,),
        in_specs=[pl.BlockSpec((D, tile), lambda i, c: (0, i)), pl.BlockSpec((D, XR), const2, pipeline_mode=pl.Buffered(1))]
        + [whole(pl.ANY) for _ in extra],
        out_specs=[pl.BlockSpec((EMB, tile), place), pl.BlockSpec((DENSE, tile), place), pl.BlockSpec((8, 128), const2)],
        scratch_shapes=[pltpu.VMEM((XR, D), BF)],
    )
    return pl.pallas_call(
        input_kernel,
        grid_spec=spec,
        out_shape=[jax.ShapeDtypeStruct((EMB, 2 * half), F32), jax.ShapeDtypeStruct((DENSE, 2 * half), F32), jax.ShapeDtypeStruct((8, 128), F32)],
        input_output_aliases={} if other is None else {4: 0, 5: 1},
        compiler_params=pltpu.CompilerParams(vmem_limit_bytes=32 * 1024 * 1024),
        cost_estimate=pl.CostEstimate(flops=4_000_000_000, bytes_accessed=9_000_000, transcendentals=0),
        name=name,
    )(table, hg, wat, *extra)


def widen(a):
    return jnp.concatenate([a.astype(F32), jnp.zeros((a.shape[0], 128 - a.shape[1]), F32)], axis=1)


def square(rows):
    count = sum(a.shape[0] for a in rows)
    return jnp.concatenate(rows + [jnp.zeros((128 - count, 128), F32)], axis=0)


def pack_kernel(core_ref, emb_ref, dense_ref, bias_ref, w1_ref, w2_ref, b1_ref, b2_ref, gate_ref, tower_ref, *refs):
    sizes_ref, label_ref, u_ref, line_ref = refs[4:]
    rows = label_ref.shape[1]
    line_ref[:, 0:rows] = label_ref[...].astype(F32)
    for j in range(4):
        line_ref[:, rows + 128 * j : rows + 128 * j + 128] = widen(refs[j][...])
    users = sizes_ref.shape[1]
    for b in range(sizes_ref.shape[0]):
        line_ref[:, rows + 512 + users * b : rows + 512 + users * b + users] = sizes_ref[b : b + 1, :].astype(F32)
    fs = u_ref.shape[0] // 2
    turned = square([widen(r[...]) for r in (b1_ref, b2_ref, gate_ref, dense_ref, bias_ref)]).T
    lane = lax.broadcasted_iota(jnp.int32, (fs, 128), 1)
    low, high = turned[0:fs], turned[fs : 2 * fs]
    small = jnp.concatenate([widen(tower_ref[...]), jnp.zeros((fs - tower_ref.shape[0], 128), F32)], axis=0)
    small += jnp.where((lane >= TW) & (lane < TW + HALF), pltpu.roll(low, TW - HALF, 1), 0.0)
    small += jnp.where(((lane >= B1) & (lane < B1 + HALF)) | ((lane >= GA) & (lane < GA + NE)), pltpu.roll(low, B1, 1), 0.0)
    small += jnp.where((lane >= GA + NE) & (lane < GA + 2 * NE), pltpu.roll(high, GA, 1), 0.0)
    for k in range(HALF):
        u_ref[:, FH * k : FH * k + FH] = w1_ref[k]
        u_ref[0:fs, QA + EO * k : QA + EO * k + EO] = w2_ref[k]
    u_ref[0:fs, QS:UC] = small.astype(BF)
    second_core = core_ref[0] == 1
    lanes = lax.broadcasted_iota(jnp.int32, (2 * fs, 128), 1)
    last = widen(emb_ref[:, 384:EMB]) + jnp.where((lanes >= 32) & (lanes < 33 + DENSE), pltpu.roll(turned[0 : 2 * fs], 16, 1), 0.0)
    for c in range(3):
        block = emb_ref[:, 128 * c : 128 * c + 128]
        u_ref[fs:, QA + 128 * c : QA + 128 * c + 128] = jnp.where(second_core, block[fs:], block[0:fs])
    u_ref[fs:, QA + 384 : QA + 512] = jnp.where(second_core, last[fs:], last[0:fs]).astype(BF)
    u_ref[fs:, QA + 512 : UC] = jnp.zeros((fs, UC - QA - 512), BF)


def whole(memory=pltpu.VMEM):
    return pl.BlockSpec(memory_space=memory)


def pack_call(core, *parts):
    ds = parts[3].shape[1]
    return pl.pallas_call(
        pack_kernel,
        in_specs=[whole(pltpu.SMEM)] + [whole() for _ in parts],
        out_specs=[whole(), whole()],
        out_shape=[jax.ShapeDtypeStruct((ds, UC), BF), jax.ShapeDtypeStruct((1, parts[-1].shape[1] + 512 + parts[-2].size), F32)],
        name="pack",
    )(core, *parts)


def sum_kernel(groups, count, *refs):
    ins, outs = refs[:count], refs[-len(groups) :]
    for group, out in zip(groups, outs):
        total = None
        for number, at in group:
            term = ins[number][at].astype(F32)
            total = term if total is None else total + term
        out[...] = total.astype(out.dtype)


def sum_call(name, arrays, groups, shapes, token=None, through=None):
    extra = [a for a in (token, through) if a is not None]
    lead = [] if through is None else [through]
    return pl.pallas_call(
        functools.partial(sum_kernel, groups, len(arrays)),
        in_specs=[whole() for _ in arrays] + [whole(pl.ANY) for _ in extra],
        out_specs=[whole(pl.ANY) for _ in lead] + [whole() for _ in shapes],
        out_shape=[jax.ShapeDtypeStruct(a.shape, a.dtype) for a in lead] + [jax.ShapeDtypeStruct(a, BF) for a in shapes],
        input_output_aliases={len(arrays) + len(extra) - 1: 0} if lead else {},
        compiler_params=pltpu.CompilerParams(vmem_limit_bytes=16 * 1024 * 1024),
        name=name,
    )(*arrays, *extra)


def finish_kernel(scale, core_ref, token_ref, *refs):
    total = sum(r[...].astype(F32) for r in refs[:4]) * scale
    ds = total.shape[0]
    fs = ds // 2
    own_part = total[fs:, QA : QA + XR]
    far_part = sum(r[...].astype(F32) for r in refs[4:8])[:, 0:XR] * scale
    second_core = core_ref[0] == 1
    ta = jnp.concatenate([jnp.where(second_core, far_part, own_part), jnp.where(second_core, own_part, far_part)], axis=0)
    emb_ref, dense_ref, bias_ref, w1_ref, b1_ref, w2_ref, b2_ref, gate_ref, gb_ref, tower_ref, t1_ref, t2_ref, t3_ref = refs[8:]
    osz = tower_ref.shape[0]
    for k in range(HALF):
        w1_ref[k] = total[:, FH * k : FH * k + FH]
        w2_ref[k] = total[0:fs, QA + EO * k : QA + EO * k + EO]
    small = total[0:fs, QS:UC]
    turned = square([small]).T
    b1_ref[...] = turned[B1 : B1 + HALF, 0:fs]
    b2_ref[...] = turned[TW : TW + HALF, 0:osz]
    gates = turned[GA : GA + NE] + pltpu.roll(turned[GA + NE : GA + 2 * NE], fs, 1)
    gate_ref[...] = gates[:, 0 : 2 * fs]
    tower_ref[...] = small[0:osz, 0:TW]
    t1_ref[...] = small[osz : osz + 1, 0:TW]
    t2_ref[...] = small[osz + 1 : osz + 2, 0:TW]
    gb_ref[...] = small[osz + 2 : osz + 3, 0:NE]
    t3_ref[...] = small[osz + 2 : osz + 3, NE : NE + 1]
    emb_ref[...] = ta[:, 0:EMB]
    last = square([widen(ta[:, 384:XR])]).T
    dense_ref[...] = last[32 : 32 + DENSE, 0 : 2 * fs]
    bias_ref[...] = last[32 + DENSE : 33 + DENSE, 0 : 2 * fs]


def finish_call(scale, core, token, arrays, ds, fs, osz):
    shapes = [
        (ds, EMB), (DENSE, ds), (1, ds), (HALF, ds, FH), (HALF, fs), (HALF, fs, EO), (HALF, osz), (NE, ds), (1, NE),
        (osz, TW), (1, TW), (1, TW), (1, 1),
    ]
    return pl.pallas_call(
        functools.partial(finish_kernel, scale),
        in_specs=[whole(pltpu.SMEM), whole(pl.ANY)] + [whole() for _ in arrays],
        out_specs=[whole() for _ in shapes],
        out_shape=[jax.ShapeDtypeStruct(a, F32) for a in shapes],
        compiler_params=pltpu.CompilerParams(vmem_limit_bytes=8 * 1024 * 1024),
        name="finish",
    )(core, token, *arrays)


def hop(a, mask, size):
    return lax.ppermute(a, "rows", [(i, i ^ mask) for i in range(size)])


def cross(a, masks, size):
    pairs = [(2 * i + t, 2 * (i ^ masks[t]) + t) for i in range(size) for t in range(2)]
    return lax.ppermute(a, ("rows", "task"), pairs)


def partner(a):
    return lax.ppermute(a, "task", [(0, 1), (1, 0)])


def add_wide(a, b):
    return a.astype(F32) + b.astype(F32)


def halves(line, denset, core):
    rows = denset.shape[1]
    half = rows // 2
    own_line = jnp.concatenate([lax.dynamic_slice(line, (0, core * half), (1, half)), line[:, rows:]], axis=1)
    sent_line = jnp.concatenate([lax.dynamic_slice(line, (0, (1 - core) * half), (1, half)), line[:, rows : rows + 512]], axis=1)
    return own_line, partner(sent_line), lax.dynamic_slice(denset, (0, core * half), (DENSE, half))


def pad_to(a, rows, cols):
    return jnp.pad(a, ((0, rows - a.shape[0]), (0, cols - a.shape[1])))


def body(
    emb, dense, group_sizes, labels, w_emb, w_dense, b_in, expert_w1, expert_b1, expert_w2, expert_b2,
    gate_w, gate_b, tower_w1, tower_b1, tower_w2, tower_b2,
):
    size = lax.axis_size("rows")
    core = lax.axis_index("task")
    place = lax.axis_index("rows")
    user_count = group_sizes.shape[1] * group_sizes.shape[0] * size
    ds, fs, osz = D // size, FH // size, EO // size
    fast = size == 16
    smalls = (gate_b, tower_b1, tower_w2, tower_b2[None])

    if fast:
        one_core = core[None].astype(jnp.int32)
        gate_t = jnp.transpose(gate_w, (0, 2, 1))[0]
        shard, line = pack_call(
            one_core, w_emb.T, w_dense, b_in[None], expert_w1, expert_w2, expert_b1, expert_b2, gate_t, tower_w1[0], *smalls, group_sizes, labels
        )
        near = jnp.stack([shard] + [hop(shard, 4 * a, size) for a in range(1, 4)])
        own_line, far_line, own_dense = halves(line, dense.T, core)
        near, own_line, far_line, own_dense = lax.optimization_barrier((near, own_line, far_line, own_dense))
        once = cross(near, (1, 2), size)
        own_u = [near, once, cross(near, (2, 1), size), cross(once, (2, 1), size)]
        steps = jnp.arange(16, dtype=jnp.int32)
        order = place ^ (steps % 4 * 4 + steps // 4)
    else:
        gather = functools.partial(lax.all_gather, axis_name="rows", axis=0, tiled=True)
        proj = jnp.concatenate([w_emb.T, w_dense.T, b_in[:, None], jnp.zeros((ds, 82), BF)], axis=1)
        w1_all = gather(jnp.transpose(expert_w1, (1, 0, 2)).reshape(ds, QA))
        w2_all = gather(jnp.transpose(expert_w2, (1, 0, 2)).reshape(fs, HALF * EO))
        o_all = gather(jnp.concatenate([tower_w1[0], expert_b2.T], axis=1))
        b1_all, g_all, proj_all = gather(expert_b1.T), gather(gate_w[0]), gather(proj)
        small = jnp.concatenate([pad_to(o_all, FH, B1), pad_to(b1_all, FH, GA - B1), g_all[0:FH], g_all[FH:], jnp.zeros((FH, 32), BF)], axis=1)
        part = jnp.where(core == 0, proj_all[0:FH], proj_all[FH:])
        lower = jnp.concatenate([part, jnp.zeros((FH, UC - QA - 512), BF)], axis=1)
        own_u = [jnp.concatenate([w1_all, jnp.concatenate([jnp.concatenate([w2_all, small], axis=1), lower], axis=0)], axis=1)[None]]
        order = jnp.zeros((1,), jnp.int32)
        line = [labels.astype(F32)] + [pad_to(a, 1, 128).astype(F32) for a in smalls]
        line = jnp.concatenate(line + [group_sizes.astype(F32).reshape(1, -1)], axis=1)
        own_line, far_line, own_dense = halves(line, dense.T, core)
    far_u = [partner(a) for a in own_u]
    table = jnp.concatenate([core[None].astype(jnp.int32), order])

    hg, wat, own_low, own_high, du_low, du_high = main_call(table, emb.T, own_dense, own_line, far_line, group_sizes.shape, own_u, far_u)
    du_high = partner(du_high)
    scale = 1.0 / user_count
    if fast:
        hg, part = sum_call("sum_cores", [own_high, du_high], [[(0, slice(0, 8)), (1, slice(0, 8))]], [(8, ds, UC)], through=hg)
        got = cross(part, (2, 1), size)
        du_low, far_hg = partner(du_low), partner(hg)
        eg, dg, token = input_call(table, hg, wat, part, None, "input_own")
        groups = [[(j, slice(4 * b, 4 * b + 4)) for j in range(3)] for b in (1, 0)]
        part, rest = sum_call("sum_first", [own_low, du_low, got], groups, [(4, ds, UC)] * 2, token)
        got = cross(part, (1, 2), size)
        eg, dg, token = input_call(table, far_hg, wat, part, (eg, dg), "input_far")
        sums = sum_call("sum_second", [rest, got], [[(0, k), (1, k)] for k in range(4)], [(ds, UC)] * 4, token)
        parts = [sums[0]] + [hop(sums[a], 4 * a, size) for a in range(1, 4)]
        parts += [partner(a[fs:, QA : QA + 512]) for a in parts]
        out = finish_call(scale, one_core, sums[0], parts, ds, fs, osz)
        g_emb, g_dense, g_bias, g_w1, g_b1, g_w2, g_b2, g_gate, g_gb, g_tower, g_t1, g_t2, g_t3 = out
        return (
            eg.T, dg.T, g_emb.T, g_dense, g_bias[0], g_w1, g_b1, g_w2, g_b2, g_gate.T[None], g_gb, g_tower[None], g_t1, g_t2, g_t3[0],
        )
    eg, dg, token = input_call(table, hg, wat, du_high, None, "input_own")
    eg, dg, _ = input_call(table, partner(hg), wat, token, (eg, dg), "input_far")
    scatter = functools.partial(lax.psum_scatter, axis_name="rows", scatter_dimension=0, tiled=True)
    wide = add_wide(own_low[0], partner(du_low)[0])
    upper, near = wide[0:FH, QA:UC], wide[FH:, QA : QA + XR]
    far, small = partner(near), upper[:, HALF * EO :]
    ta = scatter(jnp.concatenate([jnp.where(core == 0, near, far), jnp.where(core == 0, far, near)], axis=0)) * scale
    tp = jnp.transpose((scatter(wide[:, 0:QA]) * scale).reshape(ds, HALF, FH), (1, 0, 2))
    tw2, to, tb1 = scatter(upper[:, 0 : HALF * EO]) * scale, scatter(small[0:EO, 0:B1]) * scale, scatter(small[:, B1 : B1 + HALF]) * scale
    tg = scatter(jnp.concatenate([small[:, GA : GA + NE], small[:, GA + NE : GA + 2 * NE]], axis=0)) * scale
    ts = lax.psum(small[EO : EO + 3], "rows") * scale
    return (
        eg.T,
        dg.T,
        ta[:, 0:EMB].T,
        ta[:, EMB : EMB + DENSE].T,
        ta[:, EMB + DENSE],
        tp,
        tb1.T,
        jnp.transpose(tw2.reshape(fs, HALF, EO), (1, 0, 2)),
        to[:, TW : TW + HALF].T,
        tg[None],
        ts[2:3, 0:NE],
        to[:, 0:TW][None],
        ts[0:1, 0:TW],
        ts[1:2, 0:TW],
        ts[2, NE : NE + 1],
    )


def solution(mesh):
    in_specs = (
        P("rows", None),
        P("rows", None),
        P("rows", None),
        P("task", "rows"),
        P(None, "rows"),
        P(None, "rows"),
        P("rows"),
        P("task", "rows", None),
        P("task", "rows"),
        P("task", "rows", None),
        P("task", "rows"),
        P("task", "rows", None),
        P("task", None),
        P("task", "rows", None),
        P("task", None),
        P("task", None),
        P("task"),
    )
    out_specs = (
        P("rows", None),
        P("rows", None),
        P(None, "rows"),
        P(None, "rows"),
        P("rows"),
        P("task", "rows", None),
        P("task", "rows"),
        P("task", "rows", None),
        P("task", "rows"),
        P("task", "rows", None),
        P("task", None),
        P("task", "rows", None),
        P("task", None),
        P("task", None),
        P("task"),
    )
    return jax.shard_map(body, mesh=mesh, in_specs=in_specs, out_specs=out_specs, check_vma=False)
```

```python
import functools

import jax
import jax.numpy as jnp
from jax import lax
from jax.experimental import pallas as pl
from jax.experimental.pallas import tpu as pltpu
from jax.sharding import PartitionSpec as P

F32 = jnp.float32
BF = jnp.bfloat16
NT = (((1,), (1,)), ((), ()))
D, FH, EO, TW, NE = 512, 256, 128, 64, 8
HALF = NE // 2
EMB, DENSE = 416, 13
XR = 448
QA = HALF * FH
QS = QA + HALF * EO
UC = QS + 128
B1, GA = 72, 80
FG = NE * FH + 128
TILE = 1024
SUB = 512


def mm(a, b):
    return jnp.dot(a, b, preferred_element_type=F32)


def mm_nt(a, b):
    return lax.dot_general(a, b, NT, preferred_element_type=F32)


def act_narrow(half):
    return act_pair(half.astype(BF))


def act_pair(half):
    t = jnp.tanh(half)
    q = 1.0 + t
    m = half * q
    return m, q + m * (1.0 - t)


def swap_halves(a, flag):
    return jnp.where(flag, jnp.concatenate([a[HALF:NE], a[0:HALF]], axis=0), a)


def lane_fold(a):
    total = a[:, 0:128]
    for c in range(1, a.shape[1] // 128):
        total = total + a[:, 128 * c : 128 * c + 128]
    return total


def chunk_at(n, chunks, flag):
    if chunks == 1 or n // 4 in (0, 3):
        return n
    return n + 4 * flag if n // 4 == 1 else n - 4 * flag


LAG = 4


def take_turns(chains, lag):
    going = [(chain, lag * j) for j, chain in enumerate(chains)]
    while going:
        left = []
        for chain, wait in going:
            if wait > 0:
                left.append((chain, wait - 1))
            elif next(chain, True) is None:
                left.append((chain, 0))
        going = left


def main_kernel(pieces, chunks, batch_rows, tab_ref, *refs):
    emb_ref, dense_ref, line_ref, far_line_ref = refs[:4]
    u_refs = (refs[4 : 4 + pieces], refs[4 + pieces : 4 + 2 * pieces])
    quarters = min(4, chunks)
    hg_ref, wat_s, *du_refs = refs[4 + 2 * pieces : 6 + 2 * pieces + 2 * quarters]
    (
        x_s, hid_s, mid_s, sl1_s, out_s, sl2_s, sg_s, fg_s, mix_s,
        w1_s, w1t_s, ga_s, w2t_s, w2_s, b1_s, b2_s, gb_s, tt_s, tw_s, tcol_s, q_s,
        dwa_s, dw1_s, dw2_s, dtw_s, dcol_s, dlog_s, dsm_s, start_s, row_s,
    ) = refs[6 + 2 * pieces + 2 * quarters :]
    n = SUB
    fs, osz, ds = FH // chunks, EO // chunks, D // chunks
    step = pl.program_id(0)
    core = tab_ref[0]
    second_core = core == 1

    @pl.when(step == 0)
    def _():
        row_number = lax.broadcasted_iota(jnp.int32, (32, n), 0)
        ones = jnp.where(lax.broadcasted_iota(jnp.int32, (16, n), 0) == 0, 1.0, 0.0).astype(BF)
        for h in range(TILE // SUB):
            x_s[h, EMB:XR, :] = jnp.where(row_number == DENSE, 1.0, 0.0).astype(BF)
            hid_s[h, D : D + 16, :] = ones
            for k in range(NE):
                mid_s[h, k, FH : FH + 16, :] = ones
            mix_s[h, 2 * EO : 2 * EO + 16, :] = ones
            fg_s[h, NE * FH + 16 : FG, :] = jnp.zeros((FG - NE * FH - 16, n), BF)
        for ref in (dwa_s, dw1_s, dw2_s, dtw_s, dcol_s, dlog_s):
            ref[...] = jnp.zeros_like(ref)
        users = start_s.shape[1]
        after = row_s.shape[1] + 512
        sizes = [line_ref[:, after + users * b : after + users * b + users] for b in range(start_s.shape[0])]
        fill_weights(core, batch_rows, jnp.concatenate(sizes, axis=0), start_s, row_s)
        gates = []
        for side in range(2):
            base = HALF * FH * side
            holder = core if side == 0 else 1 - core
            for c in range(chunks):
                ref, c_in = u_refs[side][c * pieces // chunks], c % (chunks // pieces)
                at = chunk_at(c, chunks, holder)
                to = pl.multiple_of(ds * at, ds)
                w1_s[pl.ds(to, ds), base : base + QA] = ref[c_in, :, 0:QA]
                q_s[tab_ref[1 + at]] = ref[c_in, 0:fs, QA:UC].astype(F32)
                small = ref[c_in, 0:fs, QS:UC].astype(F32)
                ga_s[pl.ds(to, fs), :] = small
                ga_s[pl.ds(pl.multiple_of(to + fs, fs), fs), :] = pltpu.roll(small, 128 - NE, 1)
                wat_s[pl.ds(pl.multiple_of(to + holder * fs, fs), fs), :] = ref[c_in, fs:ds, QA : QA + XR]
            for k in range(HALF):
                block = w1_s[:, base + FH * k : base + FH * k + FH]
                w1t_s[base + FH * k : base + FH * k + FH, :] = (block.astype(F32).T * 0.5).astype(BF)
            gates.append(swap_halves(ga_s[...].T[GA : GA + NE], second_core))
            cols = HALF * EO
            w2 = q_s[:, :, 0:cols].reshape(FH, cols) * 0.5
            w2_s[:, cols * side : cols * side + cols] = w2.astype(BF)
            w2t_s[cols * side : cols * side + cols, :] = w2.T.astype(BF)
            b1_s[side] = q_s[:, :, cols : cols + 128].reshape(FH, 128) * 0.5
            last = q_s[:, 0:osz, cols : cols + 128].reshape(EO, 128)
            b2_s[side] = last * 0.5
            tower = last[:, 0:TW]
            rest = jnp.zeros_like(tower)
            both = jnp.concatenate([tower, rest] if side == 0 else [rest, tower], axis=1)
            tw_s[EO * side : EO * side + EO, :] = both.astype(BF)
            tt_s[:, EO * side : EO * side + EO] = (both.T * 0.5).astype(BF)
        gates = jnp.concatenate(gates, axis=0)
        w1t_s[NE * FH : NE * FH + 16, :] = gates.astype(BF)
        pad = jnp.concatenate([gates, jnp.zeros((112, D), F32)], axis=0)
        w1_s[:, NE * FH : FG] = pad.T.astype(BF)
        half = row_s.shape[1]
        vecs = [square([r[:, half + 128 * j : half + 128 * j + 128] for j in range(4)]).T for r in (line_ref, far_line_ref)]
        gb_s[...] = jnp.concatenate([swap_halves(v[0:NE, 0:1], second_core) for v in vecs], axis=0)
        b1 = jnp.concatenate([v[0:TW, 1:2] for v in vecs], axis=0)
        head = jnp.concatenate([v[0:TW, 2:3] for v in vecs], axis=0)
        last = jnp.concatenate([v[0:1, 3:4] for v in vecs] * TW, axis=0)
        tcol_s[...] = jnp.concatenate([b1 * 0.5, head, head * 0.5, last], axis=1)

    def chain(h):
        at = slice(SUB * h, SUB * h + SUB)
        x_s[h, 0:EMB, :] = emb_ref[:, at]
        x_s[h, EMB : EMB + DENSE, :] = dense_ref[:, pl.ds(pl.multiple_of(step * TILE + SUB * h, SUB), SUB)]
        hid = mm(wat_s[...], x_s[h]).astype(BF)
        hid_s[h, 0:D, :] = hid
        yield
        logits = mm(w1t_s[NE * FH : NE * FH + 16, :], hid) + gb_s[...]
        probs = []
        for t in range(2):
            lt = logits[NE * t : NE * t + NE]
            e = jnp.exp(lt - jnp.max(lt, axis=0, keepdims=True))
            probs.append(e / jnp.sum(e, axis=0, keepdims=True))
        mix = [None, None]
        pend = None
        nxt = mm(w1t_s[0:FH, :], hid)
        yield
        for k in range(NE + 1):
            pre = nxt
            if k < NE - 1:
                nxt = mm(w1t_s[FH * (k + 1) : FH * (k + 2), :], hid)
            if k < NE:
                m, s = act_narrow(pre + b1_s[k // HALF, :, B1 + k % HALF : B1 + k % HALF + 1])
                mid_s[h, k, 0:FH, :] = m
                sl1_s[h, FH * k : FH * k + FH, :] = s
                pre2 = mm(w2t_s[EO * k : EO * k + EO, :], m)
            if pend is not None:
                j = k - 1
                o, s = act_narrow(pend + b2_s[j // HALF, :, TW + j % HALF : TW + j % HALF + 1])
                out_s[h, EO * j : EO * j + EO, :] = o
                sl2_s[h, EO * j : EO * j + EO, :] = s
                o = o.astype(F32)
                for t in range(2):
                    term = probs[t][j : j + 1, :] * o
                    mix[t] = term if j == 0 else mix[t] + term
            pend = pre2
            yield
        mix_s[h, 0:EO, :] = mix[0].astype(BF)
        mix_s[h, EO : 2 * EO, :] = mix[1].astype(BF)
        act, slope = act_pair(mm(tt_s[...], mix_s[h, 0 : 2 * EO, :]) + tcol_s[:, 0:1])
        weighted = act * tcol_s[:, 1:2]
        lgos = []
        for t in range(2):
            logit = jnp.sum(weighted[TW * t : TW * t + TW], axis=0, keepdims=True) + tcol_s[t : t + 1, 3:4]
            label = (line_ref, far_line_ref)[t][:, pl.ds(pl.multiple_of(step * TILE + SUB * h, SUB), SUB)]
            lgos.append(row_s[:, pl.ds(pl.multiple_of(step * TILE + SUB * h, SUB), SUB)] * (0.5 * jnp.tanh(0.5 * logit) + 0.5 - label))
        lgo = jnp.concatenate([jnp.broadcast_to(lgos[t], (TW, SUB)) for t in range(2)], axis=0)
        dcol_s[...] += lane_fold(lgo * act)
        dlog_s[...] += lane_fold(jnp.concatenate([jnp.broadcast_to(lgos[t], (8, SUB)) for t in range(2)], axis=0))
        tg = (lgo * (tcol_s[:, 2:3] * slope)).astype(BF)
        yield
        dtw_s[...] += mm_nt(mix_s[h], tg)
        mgh = mm(tw_s[...], tg) * 0.5
        yield
        pgs = [[], []]
        mgs = [None] * NE
        for k in range(NE + 2):
            if k < NE:
                o = out_s[h, EO * k : EO * k + EO, :]
                og = None
                for t in range(2):
                    mg = mgh[EO * t : EO * t + EO]
                    pgs[t].append(jnp.sum((o * mg.astype(BF)).astype(F32), axis=0, keepdims=True))
                    term = probs[t][k : k + 1, :] * mg
                    og = term if og is None else og + term
                sg = og.astype(BF) * sl2_s[h, EO * k : EO * k + EO, :]
                sg_s[h, EO * (k % 2) : EO * (k % 2) + EO, :] = sg
                mgs[k] = mm(w2_s[:, EO * k : EO * k + EO], sg)
            if 1 <= k < NE + 1:
                j = k - 1
                dw2_s[:, EO * j : EO * j + EO] += mm_nt(mid_s[h, j], sg_s[h, EO * (j % 2) : EO * (j % 2) + EO, :])
                fg = mgs[j].astype(BF) * sl1_s[h, FH * j : FH * j + FH, :]
                fg_s[h, FH * j : FH * j + FH, :] = fg
            if k >= 2:
                j = k - 2
                dw1_s[:, FH * j : FH * j + FH] += mm_nt(hid_s[h], fg_s[h, FH * j : FH * j + FH, :])
            yield
        lgs = []
        for t in range(2):
            pg = jnp.concatenate(pgs[t], axis=0)
            lgs.append(2.0 * probs[t] * (pg - jnp.sum(probs[t] * pg, axis=0, keepdims=True)))
        fg_s[h, NE * FH : NE * FH + 16, :] = jnp.concatenate(lgs, axis=0).astype(BF)
        yield
        dw1_s[:, NE * FH : FG] += mm_nt(hid_s[h], fg_s[h, NE * FH : FG, :])
        hg = mm(w1_s[...], fg_s[h]).astype(BF)
        hg_ref[:, at] = hg
        yield
        dwa_s[...] += mm_nt(hg, x_s[h])
        yield

    take_turns([chain(h) for h in range(TILE // SUB)], LAG)

    @pl.when(step == pl.num_programs(0) - 1)
    def _():
        gate = dw1_s[:, NE * FH : FG].T
        dlog = jnp.sum(dlog_s[...], axis=1, keepdims=True)
        dcol = jnp.sum(dcol_s[...].T, axis=0, keepdims=True)
        for side in range(2):
            own_gate = swap_halves(gate[NE * side : NE * side + NE], second_core)
            ga_s[...] = jnp.concatenate([own_gate[:, 0:D], jnp.zeros((120, D), F32)], axis=0).T
            b1 = [dw1_s[D : D + 1, FH * k : FH * k + FH] for k in range(HALF * side, HALF * side + HALF)]
            b1 = jnp.concatenate(b1 + [jnp.zeros((124, FH), F32)], axis=0).T
            b2 = [dw2_s[FH : FH + 1, EO * k : EO * k + EO] for k in range(HALF * side, HALF * side + HALF)]
            b2 = jnp.concatenate(b2 + [jnp.zeros((60, EO), F32)], axis=0).T
            tower = dtw_s[EO * side : EO * side + EO, TW * side : TW * side + TW]
            tower = jnp.concatenate([tower, b2], axis=1)
            lanes = slice(TW * side, TW * side + TW)
            blank = jnp.zeros((1, TW), F32)
            lines = [jnp.concatenate([a, blank], axis=1) for a in (dtw_s[2 * EO : 2 * EO + 1, lanes], dcol[:, lanes])]
            gate_b = jnp.sum(jnp.where(lax.broadcasted_iota(jnp.int32, (NE, D + 16), 1) == D, own_gate, 0.0), axis=1, keepdims=True)
            small = jnp.concatenate([gate_b, dlog[8 * side : 8 * side + 8]], axis=0)
            small = jnp.concatenate([jnp.broadcast_to(small, (16, 128)), jnp.zeros((112, 128), F32)], axis=0).T[0:1]
            tail = jnp.concatenate(lines + [small, jnp.zeros((fs - osz - 3, 128), F32)], axis=0)
            b1 = pltpu.roll(b1, B1, 1)
            for c in range(chunks):
                dsm_s[fs * c : fs * c + fs, :] = b1[fs * c : fs * c + fs] + jnp.concatenate([tower[osz * c : osz * c + osz], tail], axis=0)
            holder = core if side == 0 else 1 - core
            cols = HALF * EO
            for n in range(chunks):
                ref, c = du_refs[quarters * side + n * quarters // chunks], n % (chunks // quarters)
                at = chunk_at(n, chunks, holder)
                to = pl.multiple_of(ds * at, ds)
                where = pl.ds(pl.multiple_of(tab_ref[1 + at] * fs, fs), fs)
                ref[c, :, 0:QA] = dw1_s[pl.ds(to, ds), QA * side : QA * side + QA].astype(BF)
                ref[c, 0:fs, QA:QS] = dw2_s[where, cols * side : cols * side + cols].astype(BF)
                low = pltpu.roll(ga_s[pl.ds(to, fs), :], GA, 1)
                high = pltpu.roll(ga_s[pl.ds(pl.multiple_of(to + fs, fs), fs), :], GA + NE, 1)
                ref[c, 0:fs, QS:UC] = (dsm_s[where, :] + low + high).astype(BF)
                lower = dwa_s[pl.ds(pl.multiple_of(to + holder * fs, fs), fs), :]
                ref[c, fs:ds, QA:UC] = jnp.concatenate([lower, jnp.zeros((fs, UC - QA - XR), F32)], axis=1).astype(BF)


def fill_weights(core, batch_rows, sizes, start_s, out_ref):
    batches, users = sizes.shape
    counts = jnp.concatenate([sizes.astype(F32), jnp.zeros((16 - batches, users), F32)], axis=0)
    turned = jnp.concatenate([counts, jnp.zeros((112, users), F32)], axis=0).T
    before = lax.broadcasted_iota(jnp.int32, (users, users), 1) < lax.broadcasted_iota(jnp.int32, (users, users), 0)
    starts = mm(jnp.where(before, 1.0, 0.0).astype(BF), turned.astype(BF))
    for b in range(batches):
        start_s[b] = jnp.broadcast_to(starts[:, b : b + 1], (users, 128))
    first = lax.broadcasted_iota(jnp.int32, counts.shape, 1) == 0
    rises = counts - jnp.where(first, 0.0, pltpu.roll(counts, 1, 1))
    line = lax.broadcasted_iota(jnp.int32, counts.shape, 0)
    steps = out_ref.shape[1] // SUB
    for step in range(steps):
        at_step = core * steps + step
        batch = at_step // (batch_rows // SUB)
        first_row = (at_step % (batch_rows // SUB) * SUB).astype(F32)
        begins = start_s[batch]
        places = first_row + lax.broadcasted_iota(jnp.int32, (1, 128), 1).astype(F32)
        begun = [jnp.where(begins <= places + 128.0 * c, 1.0, 0.0).astype(BF) for c in range(SUB // 128)]
        rise = jnp.where(line == batch, rises, 0.0).astype(BF)
        size = jnp.sum(mm(rise, jnp.concatenate(begun, axis=1)), axis=0, keepdims=True)
        out_ref[:, SUB * step : SUB * step + SUB] = 1.0 / size


def const2(i, c):
    return (0, 0)


def main_call(table, embt, denset, line, far_line, sizes_shape, own_u, far_u):
    rows = embt.shape[1]
    half = rows // 2
    steps = half // TILE
    pieces = len(own_u)
    chunks = sum(a.shape[0] for a in own_u)
    fs, ds = FH // chunks, D // chunks

    def own(i, c):
        return (0, c[0] * steps + i)

    quarters = min(4, chunks)
    grads = [(chunks // quarters, ds, UC)] * (2 * quarters)
    parts = TILE // SUB
    spec = pltpu.PrefetchScalarGridSpec(
        num_scalar_prefetch=1,
        grid=(steps,),
        in_specs=[
            pl.BlockSpec((EMB, TILE), own),
            whole(),
            whole(),
            whole(),
        ]
        + [whole() for _ in (*own_u, *far_u)],
        out_specs=[pl.BlockSpec((D, TILE), lambda i, c: (0, i))] + [whole()] * (1 + 2 * quarters),
        scratch_shapes=[
            pltpu.VMEM((parts, XR, SUB), BF),
            pltpu.VMEM((parts, D + 16, SUB), BF),
            pltpu.VMEM((parts, NE, FH + 16, SUB), BF),
            pltpu.VMEM((parts, NE * FH, SUB), BF),
            pltpu.VMEM((parts, NE * EO, SUB), BF),
            pltpu.VMEM((parts, NE * EO, SUB), BF),
            pltpu.VMEM((parts, 2 * EO, SUB), BF),
            pltpu.VMEM((parts, FG, SUB), BF),
            pltpu.VMEM((parts, 2 * EO + 16, SUB), BF),
            pltpu.VMEM((D, FG), BF),
            pltpu.VMEM((NE * FH + 16, D), BF),
            pltpu.VMEM((D, 128), F32),
            pltpu.VMEM((NE * EO, FH), BF),
            pltpu.VMEM((FH, NE * EO), BF),
            pltpu.VMEM((2, FH, 128), F32),
            pltpu.VMEM((2, EO, 128), F32),
            pltpu.VMEM((16, 1), F32),
            pltpu.VMEM((2 * TW, 2 * EO), BF),
            pltpu.VMEM((2 * EO, 2 * TW), BF),
            pltpu.VMEM((2 * TW, 4), F32),
            pltpu.VMEM((chunks, fs, UC - QA), F32),
            pltpu.VMEM((D, XR), F32),
            pltpu.VMEM((D + 16, FG), F32),
            pltpu.VMEM((FH + 16, NE * EO), F32),
            pltpu.VMEM((2 * EO + 16, 2 * TW), F32),
            pltpu.VMEM((2 * TW, 128), F32),
            pltpu.VMEM((16, 128), F32),
            pltpu.VMEM((FH, 128), F32),
            pltpu.VMEM((*sizes_shape, 128), F32),
            pltpu.VMEM((1, half), F32),
        ],
    )
    return pl.pallas_call(
        functools.partial(main_kernel, pieces, chunks, rows // sizes_shape[0]),
        grid_spec=spec,
        out_shape=[jax.ShapeDtypeStruct((D, half), BF), jax.ShapeDtypeStruct((D, XR), BF)]
        + [jax.ShapeDtypeStruct(a, BF) for a in grads],
        compiler_params=pltpu.CompilerParams(vmem_limit_bytes=48 * 1024 * 1024),
        cost_estimate=pl.CostEstimate(flops=50_000_000_000, bytes_accessed=24_000_000, transcendentals=0),
        name="experts",
    )(table, embt, denset, line, far_line, *own_u, *far_u)


def input_kernel(tab_ref, hg_ref, wat_ref, *refs):
    eg_ref, dg_ref, done_ref, wa_s = refs[-4:]

    @pl.when(pl.program_id(0) == 0)
    def _():
        wa_s[...] = wat_ref[...].astype(F32).T.astype(BF)
        done_ref[...] = jnp.zeros_like(done_ref)

    eg = mm(wa_s[...], hg_ref[...])
    eg_ref[...] = eg[0:EMB]
    dg_ref[...] = eg[EMB : EMB + DENSE]


def input_call(table, hg, wat, token, other, name):
    half = hg.shape[1]
    tile = TILE
    steps = half // tile

    def place(i, c):
        return (0, (c[0] if other is None else 1 - c[0]) * steps + i)

    extra = [token] + (list(other) if other is not None else [])
    spec = pltpu.PrefetchScalarGridSpec(
        num_scalar_prefetch=1,
        grid=(steps,),
        in_specs=[pl.BlockSpec((D, tile), lambda i, c: (0, i)), pl.BlockSpec((D, XR), const2, pipeline_mode=pl.Buffered(1))]
        + [whole(pl.ANY) for _ in extra],
        out_specs=[pl.BlockSpec((EMB, tile), place), pl.BlockSpec((DENSE, tile), place), pl.BlockSpec((8, 128), const2)],
        scratch_shapes=[pltpu.VMEM((XR, D), BF)],
    )
    return pl.pallas_call(
        input_kernel,
        grid_spec=spec,
        out_shape=[jax.ShapeDtypeStruct((EMB, 2 * half), F32), jax.ShapeDtypeStruct((DENSE, 2 * half), F32), jax.ShapeDtypeStruct((8, 128), F32)],
        input_output_aliases={} if other is None else {4: 0, 5: 1},
        compiler_params=pltpu.CompilerParams(vmem_limit_bytes=32 * 1024 * 1024),
        cost_estimate=pl.CostEstimate(flops=4_000_000_000, bytes_accessed=9_000_000, transcendentals=0),
        name=name,
    )(table, hg, wat, *extra)


def widen(a):
    return jnp.concatenate([a.astype(F32), jnp.zeros((a.shape[0], 128 - a.shape[1]), F32)], axis=1)


def square(rows):
    count = sum(a.shape[0] for a in rows)
    return jnp.concatenate(rows + [jnp.zeros((128 - count, 128), F32)], axis=0)


def pack_kernel(core_ref, emb_ref, dense_ref, bias_ref, w1_ref, w2_ref, b1_ref, b2_ref, gate_ref, tower_ref, *refs):
    sizes_ref, label_ref, u_ref, line_ref = refs[4:]
    rows = label_ref.shape[1]
    line_ref[:, 0:rows] = label_ref[...].astype(F32)
    for j in range(4):
        line_ref[:, rows + 128 * j : rows + 128 * j + 128] = widen(refs[j][...])
    users = sizes_ref.shape[1]
    for b in range(sizes_ref.shape[0]):
        line_ref[:, rows + 512 + users * b : rows + 512 + users * b + users] = sizes_ref[b : b + 1, :].astype(F32)
    fs = u_ref.shape[0] // 2
    turned = square([widen(r[...]) for r in (b1_ref, b2_ref, gate_ref, dense_ref, bias_ref)]).T
    lane = lax.broadcasted_iota(jnp.int32, (fs, 128), 1)
    low, high = turned[0:fs], turned[fs : 2 * fs]
    small = jnp.concatenate([widen(tower_ref[...]), jnp.zeros((fs - tower_ref.shape[0], 128), F32)], axis=0)
    small += jnp.where((lane >= TW) & (lane < TW + HALF), pltpu.roll(low, TW - HALF, 1), 0.0)
    small += jnp.where(((lane >= B1) & (lane < B1 + HALF)) | ((lane >= GA) & (lane < GA + NE)), pltpu.roll(low, B1, 1), 0.0)
    small += jnp.where((lane >= GA + NE) & (lane < GA + 2 * NE), pltpu.roll(high, GA, 1), 0.0)
    for k in range(HALF):
        u_ref[:, FH * k : FH * k + FH] = w1_ref[k]
        u_ref[0:fs, QA + EO * k : QA + EO * k + EO] = w2_ref[k]
    u_ref[0:fs, QS:UC] = small.astype(BF)
    second_core = core_ref[0] == 1
    lanes = lax.broadcasted_iota(jnp.int32, (2 * fs, 128), 1)
    last = widen(emb_ref[:, 384:EMB]) + jnp.where((lanes >= 32) & (lanes < 33 + DENSE), pltpu.roll(turned[0 : 2 * fs], 16, 1), 0.0)
    for c in range(3):
        block = emb_ref[:, 128 * c : 128 * c + 128]
        u_ref[fs:, QA + 128 * c : QA + 128 * c + 128] = jnp.where(second_core, block[fs:], block[0:fs])
    u_ref[fs:, QA + 384 : QA + 512] = jnp.where(second_core, last[fs:], last[0:fs]).astype(BF)
    u_ref[fs:, QA + 512 : UC] = jnp.zeros((fs, UC - QA - 512), BF)


def whole(memory=pltpu.VMEM):
    return pl.BlockSpec(memory_space=memory)


def pack_call(core, *parts):
    ds = parts[3].shape[1]
    return pl.pallas_call(
        pack_kernel,
        in_specs=[whole(pltpu.SMEM)] + [whole() for _ in parts],
        out_specs=[whole(), whole()],
        out_shape=[jax.ShapeDtypeStruct((ds, UC), BF), jax.ShapeDtypeStruct((1, parts[-1].shape[1] + 512 + parts[-2].size), F32)],
        name="pack",
    )(core, *parts)


def sum_kernel(groups, count, *refs):
    ins, outs = refs[:count], refs[-len(groups) :]
    for group, out in zip(groups, outs):
        total = None
        for number, at in group:
            term = ins[number][at].astype(F32)
            total = term if total is None else total + term
        out[...] = total.astype(out.dtype)


def sum_call(name, arrays, groups, shapes, token=None, through=None):
    extra = [a for a in (token, through) if a is not None]
    lead = [] if through is None else [through]
    return pl.pallas_call(
        functools.partial(sum_kernel, groups, len(arrays)),
        in_specs=[whole() for _ in arrays] + [whole(pl.ANY) for _ in extra],
        out_specs=[whole(pl.ANY) for _ in lead] + [whole() for _ in shapes],
        out_shape=[jax.ShapeDtypeStruct(a.shape, a.dtype) for a in lead] + [jax.ShapeDtypeStruct(a, BF) for a in shapes],
        input_output_aliases={len(arrays) + len(extra) - 1: 0} if lead else {},
        compiler_params=pltpu.CompilerParams(vmem_limit_bytes=16 * 1024 * 1024),
        name=name,
    )(*arrays, *extra)


def finish_kernel(scale, core_ref, token_ref, *refs):
    total = sum(r[...].astype(F32) for r in refs[:4]) * scale
    ds = total.shape[0]
    fs = ds // 2
    own_part = total[fs:, QA : QA + XR]
    far_part = sum(r[...].astype(F32) for r in refs[4:8])[:, 0:XR] * scale
    second_core = core_ref[0] == 1
    ta = jnp.concatenate([jnp.where(second_core, far_part, own_part), jnp.where(second_core, own_part, far_part)], axis=0)
    emb_ref, dense_ref, bias_ref, w1_ref, b1_ref, w2_ref, b2_ref, gate_ref, gb_ref, tower_ref, t1_ref, t2_ref, t3_ref = refs[8:]
    osz = tower_ref.shape[0]
    for k in range(HALF):
        w1_ref[k] = total[:, FH * k : FH * k + FH]
        w2_ref[k] = total[0:fs, QA + EO * k : QA + EO * k + EO]
    small = total[0:fs, QS:UC]
    turned = square([small]).T
    b1_ref[...] = turned[B1 : B1 + HALF, 0:fs]
    b2_ref[...] = turned[TW : TW + HALF, 0:osz]
    gates = turned[GA : GA + NE] + pltpu.roll(turned[GA + NE : GA + 2 * NE], fs, 1)
    gate_ref[...] = gates[:, 0 : 2 * fs]
    tower_ref[...] = small[0:osz, 0:TW]
    t1_ref[...] = small[osz : osz + 1, 0:TW]
    t2_ref[...] = small[osz + 1 : osz + 2, 0:TW]
    gb_ref[...] = small[osz + 2 : osz + 3, 0:NE]
    t3_ref[...] = small[osz + 2 : osz + 3, NE : NE + 1]
    emb_ref[...] = ta[:, 0:EMB]
    last = square([widen(ta[:, 384:XR])]).T
    dense_ref[...] = last[32 : 32 + DENSE, 0 : 2 * fs]
    bias_ref[...] = last[32 + DENSE : 33 + DENSE, 0 : 2 * fs]


def finish_call(scale, core, token, arrays, ds, fs, osz):
    shapes = [
        (ds, EMB), (DENSE, ds), (1, ds), (HALF, ds, FH), (HALF, fs), (HALF, fs, EO), (HALF, osz), (NE, ds), (1, NE),
        (osz, TW), (1, TW), (1, TW), (1, 1),
    ]
    return pl.pallas_call(
        functools.partial(finish_kernel, scale),
        in_specs=[whole(pltpu.SMEM), whole(pl.ANY)] + [whole() for _ in arrays],
        out_specs=[whole() for _ in shapes],
        out_shape=[jax.ShapeDtypeStruct(a, F32) for a in shapes],
        compiler_params=pltpu.CompilerParams(vmem_limit_bytes=8 * 1024 * 1024),
        name="finish",
    )(core, token, *arrays)


def hop(a, mask, size):
    return lax.ppermute(a, "rows", [(i, i ^ mask) for i in range(size)])


def cross(a, masks, size):
    pairs = [(2 * i + t, 2 * (i ^ masks[t]) + t) for i in range(size) for t in range(2)]
    return lax.ppermute(a, ("rows", "task"), pairs)


def partner(a):
    return lax.ppermute(a, "task", [(0, 1), (1, 0)])


def add_wide(a, b):
    return a.astype(F32) + b.astype(F32)


def halves(line, denset, core):
    rows = denset.shape[1]
    half = rows // 2
    own_line = jnp.concatenate([lax.dynamic_slice(line, (0, core * half), (1, half)), line[:, rows:]], axis=1)
    sent_line = jnp.concatenate([lax.dynamic_slice(line, (0, (1 - core) * half), (1, half)), line[:, rows : rows + 512]], axis=1)
    return own_line, partner(sent_line), lax.dynamic_slice(denset, (0, core * half), (DENSE, half))


def pad_to(a, rows, cols):
    return jnp.pad(a, ((0, rows - a.shape[0]), (0, cols - a.shape[1])))


def body(
    emb, dense, group_sizes, labels, w_emb, w_dense, b_in, expert_w1, expert_b1, expert_w2, expert_b2,
    gate_w, gate_b, tower_w1, tower_b1, tower_w2, tower_b2,
):
    size = lax.axis_size("rows")
    core = lax.axis_index("task")
    place = lax.axis_index("rows")
    user_count = group_sizes.shape[1] * group_sizes.shape[0] * size
    ds, fs, osz = D // size, FH // size, EO // size
    fast = size == 16
    smalls = (gate_b, tower_b1, tower_w2, tower_b2[None])

    if fast:
        one_core = core[None].astype(jnp.int32)
        gate_t = jnp.transpose(gate_w, (0, 2, 1))[0]
        shard, line = pack_call(
            one_core, w_emb.T, w_dense, b_in[None], expert_w1, expert_w2, expert_b1, expert_b2, gate_t, tower_w1[0], *smalls, group_sizes, labels
        )
        near = jnp.stack([shard] + [hop(shard, 4 * a, size) for a in range(1, 4)])
        own_line, far_line, own_dense = halves(line, dense.T, core)
        near, own_line, far_line, own_dense = lax.optimization_barrier((near, own_line, far_line, own_dense))
        once = cross(near, (1, 2), size)
        own_u = [near, once, cross(near, (2, 1), size), cross(once, (2, 1), size)]
        steps = jnp.arange(16, dtype=jnp.int32)
        order = place ^ (steps % 4 * 4 + steps // 4)
    else:
        gather = functools.partial(lax.all_gather, axis_name="rows", axis=0, tiled=True)
        proj = jnp.concatenate([w_emb.T, w_dense.T, b_in[:, None], jnp.zeros((ds, 82), BF)], axis=1)
        w1_all = gather(jnp.transpose(expert_w1, (1, 0, 2)).reshape(ds, QA))
        w2_all = gather(jnp.transpose(expert_w2, (1, 0, 2)).reshape(fs, HALF * EO))
        o_all = gather(jnp.concatenate([tower_w1[0], expert_b2.T], axis=1))
        b1_all, g_all, proj_all = gather(expert_b1.T), gather(gate_w[0]), gather(proj)
        small = jnp.concatenate([pad_to(o_all, FH, B1), pad_to(b1_all, FH, GA - B1), g_all[0:FH], g_all[FH:], jnp.zeros((FH, 32), BF)], axis=1)
        part = jnp.where(core == 0, proj_all[0:FH], proj_all[FH:])
        lower = jnp.concatenate([part, jnp.zeros((FH, UC - QA - 512), BF)], axis=1)
        own_u = [jnp.concatenate([w1_all, jnp.concatenate([jnp.concatenate([w2_all, small], axis=1), lower], axis=0)], axis=1)[None]]
        order = jnp.zeros((1,), jnp.int32)
        line = [labels.astype(F32)] + [pad_to(a, 1, 128).astype(F32) for a in smalls]
        line = jnp.concatenate(line + [group_sizes.astype(F32).reshape(1, -1)], axis=1)
        own_line, far_line, own_dense = halves(line, dense.T, core)
    far_u = [partner(a) for a in own_u]
    table = jnp.concatenate([core[None].astype(jnp.int32), order])

    hg, wat, *grads = main_call(table, emb.T, own_dense, own_line, far_line, group_sizes.shape, own_u, far_u)
    own, far = grads[: len(grads) // 2], grads[len(grads) // 2 :]
    scale = 1.0 / user_count
    if fast:
        quarter, every = (4, ds, UC), slice(0, 4)
        (third,) = sum_call("sum_fourth", [own[3], partner(far[3])], [[(0, every), (1, every)]], [quarter])
        got_third = cross(third, (2, 1), size)
        hg, second = sum_call("sum_third", [own[2], partner(far[2])], [[(0, every), (1, every)]], [quarter], third, hg)
        got_second = cross(second, (2, 1), size)
        far_first, far_hg = partner(far[1]), partner(hg)
        eg, dg, token = input_call(table, hg, wat, second, None, "input_own")
        (first,) = sum_call("sum_second", [own[1], far_first, got_third], [[(j, every) for j in range(3)]], [quarter], token)
        got_first = cross(first, (1, 2), size)
        far_none = partner(far[0])
        eg, dg, token = input_call(table, far_hg, wat, first, (eg, dg), "input_far")
        groups = [[(j, k) for j in range(4)] for k in range(4)]
        sums = sum_call("sum_first", [own[0], far_none, got_second, got_first], groups, [(ds, UC)] * 4, token)
        parts = [sums[0]] + [hop(sums[a], 4 * a, size) for a in range(1, 4)]
        parts += [partner(a[fs:, QA : QA + 512]) for a in parts]
        out = finish_call(scale, one_core, sums[0], parts, ds, fs, osz)
        g_emb, g_dense, g_bias, g_w1, g_b1, g_w2, g_b2, g_gate, g_gb, g_tower, g_t1, g_t2, g_t3 = out
        return (
            eg.T, dg.T, g_emb.T, g_dense, g_bias[0], g_w1, g_b1, g_w2, g_b2, g_gate.T[None], g_gb, g_tower[None], g_t1, g_t2, g_t3[0],
        )
    eg, dg, token = input_call(table, hg, wat, far[0], None, "input_own")
    eg, dg, _ = input_call(table, partner(hg), wat, token, (eg, dg), "input_far")
    scatter = functools.partial(lax.psum_scatter, axis_name="rows", scatter_dimension=0, tiled=True)
    wide = add_wide(own[0][0], partner(far[0])[0])
    upper, near = wide[0:FH, QA:UC], wide[FH:, QA : QA + XR]
    far, small = partner(near), upper[:, HALF * EO :]
    ta = scatter(jnp.concatenate([jnp.where(core == 0, near, far), jnp.where(core == 0, far, near)], axis=0)) * scale
    tp = jnp.transpose((scatter(wide[:, 0:QA]) * scale).reshape(ds, HALF, FH), (1, 0, 2))
    tw2, to, tb1 = scatter(upper[:, 0 : HALF * EO]) * scale, scatter(small[0:EO, 0:B1]) * scale, scatter(small[:, B1 : B1 + HALF]) * scale
    tg = scatter(jnp.concatenate([small[:, GA : GA + NE], small[:, GA + NE : GA + 2 * NE]], axis=0)) * scale
    ts = lax.psum(small[EO : EO + 3], "rows") * scale
    return (
        eg.T,
        dg.T,
        ta[:, 0:EMB].T,
        ta[:, EMB : EMB + DENSE].T,
        ta[:, EMB + DENSE],
        tp,
        tb1.T,
        jnp.transpose(tw2.reshape(fs, HALF, EO), (1, 0, 2)),
        to[:, TW : TW + HALF].T,
        tg[None],
        ts[2:3, 0:NE],
        to[:, 0:TW][None],
        ts[0:1, 0:TW],
        ts[1:2, 0:TW],
        ts[2, NE : NE + 1],
    )


def solution(mesh):
    in_specs = (
        P("rows", None),
        P("rows", None),
        P("rows", None),
        P("task", "rows"),
        P(None, "rows"),
        P(None, "rows"),
        P("rows"),
        P("task", "rows", None),
        P("task", "rows"),
        P("task", "rows", None),
        P("task", "rows"),
        P("task", "rows", None),
        P("task", None),
        P("task", "rows", None),
        P("task", None),
        P("task", None),
        P("task"),
    )
    out_specs = (
        P("rows", None),
        P("rows", None),
        P(None, "rows"),
        P(None, "rows"),
        P("rows"),
        P("task", "rows", None),
        P("task", "rows"),
        P("task", "rows", None),
        P("task", "rows"),
        P("task", "rows", None),
        P("task", None),
        P("task", "rows", None),
        P("task", None),
        P("task", None),
        P("task"),
    )
    return jax.shard_map(body, mesh=mesh, in_specs=in_specs, out_specs=out_specs, check_vma=False)
```

```python
import functools

import jax
import jax.numpy as jnp
from jax import lax
from jax.experimental import pallas as pl
from jax.experimental.pallas import tpu as pltpu
from jax.sharding import PartitionSpec as P

F32 = jnp.float32
BF = jnp.bfloat16
NT = (((1,), (1,)), ((), ()))
D, FH, EO, TW, NE = 512, 256, 128, 64, 8
HALF = NE // 2
EMB, DENSE = 416, 13
XR = 448
QA = HALF * FH
QS = QA + HALF * EO
UC = QS + 128
B1, GA = 72, 80
FG = NE * FH + 128
TILE = 1024
SUB = 512


def mm(a, b):
    return jnp.dot(a, b, preferred_element_type=F32)


def mm_nt(a, b):
    return lax.dot_general(a, b, NT, preferred_element_type=F32)


def act_narrow(half):
    return act_pair(half.astype(BF))


def act_pair(half):
    t = jnp.tanh(half)
    q = 1.0 + t
    m = half * q
    return m, q + m * (1.0 - t)


def swap_halves(a, flag):
    return jnp.where(flag, jnp.concatenate([a[HALF:NE], a[0:HALF]], axis=0), a)


def lane_fold(a):
    total = a[:, 0:128]
    for c in range(1, a.shape[1] // 128):
        total = total + a[:, 128 * c : 128 * c + 128]
    return total


def chunk_at(n, chunks, flag):
    if chunks == 1 or n // 4 in (0, 3):
        return n
    return n + 4 * flag if n // 4 == 1 else n - 4 * flag


LAG = 4


def take_turns(chains, lag):
    going = [(chain, lag * j) for j, chain in enumerate(chains)]
    while going:
        left = []
        for chain, wait in going:
            if wait > 0:
                left.append((chain, wait - 1))
            elif next(chain, True) is None:
                left.append((chain, 0))
        going = left


def main_kernel(pieces, chunks, batch_rows, tab_ref, *refs):
    emb_ref, dense_ref, line_ref, far_line_ref = refs[:4]
    u_refs = (refs[4 : 4 + pieces], refs[4 + pieces : 4 + 2 * pieces])
    quarters = min(4, chunks)
    hg_ref, wat_s, *du_refs = refs[4 + 2 * pieces : 6 + 2 * pieces + 2 * quarters]
    (
        x_s, hid_s, mid_s, sl1_s, out_s, sl2_s, sg_s, fg_s, mix_s,
        w1_s, w1t_s, ga_s, w2t_s, w2_s, b1_s, b2_s, gb_s, tt_s, tw_s, tcol_s, q_s,
        dwa_s, dw1_s, dw2_s, dtw_s, dcol_s, dlog_s, dsm_s, start_s, row_s,
    ) = refs[6 + 2 * pieces + 2 * quarters :]
    n = SUB
    fs, osz, ds = FH // chunks, EO // chunks, D // chunks
    step = pl.program_id(0)
    core = tab_ref[0]
    second_core = core == 1

    @pl.when(step == 0)
    def _():
        row_number = lax.broadcasted_iota(jnp.int32, (32, n), 0)
        ones = jnp.where(lax.broadcasted_iota(jnp.int32, (16, n), 0) == 0, 1.0, 0.0).astype(BF)
        for h in range(TILE // SUB):
            x_s[h, EMB:XR, :] = jnp.where(row_number == DENSE, 1.0, 0.0).astype(BF)
            hid_s[h, D : D + 16, :] = ones
            for k in range(NE):
                mid_s[h, k, FH : FH + 16, :] = ones
            mix_s[h, 2 * EO : 2 * EO + 16, :] = ones
            fg_s[h, NE * FH + 16 : FG, :] = jnp.zeros((FG - NE * FH - 16, n), BF)
        for ref in (dwa_s, dw1_s, dw2_s, dtw_s, dcol_s, dlog_s):
            ref[...] = jnp.zeros_like(ref)
        users = start_s.shape[1]
        after = row_s.shape[1] + 512
        sizes = [line_ref[:, after + users * b : after + users * b + users] for b in range(start_s.shape[0])]
        fill_weights(core, batch_rows, jnp.concatenate(sizes, axis=0), start_s, row_s)
        gates = []
        for side in range(2):
            base = HALF * FH * side
            holder = core if side == 0 else 1 - core
            for c in range(chunks):
                ref, c_in = u_refs[side][c * pieces // chunks], c % (chunks // pieces)
                at = chunk_at(c, chunks, holder)
                to = pl.multiple_of(ds * at, ds)
                w1_s[pl.ds(to, ds), base : base + QA] = ref[c_in, :, 0:QA]
                q_s[tab_ref[1 + at]] = ref[c_in, 0:fs, QA:UC].astype(F32)
                small = ref[c_in, 0:fs, QS:UC].astype(F32)
                ga_s[pl.ds(to, fs), :] = small
                ga_s[pl.ds(pl.multiple_of(to + fs, fs), fs), :] = pltpu.roll(small, 128 - NE, 1)
                wat_s[pl.ds(pl.multiple_of(to + holder * fs, fs), fs), :] = ref[c_in, fs:ds, QA : QA + XR]
            for k in range(HALF):
                block = w1_s[:, base + FH * k : base + FH * k + FH]
                w1t_s[base + FH * k : base + FH * k + FH, :] = (block.astype(F32).T * 0.5).astype(BF)
            gates.append(swap_halves(ga_s[...].T[GA : GA + NE], second_core))
            cols = HALF * EO
            w2 = q_s[:, :, 0:cols].reshape(FH, cols) * 0.5
            w2_s[:, cols * side : cols * side + cols] = w2.astype(BF)
            w2t_s[cols * side : cols * side + cols, :] = w2.T.astype(BF)
            b1_s[side] = q_s[:, :, cols : cols + 128].reshape(FH, 128) * 0.5
            last = q_s[:, 0:osz, cols : cols + 128].reshape(EO, 128)
            b2_s[side] = last * 0.5
            tower = last[:, 0:TW]
            rest = jnp.zeros_like(tower)
            both = jnp.concatenate([tower, rest] if side == 0 else [rest, tower], axis=1)
            tw_s[EO * side : EO * side + EO, :] = both.astype(BF)
            tt_s[:, EO * side : EO * side + EO] = (both.T * 0.5).astype(BF)
        gates = jnp.concatenate(gates, axis=0)
        w1t_s[NE * FH : NE * FH + 16, :] = gates.astype(BF)
        pad = jnp.concatenate([gates, jnp.zeros((112, D), F32)], axis=0)
        w1_s[:, NE * FH : FG] = pad.T.astype(BF)
        half = row_s.shape[1]
        vecs = [square([r[:, half + 128 * j : half + 128 * j + 128] for j in range(4)]).T for r in (line_ref, far_line_ref)]
        gb_s[...] = jnp.concatenate([swap_halves(v[0:NE, 0:1], second_core) for v in vecs], axis=0)
        b1 = jnp.concatenate([v[0:TW, 1:2] for v in vecs], axis=0)
        head = jnp.concatenate([v[0:TW, 2:3] for v in vecs], axis=0)
        last = jnp.concatenate([v[0:1, 3:4] for v in vecs] * TW, axis=0)
        tcol_s[...] = jnp.concatenate([b1 * 0.5, head, head * 0.5, last], axis=1)

    def chain(h):
        at = slice(SUB * h, SUB * h + SUB)
        x_s[h, 0:EMB, :] = emb_ref[:, at]
        x_s[h, EMB : EMB + DENSE, :] = dense_ref[:, pl.ds(pl.multiple_of(step * TILE + SUB * h, SUB), SUB)]
        hid = mm(wat_s[...], x_s[h]).astype(BF)
        hid_s[h, 0:D, :] = hid
        yield
        logits = mm(w1t_s[NE * FH : NE * FH + 16, :], hid) + gb_s[...]
        probs = []
        for t in range(2):
            lt = logits[NE * t : NE * t + NE]
            e = jnp.exp(lt - jnp.max(lt, axis=0, keepdims=True))
            probs.append(e / jnp.sum(e, axis=0, keepdims=True))
        mix = [None, None]
        pend = None
        nxt = mm(w1t_s[0:FH, :], hid)
        yield
        for k in range(NE + 1):
            pre = nxt
            if k < NE - 1:
                nxt = mm(w1t_s[FH * (k + 1) : FH * (k + 2), :], hid)
            if k < NE:
                m, s = act_narrow(pre + b1_s[k // HALF, :, B1 + k % HALF : B1 + k % HALF + 1])
                mid_s[h, k, 0:FH, :] = m
                sl1_s[h, FH * k : FH * k + FH, :] = s
                pre2 = mm(w2t_s[EO * k : EO * k + EO, :], m)
            if pend is not None:
                j = k - 1
                o, s = act_narrow(pend + b2_s[j // HALF, :, TW + j % HALF : TW + j % HALF + 1])
                out_s[h, EO * j : EO * j + EO, :] = o
                sl2_s[h, EO * j : EO * j + EO, :] = s
                o = o.astype(F32)
                for t in range(2):
                    term = probs[t][j : j + 1, :] * o
                    mix[t] = term if j == 0 else mix[t] + term
            pend = pre2
            yield
        mix_s[h, 0:EO, :] = mix[0].astype(BF)
        mix_s[h, EO : 2 * EO, :] = mix[1].astype(BF)
        act, slope = act_pair(mm(tt_s[...], mix_s[h, 0 : 2 * EO, :]) + tcol_s[:, 0:1])
        weighted = act * tcol_s[:, 1:2]
        lgos = []
        for t in range(2):
            logit = jnp.sum(weighted[TW * t : TW * t + TW], axis=0, keepdims=True) + tcol_s[t : t + 1, 3:4]
            label = (line_ref, far_line_ref)[t][:, pl.ds(pl.multiple_of(step * TILE + SUB * h, SUB), SUB)]
            lgos.append(row_s[:, pl.ds(pl.multiple_of(step * TILE + SUB * h, SUB), SUB)] * (0.5 * jnp.tanh(0.5 * logit) + 0.5 - label))
        lgo = jnp.concatenate([jnp.broadcast_to(lgos[t], (TW, SUB)) for t in range(2)], axis=0)
        dcol_s[...] += lane_fold(lgo * act)
        dlog_s[...] += lane_fold(jnp.concatenate([jnp.broadcast_to(lgos[t], (8, SUB)) for t in range(2)], axis=0))
        tg = (lgo * (tcol_s[:, 2:3] * slope)).astype(BF)
        yield
        dtw_s[...] += mm_nt(mix_s[h], tg)
        mgh = mm(tw_s[...], tg) * 0.5
        yield
        pgs = [[], []]
        mgs = [None] * NE
        for k in range(NE + 2):
            if k < NE:
                o = out_s[h, EO * k : EO * k + EO, :]
                og = None
                for t in range(2):
                    mg = mgh[EO * t : EO * t + EO]
                    pgs[t].append(jnp.sum((o * mg.astype(BF)).astype(F32), axis=0, keepdims=True))
                    term = probs[t][k : k + 1, :] * mg
                    og = term if og is None else og + term
                sg = og.astype(BF) * sl2_s[h, EO * k : EO * k + EO, :]
                sg_s[h, EO * (k % 2) : EO * (k % 2) + EO, :] = sg
                mgs[k] = mm(w2_s[:, EO * k : EO * k + EO], sg)
            if 1 <= k < NE + 1:
                j = k - 1
                dw2_s[:, EO * j : EO * j + EO] += mm_nt(mid_s[h, j], sg_s[h, EO * (j % 2) : EO * (j % 2) + EO, :])
                fg = mgs[j].astype(BF) * sl1_s[h, FH * j : FH * j + FH, :]
                fg_s[h, FH * j : FH * j + FH, :] = fg
            if k >= 2:
                j = k - 2
                dw1_s[:, FH * j : FH * j + FH] += mm_nt(hid_s[h], fg_s[h, FH * j : FH * j + FH, :])
            yield
        lgs = []
        for t in range(2):
            pg = jnp.concatenate(pgs[t], axis=0)
            lgs.append(2.0 * probs[t] * (pg - jnp.sum(probs[t] * pg, axis=0, keepdims=True)))
        fg_s[h, NE * FH : NE * FH + 16, :] = jnp.concatenate(lgs, axis=0).astype(BF)
        yield
        dw1_s[:, NE * FH : FG] += mm_nt(hid_s[h], fg_s[h, NE * FH : FG, :])
        hg = mm(w1_s[...], fg_s[h]).astype(BF)
        hg_ref[:, at] = hg
        yield
        dwa_s[...] += mm_nt(hg, x_s[h])
        yield

    take_turns([chain(h) for h in range(TILE // SUB)], LAG)

    @pl.when(step == pl.num_programs(0) - 1)
    def _():
        gate = dw1_s[:, NE * FH : FG].T
        dlog = jnp.sum(dlog_s[...], axis=1, keepdims=True)
        dcol = jnp.sum(dcol_s[...].T, axis=0, keepdims=True)
        for side in range(2):
            own_gate = swap_halves(gate[NE * side : NE * side + NE], second_core)
            ga_s[...] = jnp.concatenate([own_gate[:, 0:D], jnp.zeros((120, D), F32)], axis=0).T
            b1 = [dw1_s[D : D + 1, FH * k : FH * k + FH] for k in range(HALF * side, HALF * side + HALF)]
            b1 = jnp.concatenate(b1 + [jnp.zeros((124, FH), F32)], axis=0).T
            b2 = [dw2_s[FH : FH + 1, EO * k : EO * k + EO] for k in range(HALF * side, HALF * side + HALF)]
            b2 = jnp.concatenate(b2 + [jnp.zeros((60, EO), F32)], axis=0).T
            tower = dtw_s[EO * side : EO * side + EO, TW * side : TW * side + TW]
            tower = jnp.concatenate([tower, b2], axis=1)
            lanes = slice(TW * side, TW * side + TW)
            blank = jnp.zeros((1, TW), F32)
            lines = [jnp.concatenate([a, blank], axis=1) for a in (dtw_s[2 * EO : 2 * EO + 1, lanes], dcol[:, lanes])]
            gate_b = jnp.sum(jnp.where(lax.broadcasted_iota(jnp.int32, (NE, D + 16), 1) == D, own_gate, 0.0), axis=1, keepdims=True)
            small = jnp.concatenate([gate_b, dlog[8 * side : 8 * side + 8]], axis=0)
            small = jnp.concatenate([jnp.broadcast_to(small, (16, 128)), jnp.zeros((112, 128), F32)], axis=0).T[0:1]
            tail = jnp.concatenate(lines + [small, jnp.zeros((fs - osz - 3, 128), F32)], axis=0)
            b1 = pltpu.roll(b1, B1, 1)
            for c in range(chunks):
                dsm_s[fs * c : fs * c + fs, :] = b1[fs * c : fs * c + fs] + jnp.concatenate([tower[osz * c : osz * c + osz], tail], axis=0)
            holder = core if side == 0 else 1 - core
            cols = HALF * EO
            for n in range(chunks):
                ref, c = du_refs[quarters * side + n * quarters // chunks], n % (chunks // quarters)
                at = chunk_at(n, chunks, holder)
                to = pl.multiple_of(ds * at, ds)
                where = pl.ds(pl.multiple_of(tab_ref[1 + at] * fs, fs), fs)
                ref[c, :, 0:QA] = dw1_s[pl.ds(to, ds), QA * side : QA * side + QA].astype(BF)
                ref[c, 0:fs, QA:QS] = dw2_s[where, cols * side : cols * side + cols].astype(BF)
                low = pltpu.roll(ga_s[pl.ds(to, fs), :], GA, 1)
                high = pltpu.roll(ga_s[pl.ds(pl.multiple_of(to + fs, fs), fs), :], GA + NE, 1)
                ref[c, 0:fs, QS:UC] = (dsm_s[where, :] + low + high).astype(BF)
                lower = dwa_s[pl.ds(pl.multiple_of(to + holder * fs, fs), fs), :]
                ref[c, fs:ds, QA:UC] = jnp.concatenate([lower, jnp.zeros((fs, UC - QA - XR), F32)], axis=1).astype(BF)


def fill_weights(core, batch_rows, sizes, start_s, out_ref):
    batches, users = sizes.shape
    counts = jnp.concatenate([sizes.astype(F32), jnp.zeros((16 - batches, users), F32)], axis=0)
    turned = jnp.concatenate([counts, jnp.zeros((112, users), F32)], axis=0).T
    before = lax.broadcasted_iota(jnp.int32, (users, users), 1) < lax.broadcasted_iota(jnp.int32, (users, users), 0)
    starts = mm(jnp.where(before, 1.0, 0.0).astype(BF), turned.astype(BF))
    for b in range(batches):
        start_s[b] = jnp.broadcast_to(starts[:, b : b + 1], (users, 128))
    first = lax.broadcasted_iota(jnp.int32, counts.shape, 1) == 0
    rises = counts - jnp.where(first, 0.0, pltpu.roll(counts, 1, 1))
    line = lax.broadcasted_iota(jnp.int32, counts.shape, 0)
    steps = out_ref.shape[1] // SUB
    for step in range(steps):
        at_step = core * steps + step
        batch = at_step // (batch_rows // SUB)
        first_row = (at_step % (batch_rows // SUB) * SUB).astype(F32)
        begins = start_s[batch]
        places = first_row + lax.broadcasted_iota(jnp.int32, (1, 128), 1).astype(F32)
        begun = [jnp.where(begins <= places + 128.0 * c, 1.0, 0.0).astype(BF) for c in range(SUB // 128)]
        rise = jnp.where(line == batch, rises, 0.0).astype(BF)
        size = jnp.sum(mm(rise, jnp.concatenate(begun, axis=1)), axis=0, keepdims=True)
        out_ref[:, SUB * step : SUB * step + SUB] = 1.0 / size


def const2(i, c):
    return (0, 0)


def main_call(table, embt, denset, line, far_line, sizes_shape, own_u, far_u):
    rows = embt.shape[1]
    half = rows // 2
    steps = half // TILE
    pieces = len(own_u)
    chunks = sum(a.shape[0] for a in own_u)
    fs, ds = FH // chunks, D // chunks

    def own(i, c):
        return (0, c[0] * steps + i)

    quarters = min(4, chunks)
    grads = [(chunks // quarters, ds, UC)] * (2 * quarters)
    parts = TILE // SUB
    spec = pltpu.PrefetchScalarGridSpec(
        num_scalar_prefetch=1,
        grid=(steps,),
        in_specs=[
            pl.BlockSpec((EMB, TILE), own),
            whole(),
            whole(),
            whole(),
        ]
        + [whole() for _ in (*own_u, *far_u)],
        out_specs=[pl.BlockSpec((D, TILE), lambda i, c: (0, i))] + [whole()] * (1 + 2 * quarters),
        scratch_shapes=[
            pltpu.VMEM((parts, XR, SUB), BF),
            pltpu.VMEM((parts, D + 16, SUB), BF),
            pltpu.VMEM((parts, NE, FH + 16, SUB), BF),
            pltpu.VMEM((parts, NE * FH, SUB), BF),
            pltpu.VMEM((parts, NE * EO, SUB), BF),
            pltpu.VMEM((parts, NE * EO, SUB), BF),
            pltpu.VMEM((parts, 2 * EO, SUB), BF),
            pltpu.VMEM((parts, FG, SUB), BF),
            pltpu.VMEM((parts, 2 * EO + 16, SUB), BF),
            pltpu.VMEM((D, FG), BF),
            pltpu.VMEM((NE * FH + 16, D), BF),
            pltpu.VMEM((D, 128), F32),
            pltpu.VMEM((NE * EO, FH), BF),
            pltpu.VMEM((FH, NE * EO), BF),
            pltpu.VMEM((2, FH, 128), F32),
            pltpu.VMEM((2, EO, 128), F32),
            pltpu.VMEM((16, 1), F32),
            pltpu.VMEM((2 * TW, 2 * EO), BF),
            pltpu.VMEM((2 * EO, 2 * TW), BF),
            pltpu.VMEM((2 * TW, 4), F32),
            pltpu.VMEM((chunks, fs, UC - QA), F32),
            pltpu.VMEM((D, XR), F32),
            pltpu.VMEM((D + 16, FG), F32),
            pltpu.VMEM((FH + 16, NE * EO), F32),
            pltpu.VMEM((2 * EO + 16, 2 * TW), F32),
            pltpu.VMEM((2 * TW, 128), F32),
            pltpu.VMEM((16, 128), F32),
            pltpu.VMEM((FH, 128), F32),
            pltpu.VMEM((*sizes_shape, 128), F32),
            pltpu.VMEM((1, half), F32),
        ],
    )
    return pl.pallas_call(
        functools.partial(main_kernel, pieces, chunks, rows // sizes_shape[0]),
        grid_spec=spec,
        out_shape=[jax.ShapeDtypeStruct((D, half), BF), jax.ShapeDtypeStruct((D, XR), BF)]
        + [jax.ShapeDtypeStruct(a, BF) for a in grads],
        compiler_params=pltpu.CompilerParams(vmem_limit_bytes=48 * 1024 * 1024),
        cost_estimate=pl.CostEstimate(flops=50_000_000_000, bytes_accessed=24_000_000, transcendentals=0),
        name="experts",
    )(table, embt, denset, line, far_line, *own_u, *far_u)


def input_kernel(tab_ref, hg_ref, wat_ref, *refs):
    eg_ref, dg_ref, done_ref, wa_s = refs[-4:]

    @pl.when(pl.program_id(0) == 0)
    def _():
        wa_s[...] = wat_ref[...].astype(F32).T.astype(BF)
        done_ref[...] = jnp.zeros_like(done_ref)

    eg = mm(wa_s[...], hg_ref[...])
    eg_ref[...] = eg[0:EMB]
    dg_ref[...] = eg[EMB : EMB + DENSE]


def input_call(table, hg, wat, token, other, name):
    half = hg.shape[1]
    tile = TILE
    steps = half // tile

    def place(i, c):
        return (0, (c[0] if other is None else 1 - c[0]) * steps + i)

    extra = [token] + (list(other) if other is not None else [])
    spec = pltpu.PrefetchScalarGridSpec(
        num_scalar_prefetch=1,
        grid=(steps,),
        in_specs=[pl.BlockSpec((D, tile), lambda i, c: (0, i)), pl.BlockSpec((D, XR), const2, pipeline_mode=pl.Buffered(1))]
        + [whole(pl.ANY) for _ in extra],
        out_specs=[pl.BlockSpec((EMB, tile), place), pl.BlockSpec((DENSE, tile), place), pl.BlockSpec((8, 128), const2)],
        scratch_shapes=[pltpu.VMEM((XR, D), BF)],
    )
    return pl.pallas_call(
        input_kernel,
        grid_spec=spec,
        out_shape=[jax.ShapeDtypeStruct((EMB, 2 * half), F32), jax.ShapeDtypeStruct((DENSE, 2 * half), F32), jax.ShapeDtypeStruct((8, 128), F32)],
        input_output_aliases={} if other is None else {4: 0, 5: 1},
        compiler_params=pltpu.CompilerParams(vmem_limit_bytes=32 * 1024 * 1024),
        cost_estimate=pl.CostEstimate(flops=4_000_000_000, bytes_accessed=9_000_000, transcendentals=0),
        name=name,
    )(table, hg, wat, *extra)


def widen(a):
    return jnp.concatenate([a.astype(F32), jnp.zeros((a.shape[0], 128 - a.shape[1]), F32)], axis=1)


def square(rows):
    count = sum(a.shape[0] for a in rows)
    return jnp.concatenate(rows + [jnp.zeros((128 - count, 128), F32)], axis=0)


def pack_kernel(core_ref, emb_ref, dense_ref, bias_ref, w1_ref, w2_ref, b1_ref, b2_ref, gate_ref, tower_ref, *refs):
    sizes_ref, label_ref, u_ref, line_ref = refs[4:]
    rows = label_ref.shape[1]
    line_ref[:, 0:rows] = label_ref[...].astype(F32)
    for j in range(4):
        line_ref[:, rows + 128 * j : rows + 128 * j + 128] = widen(refs[j][...])
    users = sizes_ref.shape[1]
    for b in range(sizes_ref.shape[0]):
        line_ref[:, rows + 512 + users * b : rows + 512 + users * b + users] = sizes_ref[b : b + 1, :].astype(F32)
    fs = u_ref.shape[0] // 2
    turned = square([widen(r[...]) for r in (b1_ref, b2_ref, gate_ref, dense_ref, bias_ref)]).T
    lane = lax.broadcasted_iota(jnp.int32, (fs, 128), 1)
    low, high = turned[0:fs], turned[fs : 2 * fs]
    small = jnp.concatenate([widen(tower_ref[...]), jnp.zeros((fs - tower_ref.shape[0], 128), F32)], axis=0)
    small += jnp.where((lane >= TW) & (lane < TW + HALF), pltpu.roll(low, TW - HALF, 1), 0.0)
    small += jnp.where(((lane >= B1) & (lane < B1 + HALF)) | ((lane >= GA) & (lane < GA + NE)), pltpu.roll(low, B1, 1), 0.0)
    small += jnp.where((lane >= GA + NE) & (lane < GA + 2 * NE), pltpu.roll(high, GA, 1), 0.0)
    for k in range(HALF):
        u_ref[:, FH * k : FH * k + FH] = w1_ref[k]
        u_ref[0:fs, QA + EO * k : QA + EO * k + EO] = w2_ref[k]
    u_ref[0:fs, QS:UC] = small.astype(BF)
    second_core = core_ref[0] == 1
    lanes = lax.broadcasted_iota(jnp.int32, (2 * fs, 128), 1)
    last = widen(emb_ref[:, 384:EMB]) + jnp.where((lanes >= 32) & (lanes < 33 + DENSE), pltpu.roll(turned[0 : 2 * fs], 16, 1), 0.0)
    for c in range(3):
        block = emb_ref[:, 128 * c : 128 * c + 128]
        u_ref[fs:, QA + 128 * c : QA + 128 * c + 128] = jnp.where(second_core, block[fs:], block[0:fs])
    u_ref[fs:, QA + 384 : QA + 512] = jnp.where(second_core, last[fs:], last[0:fs]).astype(BF)
    u_ref[fs:, QA + 512 : UC] = jnp.zeros((fs, UC - QA - 512), BF)


def whole(memory=pltpu.VMEM):
    return pl.BlockSpec(memory_space=memory)


def pack_call(core, *parts):
    ds = parts[3].shape[1]
    return pl.pallas_call(
        pack_kernel,
        in_specs=[whole(pltpu.SMEM)] + [whole() for _ in parts],
        out_specs=[whole(), whole()],
        out_shape=[jax.ShapeDtypeStruct((ds, UC), BF), jax.ShapeDtypeStruct((1, parts[-1].shape[1] + 512 + parts[-2].size), F32)],
        name="pack",
    )(core, *parts)


def sum_kernel(groups, count, *refs):
    ins, outs = refs[:count], refs[-len(groups) :]
    for group, out in zip(groups, outs):
        total = None
        for number, at in group:
            term = ins[number][at].astype(F32)
            total = term if total is None else total + term
        out[...] = total.astype(out.dtype)


def sum_call(name, arrays, groups, shapes, token=None, through=None):
    extra = [a for a in (token, through) if a is not None]
    lead = [] if through is None else [through]
    return pl.pallas_call(
        functools.partial(sum_kernel, groups, len(arrays)),
        in_specs=[whole() for _ in arrays] + [whole(pl.ANY) for _ in extra],
        out_specs=[whole(pl.ANY) for _ in lead] + [whole() for _ in shapes],
        out_shape=[jax.ShapeDtypeStruct(a.shape, a.dtype) for a in lead] + [jax.ShapeDtypeStruct(a, BF) for a in shapes],
        input_output_aliases={len(arrays) + len(extra) - 1: 0} if lead else {},
        compiler_params=pltpu.CompilerParams(vmem_limit_bytes=16 * 1024 * 1024),
        name=name,
    )(*arrays, *extra)


def finish_kernel(scale, core_ref, token_ref, *refs):
    total = sum(r[...].astype(F32) for r in refs[:4]) * scale
    ds = total.shape[0]
    fs = ds // 2
    own_part = total[fs:, QA : QA + XR]
    far_part = sum(r[...].astype(F32) for r in refs[4:8])[:, 0:XR] * scale
    second_core = core_ref[0] == 1
    ta = jnp.concatenate([jnp.where(second_core, far_part, own_part), jnp.where(second_core, own_part, far_part)], axis=0)
    emb_ref, dense_ref, bias_ref, w1_ref, b1_ref, w2_ref, b2_ref, gate_ref, gb_ref, tower_ref, t1_ref, t2_ref, t3_ref = refs[8:]
    osz = tower_ref.shape[0]
    for k in range(HALF):
        w1_ref[k] = total[:, FH * k : FH * k + FH]
        w2_ref[k] = total[0:fs, QA + EO * k : QA + EO * k + EO]
    small = total[0:fs, QS:UC]
    turned = square([small]).T
    b1_ref[...] = turned[B1 : B1 + HALF, 0:fs]
    b2_ref[...] = turned[TW : TW + HALF, 0:osz]
    gates = turned[GA : GA + NE] + pltpu.roll(turned[GA + NE : GA + 2 * NE], fs, 1)
    gate_ref[...] = gates[:, 0 : 2 * fs]
    tower_ref[...] = small[0:osz, 0:TW]
    t1_ref[...] = small[osz : osz + 1, 0:TW]
    t2_ref[...] = small[osz + 1 : osz + 2, 0:TW]
    gb_ref[...] = small[osz + 2 : osz + 3, 0:NE]
    t3_ref[...] = small[osz + 2 : osz + 3, NE : NE + 1]
    emb_ref[...] = ta[:, 0:EMB]
    last = square([widen(ta[:, 384:XR])]).T
    dense_ref[...] = last[32 : 32 + DENSE, 0 : 2 * fs]
    bias_ref[...] = last[32 + DENSE : 33 + DENSE, 0 : 2 * fs]


def finish_call(scale, core, token, arrays, ds, fs, osz):
    shapes = [
        (ds, EMB), (DENSE, ds), (1, ds), (HALF, ds, FH), (HALF, fs), (HALF, fs, EO), (HALF, osz), (NE, ds), (1, NE),
        (osz, TW), (1, TW), (1, TW), (1, 1),
    ]
    return pl.pallas_call(
        functools.partial(finish_kernel, scale),
        in_specs=[whole(pltpu.SMEM), whole(pl.ANY)] + [whole() for _ in arrays],
        out_specs=[whole() for _ in shapes],
        out_shape=[jax.ShapeDtypeStruct(a, F32) for a in shapes],
        compiler_params=pltpu.CompilerParams(vmem_limit_bytes=8 * 1024 * 1024),
        name="finish",
    )(core, token, *arrays)


def hop(a, mask, size):
    return lax.ppermute(a, "rows", [(i, i ^ mask) for i in range(size)])


def cross(a, masks, size):
    pairs = [(2 * i + t, 2 * (i ^ masks[t]) + t) for i in range(size) for t in range(2)]
    return lax.ppermute(a, ("rows", "task"), pairs)


def partner(a):
    return lax.ppermute(a, "task", [(0, 1), (1, 0)])


def add_wide(a, b):
    return a.astype(F32) + b.astype(F32)


def halves(line, denset, core):
    rows = denset.shape[1]
    half = rows // 2
    own_line = jnp.concatenate([lax.dynamic_slice(line, (0, core * half), (1, half)), line[:, rows:]], axis=1)
    sent_line = jnp.concatenate([lax.dynamic_slice(line, (0, (1 - core) * half), (1, half)), line[:, rows : rows + 512]], axis=1)
    return own_line, partner(sent_line), lax.dynamic_slice(denset, (0, core * half), (DENSE, half))


def pad_to(a, rows, cols):
    return jnp.pad(a, ((0, rows - a.shape[0]), (0, cols - a.shape[1])))


def body(
    emb, dense, group_sizes, labels, w_emb, w_dense, b_in, expert_w1, expert_b1, expert_w2, expert_b2,
    gate_w, gate_b, tower_w1, tower_b1, tower_w2, tower_b2,
):
    size = lax.axis_size("rows")
    core = lax.axis_index("task")
    place = lax.axis_index("rows")
    user_count = group_sizes.shape[1] * group_sizes.shape[0] * size
    ds, fs, osz = D // size, FH // size, EO // size
    fast = size == 16
    smalls = (gate_b, tower_b1, tower_w2, tower_b2[None])

    if fast:
        one_core = core[None].astype(jnp.int32)
        gate_t = jnp.transpose(gate_w, (0, 2, 1))[0]
        shard, line = pack_call(
            one_core, w_emb.T, w_dense, b_in[None], expert_w1, expert_w2, expert_b1, expert_b2, gate_t, tower_w1[0], *smalls, group_sizes, labels
        )
        pairs = [jnp.stack([shard, hop(shard, 4, size)]), jnp.stack([hop(shard, 8, size), hop(shard, 12, size)])]
        own_line, far_line, own_dense = halves(line, dense.T, core)
        once, twice = cross(pairs[0], (1, 2), size), cross(pairs[0], (2, 1), size)
        held = (pairs[1], once, twice, own_line, far_line, own_dense)
        pairs[1], once, twice, own_line, far_line, own_dense = lax.optimization_barrier(held)
        once, twice = [once, cross(pairs[1], (1, 2), size)], [twice, cross(pairs[1], (2, 1), size)]
        own_u = pairs + once + twice + [cross(a, (2, 1), size) for a in once]
        steps = jnp.arange(16, dtype=jnp.int32)
        order = place ^ (steps % 4 * 4 + steps // 4)
    else:
        gather = functools.partial(lax.all_gather, axis_name="rows", axis=0, tiled=True)
        proj = jnp.concatenate([w_emb.T, w_dense.T, b_in[:, None], jnp.zeros((ds, 82), BF)], axis=1)
        w1_all = gather(jnp.transpose(expert_w1, (1, 0, 2)).reshape(ds, QA))
        w2_all = gather(jnp.transpose(expert_w2, (1, 0, 2)).reshape(fs, HALF * EO))
        o_all = gather(jnp.concatenate([tower_w1[0], expert_b2.T], axis=1))
        b1_all, g_all, proj_all = gather(expert_b1.T), gather(gate_w[0]), gather(proj)
        small = jnp.concatenate([pad_to(o_all, FH, B1), pad_to(b1_all, FH, GA - B1), g_all[0:FH], g_all[FH:], jnp.zeros((FH, 32), BF)], axis=1)
        part = jnp.where(core == 0, proj_all[0:FH], proj_all[FH:])
        lower = jnp.concatenate([part, jnp.zeros((FH, UC - QA - 512), BF)], axis=1)
        own_u = [jnp.concatenate([w1_all, jnp.concatenate([jnp.concatenate([w2_all, small], axis=1), lower], axis=0)], axis=1)[None]]
        order = jnp.zeros((1,), jnp.int32)
        line = [labels.astype(F32)] + [pad_to(a, 1, 128).astype(F32) for a in smalls]
        line = jnp.concatenate(line + [group_sizes.astype(F32).reshape(1, -1)], axis=1)
        own_line, far_line, own_dense = halves(line, dense.T, core)
    far_u = [partner(a) for a in own_u]
    table = jnp.concatenate([core[None].astype(jnp.int32), order])

    hg, wat, *grads = main_call(table, emb.T, own_dense, own_line, far_line, group_sizes.shape, own_u, far_u)
    own, far = grads[: len(grads) // 2], grads[len(grads) // 2 :]
    scale = 1.0 / user_count
    if fast:
        quarter, every = (4, ds, UC), slice(0, 4)
        (third,) = sum_call("sum_fourth", [own[3], partner(far[3])], [[(0, every), (1, every)]], [quarter])
        got_third = cross(third, (2, 1), size)
        hg, second = sum_call("sum_third", [own[2], partner(far[2])], [[(0, every), (1, every)]], [quarter], third, hg)
        got_second = cross(second, (2, 1), size)
        far_first, far_hg = partner(far[1]), partner(hg)
        eg, dg, token = input_call(table, hg, wat, second, None, "input_own")
        (first,) = sum_call("sum_second", [own[1], far_first, got_third], [[(j, every) for j in range(3)]], [quarter], token)
        got_first = cross(first, (1, 2), size)
        far_none = partner(far[0])
        eg, dg, token = input_call(table, far_hg, wat, first, (eg, dg), "input_far")
        groups = [[(j, k) for j in range(4)] for k in range(4)]
        sums = sum_call("sum_first", [own[0], far_none, got_second, got_first], groups, [(ds, UC)] * 4, token)
        parts = [sums[0]] + [hop(sums[a], 4 * a, size) for a in range(1, 4)]
        parts += [partner(a[fs:, QA : QA + 512]) for a in parts]
        out = finish_call(scale, one_core, sums[0], parts, ds, fs, osz)
        g_emb, g_dense, g_bias, g_w1, g_b1, g_w2, g_b2, g_gate, g_gb, g_tower, g_t1, g_t2, g_t3 = out
        return (
            eg.T, dg.T, g_emb.T, g_dense, g_bias[0], g_w1, g_b1, g_w2, g_b2, g_gate.T[None], g_gb, g_tower[None], g_t1, g_t2, g_t3[0],
        )
    eg, dg, token = input_call(table, hg, wat, far[0], None, "input_own")
    eg, dg, _ = input_call(table, partner(hg), wat, token, (eg, dg), "input_far")
    scatter = functools.partial(lax.psum_scatter, axis_name="rows", scatter_dimension=0, tiled=True)
    wide = add_wide(own[0][0], partner(far[0])[0])
    upper, near = wide[0:FH, QA:UC], wide[FH:, QA : QA + XR]
    far, small = partner(near), upper[:, HALF * EO :]
    ta = scatter(jnp.concatenate([jnp.where(core == 0, near, far), jnp.where(core == 0, far, near)], axis=0)) * scale
    tp = jnp.transpose((scatter(wide[:, 0:QA]) * scale).reshape(ds, HALF, FH), (1, 0, 2))
    tw2, to, tb1 = scatter(upper[:, 0 : HALF * EO]) * scale, scatter(small[0:EO, 0:B1]) * scale, scatter(small[:, B1 : B1 + HALF]) * scale
    tg = scatter(jnp.concatenate([small[:, GA : GA + NE], small[:, GA + NE : GA + 2 * NE]], axis=0)) * scale
    ts = lax.psum(small[EO : EO + 3], "rows") * scale
    return (
        eg.T,
        dg.T,
        ta[:, 0:EMB].T,
        ta[:, EMB : EMB + DENSE].T,
        ta[:, EMB + DENSE],
        tp,
        tb1.T,
        jnp.transpose(tw2.reshape(fs, HALF, EO), (1, 0, 2)),
        to[:, TW : TW + HALF].T,
        tg[None],
        ts[2:3, 0:NE],
        to[:, 0:TW][None],
        ts[0:1, 0:TW],
        ts[1:2, 0:TW],
        ts[2, NE : NE + 1],
    )


def solution(mesh):
    in_specs = (
        P("rows", None),
        P("rows", None),
        P("rows", None),
        P("task", "rows"),
        P(None, "rows"),
        P(None, "rows"),
        P("rows"),
        P("task", "rows", None),
        P("task", "rows"),
        P("task", "rows", None),
        P("task", "rows"),
        P("task", "rows", None),
        P("task", None),
        P("task", "rows", None),
        P("task", None),
        P("task", None),
        P("task"),
    )
    out_specs = (
        P("rows", None),
        P("rows", None),
        P(None, "rows"),
        P(None, "rows"),
        P("rows"),
        P("task", "rows", None),
        P("task", "rows"),
        P("task", "rows", None),
        P("task", "rows"),
        P("task", "rows", None),
        P("task", None),
        P("task", "rows", None),
        P("task", None),
        P("task", None),
        P("task"),
    )
    return jax.shard_map(body, mesh=mesh, in_specs=in_specs, out_specs=out_specs, check_vma=False)
```

```python
import functools

import jax
import jax.numpy as jnp
from jax import lax
from jax.experimental import pallas as pl
from jax.experimental.pallas import tpu as pltpu
from jax.sharding import PartitionSpec as P

F32 = jnp.float32
BF = jnp.bfloat16
NT = (((1,), (1,)), ((), ()))
D, FH, EO, TW, NE = 512, 256, 128, 64, 8
HALF = NE // 2
EMB, DENSE = 416, 13
XR = 448
QA = HALF * FH
QS = QA + HALF * EO
UC = QS + 128
B1, GA = 72, 80
FG = NE * FH + 128
TILE = 1024
SUB = 512


def mm(a, b):
    return jnp.dot(a, b, preferred_element_type=F32)


def mm_nt(a, b):
    return lax.dot_general(a, b, NT, preferred_element_type=F32)


def act_narrow(half):
    return act_pair(half.astype(BF))


def act_pair(half):
    t = jnp.tanh(half)
    q = 1.0 + t
    m = half * q
    return m, q + m * (1.0 - t)


def swap_halves(a, flag):
    return jnp.where(flag, jnp.concatenate([a[HALF:NE], a[0:HALF]], axis=0), a)


def lane_fold(a):
    total = a[:, 0:128]
    for c in range(1, a.shape[1] // 128):
        total = total + a[:, 128 * c : 128 * c + 128]
    return total


def chunk_at(n, chunks, flag):
    if chunks == 1 or n // 4 in (0, 3):
        return n
    return n + 4 * flag if n // 4 == 1 else n - 4 * flag


LAG = 4


def take_turns(chains, lag):
    going = [(chain, lag * j) for j, chain in enumerate(chains)]
    while going:
        left = []
        for chain, wait in going:
            if wait > 0:
                left.append((chain, wait - 1))
            elif next(chain, True) is None:
                left.append((chain, 0))
        going = left


def main_kernel(pieces, chunks, batch_rows, tab_ref, *refs):
    emb_ref, dense_ref, line_ref, far_line_ref = refs[:4]
    u_refs = (refs[4 : 4 + pieces], refs[4 + pieces : 4 + 2 * pieces])
    quarters = min(4, chunks)
    hg_ref, wat_s, *du_refs = refs[4 + 2 * pieces : 6 + 2 * pieces + 2 * quarters]
    (
        x_s, hid_s, mid_s, sl1_s, out_s, sl2_s, sg_s, fg_s, mix_s,
        w1_s, w1t_s, ga_s, w2t_s, w2_s, b1_s, b2_s, gb_s, tt_s, tw_s, tcol_s, q_s,
        dwa_s, dw1_s, dw2_s, dtw_s, dcol_s, dlog_s, dsm_s, start_s, row_s,
    ) = refs[6 + 2 * pieces + 2 * quarters :]
    n = SUB
    fs, osz, ds = FH // chunks, EO // chunks, D // chunks
    step = pl.program_id(0)
    core = tab_ref[0]
    second_core = core == 1

    @pl.when(step == 0)
    def _():
        row_number = lax.broadcasted_iota(jnp.int32, (32, n), 0)
        ones = jnp.where(lax.broadcasted_iota(jnp.int32, (16, n), 0) == 0, 1.0, 0.0).astype(BF)
        for h in range(TILE // SUB):
            x_s[h, EMB:XR, :] = jnp.where(row_number == DENSE, 1.0, 0.0).astype(BF)
            hid_s[h, D : D + 16, :] = ones
            for k in range(NE):
                mid_s[h, k, FH : FH + 16, :] = ones
            mix_s[h, 2 * EO : 2 * EO + 16, :] = ones
            fg_s[h, NE * FH + 16 : FG, :] = jnp.zeros((FG - NE * FH - 16, n), BF)
        for ref in (dwa_s, dw1_s, dw2_s, dtw_s, dcol_s, dlog_s):
            ref[...] = jnp.zeros_like(ref)
        users = start_s.shape[1]
        after = row_s.shape[1] + 512
        sizes = [line_ref[:, after + users * b : after + users * b + users] for b in range(start_s.shape[0])]
        fill_weights(core, batch_rows, jnp.concatenate(sizes, axis=0), start_s, row_s)
        gates = []
        for side in range(2):
            base = HALF * FH * side
            holder = core if side == 0 else 1 - core
            for c in range(chunks):
                ref, c_in = u_refs[side][c * pieces // chunks], c % (chunks // pieces)
                at = chunk_at(c, chunks, holder)
                to = pl.multiple_of(ds * at, ds)
                w1_s[pl.ds(to, ds), base : base + QA] = ref[c_in, :, 0:QA]
                q_s[tab_ref[1 + at]] = ref[c_in, 0:fs, QA:UC].astype(F32)
                small = ref[c_in, 0:fs, QS:UC].astype(F32)
                ga_s[pl.ds(to, fs), :] = small
                ga_s[pl.ds(pl.multiple_of(to + fs, fs), fs), :] = pltpu.roll(small, 128 - NE, 1)
                wat_s[pl.ds(pl.multiple_of(to + holder * fs, fs), fs), :] = ref[c_in, fs:ds, QA : QA + XR]
            for k in range(HALF):
                block = w1_s[:, base + FH * k : base + FH * k + FH]
                w1t_s[base + FH * k : base + FH * k + FH, :] = (block.astype(F32).T * 0.5).astype(BF)
            gates.append(swap_halves(ga_s[...].T[GA : GA + NE], second_core))
            cols = HALF * EO
            w2 = q_s[:, :, 0:cols].reshape(FH, cols) * 0.5
            w2_s[:, cols * side : cols * side + cols] = w2.astype(BF)
            w2t_s[cols * side : cols * side + cols, :] = w2.T.astype(BF)
            b1_s[side] = q_s[:, :, cols : cols + 128].reshape(FH, 128) * 0.5
            last = q_s[:, 0:osz, cols : cols + 128].reshape(EO, 128)
            b2_s[side] = last * 0.5
            tower = last[:, 0:TW]
            rest = jnp.zeros_like(tower)
            both = jnp.concatenate([tower, rest] if side == 0 else [rest, tower], axis=1)
            tw_s[EO * side : EO * side + EO, :] = both.astype(BF)
            tt_s[:, EO * side : EO * side + EO] = (both.T * 0.5).astype(BF)
        gates = jnp.concatenate(gates, axis=0)
        w1t_s[NE * FH : NE * FH + 16, :] = gates.astype(BF)
        pad = jnp.concatenate([gates, jnp.zeros((112, D), F32)], axis=0)
        w1_s[:, NE * FH : FG] = pad.T.astype(BF)
        half = row_s.shape[1]
        vecs = [square([r[:, half + 128 * j : half + 128 * j + 128] for j in range(4)]).T for r in (line_ref, far_line_ref)]
        gb_s[...] = jnp.concatenate([swap_halves(v[0:NE, 0:1], second_core) for v in vecs], axis=0)
        b1 = jnp.concatenate([v[0:TW, 1:2] for v in vecs], axis=0)
        head = jnp.concatenate([v[0:TW, 2:3] for v in vecs], axis=0)
        last = jnp.concatenate([v[0:1, 3:4] for v in vecs] * TW, axis=0)
        tcol_s[...] = jnp.concatenate([b1 * 0.5, head, head * 0.5, last], axis=1)

    def chain(h):
        at = slice(SUB * h, SUB * h + SUB)
        x_s[h, 0:EMB, :] = emb_ref[:, at]
        x_s[h, EMB : EMB + DENSE, :] = dense_ref[:, pl.ds(pl.multiple_of(step * TILE + SUB * h, SUB), SUB)]
        hid = mm(wat_s[...], x_s[h]).astype(BF)
        hid_s[h, 0:D, :] = hid
        yield
        logits = mm(w1t_s[NE * FH : NE * FH + 16, :], hid) + gb_s[...]
        probs = []
        for t in range(2):
            lt = logits[NE * t : NE * t + NE]
            e = jnp.exp(lt - jnp.max(lt, axis=0, keepdims=True))
            probs.append(e / jnp.sum(e, axis=0, keepdims=True))
        mix = [None, None]
        pend = None
        nxt = mm(w1t_s[0:FH, :], hid)
        yield
        for k in range(NE + 1):
            pre = nxt
            if k < NE - 1:
                nxt = mm(w1t_s[FH * (k + 1) : FH * (k + 2), :], hid)
            if k < NE:
                m, s = act_narrow(pre + b1_s[k // HALF, :, B1 + k % HALF : B1 + k % HALF + 1])
                mid_s[h, k, 0:FH, :] = m
                sl1_s[h, FH * k : FH * k + FH, :] = s
                pre2 = mm(w2t_s[EO * k : EO * k + EO, :], m)
            if pend is not None:
                j = k - 1
                o, s = act_narrow(pend + b2_s[j // HALF, :, TW + j % HALF : TW + j % HALF + 1])
                out_s[h, EO * j : EO * j + EO, :] = o
                sl2_s[h, EO * j : EO * j + EO, :] = s
                o = o.astype(F32)
                for t in range(2):
                    term = probs[t][j : j + 1, :] * o
                    mix[t] = term if j == 0 else mix[t] + term
            pend = pre2
            yield
        mix_s[h, 0:EO, :] = mix[0].astype(BF)
        mix_s[h, EO : 2 * EO, :] = mix[1].astype(BF)
        act, slope = act_pair(mm(tt_s[...], mix_s[h, 0 : 2 * EO, :]) + tcol_s[:, 0:1])
        weighted = act * tcol_s[:, 1:2]
        lgos = []
        for t in range(2):
            logit = jnp.sum(weighted[TW * t : TW * t + TW], axis=0, keepdims=True) + tcol_s[t : t + 1, 3:4]
            label = (line_ref, far_line_ref)[t][:, pl.ds(pl.multiple_of(step * TILE + SUB * h, SUB), SUB)]
            lgos.append(row_s[:, pl.ds(pl.multiple_of(step * TILE + SUB * h, SUB), SUB)] * (0.5 * jnp.tanh(0.5 * logit) + 0.5 - label))
        lgo = jnp.concatenate([jnp.broadcast_to(lgos[t], (TW, SUB)) for t in range(2)], axis=0)
        dcol_s[...] += lane_fold(lgo * act)
        dlog_s[...] += lane_fold(jnp.concatenate([jnp.broadcast_to(lgos[t], (8, SUB)) for t in range(2)], axis=0))
        tg = (lgo * (tcol_s[:, 2:3] * slope)).astype(BF)
        yield
        dtw_s[...] += mm_nt(mix_s[h], tg)
        mgh = mm(tw_s[...], tg) * 0.5
        yield
        pgs = [[], []]
        mgs = [None] * NE
        for k in range(NE + 2):
            if k < NE:
                o = out_s[h, EO * k : EO * k + EO, :]
                og = None
                for t in range(2):
                    mg = mgh[EO * t : EO * t + EO]
                    pgs[t].append(jnp.sum((o * mg.astype(BF)).astype(F32), axis=0, keepdims=True))
                    term = probs[t][k : k + 1, :] * mg
                    og = term if og is None else og + term
                sg = og.astype(BF) * sl2_s[h, EO * k : EO * k + EO, :]
                sg_s[h, EO * (k % 2) : EO * (k % 2) + EO, :] = sg
                mgs[k] = mm(w2_s[:, EO * k : EO * k + EO], sg)
            if 1 <= k < NE + 1:
                j = k - 1
                dw2_s[:, EO * j : EO * j + EO] += mm_nt(mid_s[h, j], sg_s[h, EO * (j % 2) : EO * (j % 2) + EO, :])
                fg = mgs[j].astype(BF) * sl1_s[h, FH * j : FH * j + FH, :]
                fg_s[h, FH * j : FH * j + FH, :] = fg
            if k >= 2:
                j = k - 2
                dw1_s[:, FH * j : FH * j + FH] += mm_nt(hid_s[h], fg_s[h, FH * j : FH * j + FH, :])
            yield
        lgs = []
        for t in range(2):
            pg = jnp.concatenate(pgs[t], axis=0)
            lgs.append(2.0 * probs[t] * (pg - jnp.sum(probs[t] * pg, axis=0, keepdims=True)))
        fg_s[h, NE * FH : NE * FH + 16, :] = jnp.concatenate(lgs, axis=0).astype(BF)
        yield
        dw1_s[:, NE * FH : FG] += mm_nt(hid_s[h], fg_s[h, NE * FH : FG, :])
        hg = mm(w1_s[...], fg_s[h]).astype(BF)
        hg_ref[:, at] = hg
        yield
        dwa_s[...] += mm_nt(hg, x_s[h])
        yield

    take_turns([chain(h) for h in range(TILE // SUB)], LAG)

    @pl.when(step == pl.num_programs(0) - 1)
    def _():
        gate = dw1_s[:, NE * FH : FG].T
        dlog = jnp.sum(dlog_s[...], axis=1, keepdims=True)
        dcol = jnp.sum(dcol_s[...].T, axis=0, keepdims=True)
        for side in range(2):
            own_gate = swap_halves(gate[NE * side : NE * side + NE], second_core)
            ga_s[...] = jnp.concatenate([own_gate[:, 0:D], jnp.zeros((120, D), F32)], axis=0).T
            b1 = [dw1_s[D : D + 1, FH * k : FH * k + FH] for k in range(HALF * side, HALF * side + HALF)]
            b1 = jnp.concatenate(b1 + [jnp.zeros((124, FH), F32)], axis=0).T
            b2 = [dw2_s[FH : FH + 1, EO * k : EO * k + EO] for k in range(HALF * side, HALF * side + HALF)]
            b2 = jnp.concatenate(b2 + [jnp.zeros((60, EO), F32)], axis=0).T
            tower = dtw_s[EO * side : EO * side + EO, TW * side : TW * side + TW]
            tower = jnp.concatenate([tower, b2], axis=1)
            lanes = slice(TW * side, TW * side + TW)
            blank = jnp.zeros((1, TW), F32)
            lines = [jnp.concatenate([a, blank], axis=1) for a in (dtw_s[2 * EO : 2 * EO + 1, lanes], dcol[:, lanes])]
            gate_b = jnp.sum(jnp.where(lax.broadcasted_iota(jnp.int32, (NE, D + 16), 1) == D, own_gate, 0.0), axis=1, keepdims=True)
            small = jnp.concatenate([gate_b, dlog[8 * side : 8 * side + 8]], axis=0)
            small = jnp.concatenate([jnp.broadcast_to(small, (16, 128)), jnp.zeros((112, 128), F32)], axis=0).T[0:1]
            tail = jnp.concatenate(lines + [small, jnp.zeros((fs - osz - 3, 128), F32)], axis=0)
            b1 = pltpu.roll(b1, B1, 1)
            for c in range(chunks):
                dsm_s[fs * c : fs * c + fs, :] = b1[fs * c : fs * c + fs] + jnp.concatenate([tower[osz * c : osz * c + osz], tail], axis=0)
            holder = core if side == 0 else 1 - core
            cols = HALF * EO
            for n in range(chunks):
                ref, c = du_refs[quarters * side + n * quarters // chunks], n % (chunks // quarters)
                at = chunk_at(n, chunks, holder)
                to = pl.multiple_of(ds * at, ds)
                where = pl.ds(pl.multiple_of(tab_ref[1 + at] * fs, fs), fs)
                ref[c, :, 0:QA] = dw1_s[pl.ds(to, ds), QA * side : QA * side + QA].astype(BF)
                ref[c, 0:fs, QA:QS] = dw2_s[where, cols * side : cols * side + cols].astype(BF)
                low = pltpu.roll(ga_s[pl.ds(to, fs), :], GA, 1)
                high = pltpu.roll(ga_s[pl.ds(pl.multiple_of(to + fs, fs), fs), :], GA + NE, 1)
                ref[c, 0:fs, QS:UC] = (dsm_s[where, :] + low + high).astype(BF)
                lower = dwa_s[pl.ds(pl.multiple_of(to + holder * fs, fs), fs), :]
                ref[c, fs:ds, QA:UC] = jnp.concatenate([lower, jnp.zeros((fs, UC - QA - XR), F32)], axis=1).astype(BF)


def fill_weights(core, batch_rows, sizes, start_s, out_ref):
    batches, users = sizes.shape
    counts = jnp.concatenate([sizes.astype(F32), jnp.zeros((16 - batches, users), F32)], axis=0)
    turned = jnp.concatenate([counts, jnp.zeros((112, users), F32)], axis=0).T
    before = lax.broadcasted_iota(jnp.int32, (users, users), 1) < lax.broadcasted_iota(jnp.int32, (users, users), 0)
    starts = mm(jnp.where(before, 1.0, 0.0).astype(BF), turned.astype(BF))
    for b in range(batches):
        start_s[b] = jnp.broadcast_to(starts[:, b : b + 1], (users, 128))
    first = lax.broadcasted_iota(jnp.int32, counts.shape, 1) == 0
    rises = counts - jnp.where(first, 0.0, pltpu.roll(counts, 1, 1))
    line = lax.broadcasted_iota(jnp.int32, counts.shape, 0)
    steps = out_ref.shape[1] // SUB
    for step in range(steps):
        at_step = core * steps + step
        batch = at_step // (batch_rows // SUB)
        first_row = (at_step % (batch_rows // SUB) * SUB).astype(F32)
        begins = start_s[batch]
        places = first_row + lax.broadcasted_iota(jnp.int32, (1, 128), 1).astype(F32)
        begun = [jnp.where(begins <= places + 128.0 * c, 1.0, 0.0).astype(BF) for c in range(SUB // 128)]
        rise = jnp.where(line == batch, rises, 0.0).astype(BF)
        size = jnp.sum(mm(rise, jnp.concatenate(begun, axis=1)), axis=0, keepdims=True)
        out_ref[:, SUB * step : SUB * step + SUB] = 1.0 / size


def const2(i, c):
    return (0, 0)


def main_call(table, embt, denset, line, far_line, sizes_shape, own_u, far_u):
    rows = embt.shape[1]
    half = rows // 2
    steps = half // TILE
    pieces = len(own_u)
    chunks = sum(a.shape[0] for a in own_u)
    fs, ds = FH // chunks, D // chunks

    def own(i, c):
        return (0, c[0] * steps + i)

    quarters = min(4, chunks)
    grads = [(chunks // quarters, ds, UC)] * (2 * quarters)
    parts = TILE // SUB
    spec = pltpu.PrefetchScalarGridSpec(
        num_scalar_prefetch=1,
        grid=(steps,),
        in_specs=[
            pl.BlockSpec((EMB, TILE), own),
            whole(),
            whole(),
            whole(),
        ]
        + [whole() for _ in (*own_u, *far_u)],
        out_specs=[pl.BlockSpec((D, TILE), lambda i, c: (0, i))] + [whole()] * (1 + 2 * quarters),
        scratch_shapes=[
            pltpu.VMEM((parts, XR, SUB), BF),
            pltpu.VMEM((parts, D + 16, SUB), BF),
            pltpu.VMEM((parts, NE, FH + 16, SUB), BF),
            pltpu.VMEM((parts, NE * FH, SUB), BF),
            pltpu.VMEM((parts, NE * EO, SUB), BF),
            pltpu.VMEM((parts, NE * EO, SUB), BF),
            pltpu.VMEM((parts, 2 * EO, SUB), BF),
            pltpu.VMEM((parts, FG, SUB), BF),
            pltpu.VMEM((parts, 2 * EO + 16, SUB), BF),
            pltpu.VMEM((D, FG), BF),
            pltpu.VMEM((NE * FH + 16, D), BF),
            pltpu.VMEM((D, 128), F32),
            pltpu.VMEM((NE * EO, FH), BF),
            pltpu.VMEM((FH, NE * EO), BF),
            pltpu.VMEM((2, FH, 128), F32),
            pltpu.VMEM((2, EO, 128), F32),
            pltpu.VMEM((16, 1), F32),
            pltpu.VMEM((2 * TW, 2 * EO), BF),
            pltpu.VMEM((2 * EO, 2 * TW), BF),
            pltpu.VMEM((2 * TW, 4), F32),
            pltpu.VMEM((chunks, fs, UC - QA), F32),
            pltpu.VMEM((D, XR), F32),
            pltpu.VMEM((D + 16, FG), F32),
            pltpu.VMEM((FH + 16, NE * EO), F32),
            pltpu.VMEM((2 * EO + 16, 2 * TW), F32),
            pltpu.VMEM((2 * TW, 128), F32),
            pltpu.VMEM((16, 128), F32),
            pltpu.VMEM((FH, 128), F32),
            pltpu.VMEM((*sizes_shape, 128), F32),
            pltpu.VMEM((1, half), F32),
        ],
    )
    return pl.pallas_call(
        functools.partial(main_kernel, pieces, chunks, rows // sizes_shape[0]),
        grid_spec=spec,
        out_shape=[jax.ShapeDtypeStruct((D, half), BF), jax.ShapeDtypeStruct((D, XR), BF)]
        + [jax.ShapeDtypeStruct(a, BF) for a in grads],
        compiler_params=pltpu.CompilerParams(vmem_limit_bytes=48 * 1024 * 1024),
        cost_estimate=pl.CostEstimate(flops=50_000_000_000, bytes_accessed=24_000_000, transcendentals=0),
        name="experts",
    )(table, embt, denset, line, far_line, *own_u, *far_u)


def input_kernel(tab_ref, hg_ref, wat_ref, *refs):
    eg_ref, dg_ref, done_ref, wa_s = refs[-4:]

    @pl.when(pl.program_id(0) == 0)
    def _():
        wa_s[...] = wat_ref[...].astype(F32).T.astype(BF)
        done_ref[...] = jnp.zeros_like(done_ref)

    eg = mm(wa_s[...], hg_ref[...])
    eg_ref[...] = eg[0:EMB]
    dg_ref[...] = eg[EMB : EMB + DENSE]


def input_call(table, hg, wat, token, other, name):
    half = hg.shape[1]
    tile = TILE
    steps = half // tile

    def place(i, c):
        return (0, (c[0] if other is None else 1 - c[0]) * steps + i)

    extra = [token] + (list(other) if other is not None else [])
    spec = pltpu.PrefetchScalarGridSpec(
        num_scalar_prefetch=1,
        grid=(steps,),
        in_specs=[pl.BlockSpec((D, tile), lambda i, c: (0, i)), pl.BlockSpec((D, XR), const2, pipeline_mode=pl.Buffered(1))]
        + [whole(pl.ANY) for _ in extra],
        out_specs=[pl.BlockSpec((EMB, tile), place), pl.BlockSpec((DENSE, tile), place), pl.BlockSpec((8, 128), const2)],
        scratch_shapes=[pltpu.VMEM((XR, D), BF)],
    )
    return pl.pallas_call(
        input_kernel,
        grid_spec=spec,
        out_shape=[jax.ShapeDtypeStruct((EMB, 2 * half), F32), jax.ShapeDtypeStruct((DENSE, 2 * half), F32), jax.ShapeDtypeStruct((8, 128), F32)],
        input_output_aliases={} if other is None else {4: 0, 5: 1},
        compiler_params=pltpu.CompilerParams(vmem_limit_bytes=32 * 1024 * 1024),
        cost_estimate=pl.CostEstimate(flops=4_000_000_000, bytes_accessed=9_000_000, transcendentals=0),
        name=name,
    )(table, hg, wat, *extra)


def widen(a):
    return jnp.concatenate([a.astype(F32), jnp.zeros((a.shape[0], 128 - a.shape[1]), F32)], axis=1)


def square(rows):
    count = sum(a.shape[0] for a in rows)
    return jnp.concatenate(rows + [jnp.zeros((128 - count, 128), F32)], axis=0)


def pack_kernel(core_ref, emb_ref, dense_ref, bias_ref, w1_ref, w2_ref, b1_ref, b2_ref, gate_ref, tower_ref, *refs):
    sizes_ref, label_ref, u_ref, line_ref = refs[4:]
    rows = label_ref.shape[1]
    line_ref[:, 0:rows] = label_ref[...].astype(F32)
    for j in range(4):
        line_ref[:, rows + 128 * j : rows + 128 * j + 128] = widen(refs[j][...])
    users = sizes_ref.shape[1]
    for b in range(sizes_ref.shape[0]):
        line_ref[:, rows + 512 + users * b : rows + 512 + users * b + users] = sizes_ref[b : b + 1, :].astype(F32)
    fs = u_ref.shape[0] // 2
    turned = square([widen(r[...]) for r in (b1_ref, b2_ref, gate_ref, dense_ref, bias_ref)]).T
    lane = lax.broadcasted_iota(jnp.int32, (fs, 128), 1)
    low, high = turned[0:fs], turned[fs : 2 * fs]
    small = jnp.concatenate([widen(tower_ref[...]), jnp.zeros((fs - tower_ref.shape[0], 128), F32)], axis=0)
    small += jnp.where((lane >= TW) & (lane < TW + HALF), pltpu.roll(low, TW - HALF, 1), 0.0)
    small += jnp.where(((lane >= B1) & (lane < B1 + HALF)) | ((lane >= GA) & (lane < GA + NE)), pltpu.roll(low, B1, 1), 0.0)
    small += jnp.where((lane >= GA + NE) & (lane < GA + 2 * NE), pltpu.roll(high, GA, 1), 0.0)
    for k in range(HALF):
        u_ref[:, FH * k : FH * k + FH] = w1_ref[k]
        u_ref[0:fs, QA + EO * k : QA + EO * k + EO] = w2_ref[k]
    u_ref[0:fs, QS:UC] = small.astype(BF)
    second_core = core_ref[0] == 1
    lanes = lax.broadcasted_iota(jnp.int32, (2 * fs, 128), 1)
    last = widen(emb_ref[:, 384:EMB]) + jnp.where((lanes >= 32) & (lanes < 33 + DENSE), pltpu.roll(turned[0 : 2 * fs], 16, 1), 0.0)
    for c in range(3):
        block = emb_ref[:, 128 * c : 128 * c + 128]
        u_ref[fs:, QA + 128 * c : QA + 128 * c + 128] = jnp.where(second_core, block[fs:], block[0:fs])
    u_ref[fs:, QA + 384 : QA + 512] = jnp.where(second_core, last[fs:], last[0:fs]).astype(BF)
    u_ref[fs:, QA + 512 : UC] = jnp.zeros((fs, UC - QA - 512), BF)


def whole(memory=pltpu.VMEM):
    return pl.BlockSpec(memory_space=memory)


def pack_call(core, *parts):
    ds = parts[3].shape[1]
    return pl.pallas_call(
        pack_kernel,
        in_specs=[whole(pltpu.SMEM)] + [whole() for _ in parts],
        out_specs=[whole(), whole()],
        out_shape=[jax.ShapeDtypeStruct((ds, UC), BF), jax.ShapeDtypeStruct((1, parts[-1].shape[1] + 512 + parts[-2].size), F32)],
        name="pack",
    )(core, *parts)


def sum_kernel(groups, count, *refs):
    ins, outs = refs[:count], refs[-len(groups) :]
    for group, out in zip(groups, outs):
        total = None
        for number, at in group:
            term = ins[number][at].astype(F32)
            total = term if total is None else total + term
        out[...] = total.astype(out.dtype)


def sum_call(name, arrays, groups, shapes, token=None, through=None):
    extra = [a for a in (token, through) if a is not None]
    lead = [] if through is None else [through]
    return pl.pallas_call(
        functools.partial(sum_kernel, groups, len(arrays)),
        in_specs=[whole() for _ in arrays] + [whole(pl.ANY) for _ in extra],
        out_specs=[whole(pl.ANY) for _ in lead] + [whole() for _ in shapes],
        out_shape=[jax.ShapeDtypeStruct(a.shape, a.dtype) for a in lead] + [jax.ShapeDtypeStruct(a, BF) for a in shapes],
        input_output_aliases={len(arrays) + len(extra) - 1: 0} if lead else {},
        compiler_params=pltpu.CompilerParams(vmem_limit_bytes=16 * 1024 * 1024),
        name=name,
    )(*arrays, *extra)


def finish_kernel(scale, core_ref, token_ref, *refs):
    total = sum(r[...].astype(F32) for r in refs[:4]) * scale
    ds = total.shape[0]
    fs = ds // 2
    own_part = total[fs:, QA : QA + XR]
    far_part = sum(r[...].astype(F32) for r in refs[4:8])[:, 0:XR] * scale
    second_core = core_ref[0] == 1
    ta = jnp.concatenate([jnp.where(second_core, far_part, own_part), jnp.where(second_core, own_part, far_part)], axis=0)
    emb_ref, dense_ref, bias_ref, w1_ref, b1_ref, w2_ref, b2_ref, gate_ref, gb_ref, tower_ref, t1_ref, t2_ref, t3_ref = refs[8:]
    osz = tower_ref.shape[0]
    for k in range(HALF):
        w1_ref[k] = total[:, FH * k : FH * k + FH]
        w2_ref[k] = total[0:fs, QA + EO * k : QA + EO * k + EO]
    small = total[0:fs, QS:UC]
    turned = square([small]).T
    b1_ref[...] = turned[B1 : B1 + HALF, 0:fs]
    b2_ref[...] = turned[TW : TW + HALF, 0:osz]
    gates = turned[GA : GA + NE] + pltpu.roll(turned[GA + NE : GA + 2 * NE], fs, 1)
    gate_ref[...] = gates[:, 0 : 2 * fs]
    tower_ref[...] = small[0:osz, 0:TW]
    t1_ref[...] = small[osz : osz + 1, 0:TW]
    t2_ref[...] = small[osz + 1 : osz + 2, 0:TW]
    gb_ref[...] = small[osz + 2 : osz + 3, 0:NE]
    t3_ref[...] = small[osz + 2 : osz + 3, NE : NE + 1]
    emb_ref[...] = ta[:, 0:EMB]
    last = square([widen(ta[:, 384:XR])]).T
    dense_ref[...] = last[32 : 32 + DENSE, 0 : 2 * fs]
    bias_ref[...] = last[32 + DENSE : 33 + DENSE, 0 : 2 * fs]


def finish_call(scale, core, token, arrays, ds, fs, osz):
    shapes = [
        (ds, EMB), (DENSE, ds), (1, ds), (HALF, ds, FH), (HALF, fs), (HALF, fs, EO), (HALF, osz), (NE, ds), (1, NE),
        (osz, TW), (1, TW), (1, TW), (1, 1),
    ]
    return pl.pallas_call(
        functools.partial(finish_kernel, scale),
        in_specs=[whole(pltpu.SMEM), whole(pl.ANY)] + [whole() for _ in arrays],
        out_specs=[whole() for _ in shapes],
        out_shape=[jax.ShapeDtypeStruct(a, F32) for a in shapes],
        compiler_params=pltpu.CompilerParams(vmem_limit_bytes=8 * 1024 * 1024),
        name="finish",
    )(core, token, *arrays)


def hop(a, mask, size):
    return lax.ppermute(a, "rows", [(i, i ^ mask) for i in range(size)])


def cross(a, masks, size):
    pairs = [(2 * i + t, 2 * (i ^ masks[t]) + t) for i in range(size) for t in range(2)]
    return lax.ppermute(a, ("rows", "task"), pairs)


def partner(a):
    return lax.ppermute(a, "task", [(0, 1), (1, 0)])


def add_wide(a, b):
    return a.astype(F32) + b.astype(F32)


def halves(line, denset, core):
    rows = denset.shape[1]
    half = rows // 2
    own_line = jnp.concatenate([lax.dynamic_slice(line, (0, core * half), (1, half)), line[:, rows:]], axis=1)
    sent_line = jnp.concatenate([lax.dynamic_slice(line, (0, (1 - core) * half), (1, half)), line[:, rows : rows + 512]], axis=1)
    return own_line, partner(sent_line), lax.dynamic_slice(denset, (0, core * half), (DENSE, half))


def pad_to(a, rows, cols):
    return jnp.pad(a, ((0, rows - a.shape[0]), (0, cols - a.shape[1])))


def body(
    emb, dense, group_sizes, labels, w_emb, w_dense, b_in, expert_w1, expert_b1, expert_w2, expert_b2,
    gate_w, gate_b, tower_w1, tower_b1, tower_w2, tower_b2,
):
    size = lax.axis_size("rows")
    core = lax.axis_index("task")
    place = lax.axis_index("rows")
    user_count = group_sizes.shape[1] * group_sizes.shape[0] * size
    ds, fs, osz = D // size, FH // size, EO // size
    fast = size == 16
    smalls = (gate_b, tower_b1, tower_w2, tower_b2[None])

    if fast:
        one_core = core[None].astype(jnp.int32)
        gate_t = jnp.transpose(gate_w, (0, 2, 1))[0]
        shard, line = pack_call(
            one_core, w_emb.T, w_dense, b_in[None], expert_w1, expert_w2, expert_b1, expert_b2, gate_t, tower_w1[0], *smalls, group_sizes, labels
        )
        pairs = [jnp.stack([shard, hop(shard, 4, size)]), jnp.stack([hop(shard, 8, size), hop(shard, 12, size)])]
        own_line, far_line, own_dense = halves(line, dense.T, core)
        once, twice = cross(pairs[0], (1, 2), size), cross(pairs[0], (2, 1), size)
        held = (pairs[1], once, twice, own_line, far_line, own_dense)
        pairs[1], once, twice, own_line, far_line, own_dense = lax.optimization_barrier(held)
        once, twice = [once, cross(pairs[1], (1, 2), size)], [twice, cross(pairs[1], (2, 1), size)]
        own_u = pairs + once + twice + [cross(a, (2, 1), size) for a in once]
        steps = jnp.arange(16, dtype=jnp.int32)
        order = place ^ (steps % 4 * 4 + steps // 4)
    else:
        gather = functools.partial(lax.all_gather, axis_name="rows", axis=0, tiled=True)
        proj = jnp.concatenate([w_emb.T, w_dense.T, b_in[:, None], jnp.zeros((ds, 82), BF)], axis=1)
        w1_all = gather(jnp.transpose(expert_w1, (1, 0, 2)).reshape(ds, QA))
        w2_all = gather(jnp.transpose(expert_w2, (1, 0, 2)).reshape(fs, HALF * EO))
        o_all = gather(jnp.concatenate([tower_w1[0], expert_b2.T], axis=1))
        b1_all, g_all, proj_all = gather(expert_b1.T), gather(gate_w[0]), gather(proj)
        small = jnp.concatenate([pad_to(o_all, FH, B1), pad_to(b1_all, FH, GA - B1), g_all[0:FH], g_all[FH:], jnp.zeros((FH, 32), BF)], axis=1)
        part = jnp.where(core == 0, proj_all[0:FH], proj_all[FH:])
        lower = jnp.concatenate([part, jnp.zeros((FH, UC - QA - 512), BF)], axis=1)
        own_u = [jnp.concatenate([w1_all, jnp.concatenate([jnp.concatenate([w2_all, small], axis=1), lower], axis=0)], axis=1)[None]]
        order = jnp.zeros((1,), jnp.int32)
        line = [labels.astype(F32)] + [pad_to(a, 1, 128).astype(F32) for a in smalls]
        line = jnp.concatenate(line + [group_sizes.astype(F32).reshape(1, -1)], axis=1)
        own_line, far_line, own_dense = halves(line, dense.T, core)
    far_u = [partner(a) for a in own_u]
    table = jnp.concatenate([core[None].astype(jnp.int32), order])

    hg, wat, *grads = main_call(table, emb.T, own_dense, own_line, far_line, group_sizes.shape, own_u, far_u)
    own, far = grads[: len(grads) // 2], grads[len(grads) // 2 :]
    scale = 1.0 / user_count
    if fast:
        quarter, every = (4, ds, UC), slice(0, 4)
        (third,) = sum_call("sum_fourth", [own[3], partner(far[3])], [[(0, every), (1, every)]], [quarter])
        got_third = cross(third, (2, 1), size)
        hg, second = sum_call("sum_third", [own[2], partner(far[2])], [[(0, every), (1, every)]], [quarter], third, hg)
        got_second = cross(second, (2, 1), size)
        far_first, far_hg = partner(far[1]), partner(hg)
        eg, dg, token = input_call(table, hg, wat, second, None, "input_own")
        (first,) = sum_call("sum_second", [own[1], far_first, got_third], [[(j, every) for j in range(3)]], [quarter], token)
        got_first = cross(first, (1, 2), size)
        far_none = partner(far[0])
        eg, dg, token = input_call(table, far_hg, wat, first, (eg, dg), "input_far")
        groups = [[(j, k) for j in range(4)] for k in range(4)]
        sums = sum_call("sum_first", [own[0], far_none, got_second, got_first], groups, [(ds, UC)] * 4, token)
        parts = [sums[0]] + [hop(sums[a], 4 * a, size) for a in (3, 2, 1)]
        parts += [partner(a[fs:, QA : QA + 512]) for a in parts]
        out = finish_call(scale, one_core, sums[0], parts, ds, fs, osz)
        g_emb, g_dense, g_bias, g_w1, g_b1, g_w2, g_b2, g_gate, g_gb, g_tower, g_t1, g_t2, g_t3 = out
        return (
            eg.T, dg.T, g_emb.T, g_dense, g_bias[0], g_w1, g_b1, g_w2, g_b2, g_gate.T[None], g_gb, g_tower[None], g_t1, g_t2, g_t3[0],
        )
    eg, dg, token = input_call(table, hg, wat, far[0], None, "input_own")
    eg, dg, _ = input_call(table, partner(hg), wat, token, (eg, dg), "input_far")
    scatter = functools.partial(lax.psum_scatter, axis_name="rows", scatter_dimension=0, tiled=True)
    wide = add_wide(own[0][0], partner(far[0])[0])
    upper, near = wide[0:FH, QA:UC], wide[FH:, QA : QA + XR]
    far, small = partner(near), upper[:, HALF * EO :]
    ta = scatter(jnp.concatenate([jnp.where(core == 0, near, far), jnp.where(core == 0, far, near)], axis=0)) * scale
    tp = jnp.transpose((scatter(wide[:, 0:QA]) * scale).reshape(ds, HALF, FH), (1, 0, 2))
    tw2, to, tb1 = scatter(upper[:, 0 : HALF * EO]) * scale, scatter(small[0:EO, 0:B1]) * scale, scatter(small[:, B1 : B1 + HALF]) * scale
    tg = scatter(jnp.concatenate([small[:, GA : GA + NE], small[:, GA + NE : GA + 2 * NE]], axis=0)) * scale
    ts = lax.psum(small[EO : EO + 3], "rows") * scale
    return (
        eg.T,
        dg.T,
        ta[:, 0:EMB].T,
        ta[:, EMB : EMB + DENSE].T,
        ta[:, EMB + DENSE],
        tp,
        tb1.T,
        jnp.transpose(tw2.reshape(fs, HALF, EO), (1, 0, 2)),
        to[:, TW : TW + HALF].T,
        tg[None],
        ts[2:3, 0:NE],
        to[:, 0:TW][None],
        ts[0:1, 0:TW],
        ts[1:2, 0:TW],
        ts[2, NE : NE + 1],
    )


def solution(mesh):
    in_specs = (
        P("rows", None),
        P("rows", None),
        P("rows", None),
        P("task", "rows"),
        P(None, "rows"),
        P(None, "rows"),
        P("rows"),
        P("task", "rows", None),
        P("task", "rows"),
        P("task", "rows", None),
        P("task", "rows"),
        P("task", "rows", None),
        P("task", None),
        P("task", "rows", None),
        P("task", None),
        P("task", None),
        P("task"),
    )
    out_specs = (
        P("rows", None),
        P("rows", None),
        P(None, "rows"),
        P(None, "rows"),
        P("rows"),
        P("task", "rows", None),
        P("task", "rows"),
        P("task", "rows", None),
        P("task", "rows"),
        P("task", "rows", None),
        P("task", None),
        P("task", "rows", None),
        P("task", None),
        P("task", None),
        P("task"),
    )
    return jax.shard_map(body, mesh=mesh, in_specs=in_specs, out_specs=out_specs, check_vma=False)
```
